32 devices in a mesh: clip: 4 (over y, x), seq: 4 (over z), tp: 2 (over core).
Axes of the slice: x: 2, y: 2, z: 4, core: 2. Of those that a mesh axis runs over, the one named last changes fastest.
Arguments:
- ffn_hidden: bfloat16 [512, 10240], P('clip', 'tp'), may hold values from -6 to 6
- ffn_weight: bfloat16 [10240, 4096], P('tp', 'seq'), may hold values from -0.0625 to 0.0625
- residual: bfloat16 [512, 4096], P('clip', 'seq'), may hold values from -6 to 6
- norm_gain: float32 [4096], replicated, may hold values from 0.3 to 3
- kv_weight: bfloat16 [4096, 8, 256], P(None, ('seq', 'tp')), may hold values from -0.09375 to 0.09375
- destination: int32 [512, 1], replicated, may hold values from 0 to 3; in each aligned block of 128 rows (0 to 127, 128 to 255, ...) at most 32 rows name the same one
- queries: bfloat16 [4096, 1024], P(('clip', 'seq', 'tp')), may hold values from -360 to 360
Outputs:
- attended: bfloat16 [4096, 1024], P(('clip', 'seq', 'tp'))
The draws below stay inside these ranges and needn't reach their ends.
Inputs may be any that keep to these rules, and one draw needn't show every extreme that they name: `destination`: in each aligned block of 128 rows no clip is named by more than 32 rows, a bound that some block reaches; every clip is named by some row.
All inputs are finite; a program needn't handle non-finite values.
Results may differ from the reference program's by a relative error of at most 0.01375.
The reference program's roundings to bfloat16 on the way (of `text`, `normed`, `keyval` and `probs`) count: a program that leaves them out, or rounds other values in their place, can miss the bound.
Values may be sent and summed in bfloat16 or wider, within the bound.
No kernel may reach another device: no remote copies, remote signals or barrier semaphores. Data moves between devices by JAX's collectives and lax.ppermute only.
A program may use at most 64 MiB of HBM per device.

```python
import math
import jax
import jax.numpy as jnp
import numpy as np
from jax import lax

D_TEXT = 4096
FF = 10240
HEAD_DIM = 128
ROWS_CLIP = 128
HEADS = 8
QW = 1024
CAP = 32
SLOTS = 128
TOTAL_ROWS = 512
VIDEO = 1024
TOKENS = 4096
N_CLIP = 4


def draw_queries(key, part):
    first = jax.random.fold_in(key, 11)
    base = 1.5 * jax.random.truncated_normal(first, -6.0, 6.0, (TOKENS, QW), jnp.float32)
    return base.astype(jnp.bfloat16)


def block_levels(key, extent, cuts, least, top_value):
    gain, own = 1.0, jax.random.fold_in(key, 6)
    for position, shards_of in cuts:
        steps = jnp.exp(jax.random.uniform(jax.random.fold_in(own, position), (shards_of,), jnp.float32, least / len(cuts), top_value / len(cuts)))
        gain = gain * jnp.repeat(steps, extent[position] // shards_of).reshape([-1 if axis == position else 1 for axis in range(len(extent))])
    return gain


def shared_out(own_key, own, number, rows, amount, top, limit, skew):
    order = jax.random.permutation(own_key, amount)
    crowded, common = portions_of(amount, rows * top, limit, skew, True), portions_of(amount, rows * top, limit, skew, False)
    places = jnp.arange(amount)

    def named(sizes, rotation):
        used = int((sizes > 0).sum())
        fixed = max(1, used // 4)
        passed = fixed + (places - fixed + rotation * (used - fixed)) % max(1, amount - fixed)
        return jnp.zeros((amount,), jnp.int32).at[order[jnp.where(places < fixed, places, passed)]].set(jnp.asarray(sizes, jnp.int32))

    sizes = jnp.where(number % 4 == 0, named(crowded, number // 4), named(common, number - number // 4 - 1))
    mixed = jax.random.permutation(jax.random.fold_in(own, 3), amount)
    source_of, sink = mixed[0:amount // 2 * 2:2], mixed[1:amount // 2 * 2:2]
    room = jnp.minimum(sizes[source_of] - 1, limit - sizes[sink]) // 2
    room = jnp.where((source_of == order[0]) | (sink == order[0]) | (sizes[sink] == 0), 0, jnp.maximum(room, 0))
    passed = jax.random.randint(jax.random.fold_in(own, 4), (amount // 2,), 0, 1 << 20) % (room + 1)
    sizes = sizes.at[source_of].add(-passed).at[sink].add(passed)
    labels = jnp.searchsorted(jnp.cumsum(sizes), jnp.arange(rows * top), side="right").astype(jnp.int32)
    listing = labels.reshape(top, rows).T
    listing = listing[jax.random.permutation(jax.random.fold_in(own, 1), rows)]
    rotation = jax.random.randint(jax.random.fold_in(own, 2), (rows, 1), 0, top)
    return jnp.take_along_axis(listing, (jnp.arange(top)[None, :] + rotation) % top, axis=1)


def portions_of(number_of, total, limit, slope, full):
    loads = [(1 << 20) // math.isqrt(grade ** slope) + 1 for grade in range(1, number_of + 1)]
    largest = limit if full else min(limit, max(-(-total // number_of), total * loads[0] // sum(loads)))
    least = 1 if total - largest >= number_of - 1 else 0
    counts, spare = [largest] + [least] * (number_of - 1), total - largest - least * (number_of - 1)
    while spare > 0:
        movable = [i for i in range(1, number_of) if counts[i] < largest] or [i for i in range(1, number_of) if counts[i] < limit]
        pool, left = sum([loads[i] for i in movable]), spare
        for i in movable:
            more = min(limit - counts[i], max(1, left * loads[i] // pool), spare)
            counts[i] = counts[i] + more
            spare = spare - more
    return np.array(counts)


def bell_draw(own_key, shape, scale, reach, cuts=(), kind=jnp.bfloat16):
    level = block_levels(own_key, shape, cuts, -0.22, 0.18) if cuts else 1.0
    values = jax.random.normal(own_key, shape, jnp.float32) * scale * level
    return jnp.minimum(jnp.maximum(values, -reach), reach).astype(kind)


def setup_inputs(seed: int = 0) -> dict:
    arg_keys = jax.random.split(jax.random.key(seed), 8)
    ffn_hidden = bell_draw(arg_keys[0], (TOTAL_ROWS, FF), 1.0, 6.0, ((0, 4), (1, 2)))
    ffn_weight = bell_draw(arg_keys[1], (FF, D_TEXT), FF ** -0.5, 0.0625, ((0, 2), (1, 4)))
    residual = bell_draw(arg_keys[2], (TOTAL_ROWS, D_TEXT), 1.0, 6.0, ((0, 4), (1, 4)))
    norm_gain = jnp.clip(jnp.exp(jax.random.uniform(arg_keys[3], (D_TEXT,), jnp.float32, math.log(0.3), math.log(3.0))), 0.3, 3.0)
    kv_weight = bell_draw(arg_keys[4], (D_TEXT, HEADS, 2 * HEAD_DIM), D_TEXT ** -0.5, 0.09375, ((1, 8),))
    destination_keys = jax.random.split(jax.random.fold_in(arg_keys[5], 1), TOTAL_ROWS // ROWS_CLIP)
    destination_turns = jax.random.permutation(jax.random.fold_in(arg_keys[5], 3), TOTAL_ROWS // ROWS_CLIP)
    destination = jax.vmap(lambda own, number: shared_out(jax.random.fold_in(arg_keys[5], 2), own, number, ROWS_CLIP, N_CLIP, 1, CAP, 2))(destination_keys, destination_turns).reshape((TOTAL_ROWS, 1))
    queries = draw_queries(jax.random.fold_in(arg_keys[7], 71), 0)
    return {"ffn_hidden": ffn_hidden, "ffn_weight": ffn_weight, "residual": residual, "norm_gain": norm_gain, "kv_weight": kv_weight, "destination": destination, "queries": queries}


def attend_ref(query, keyval, valid):
    keys = keyval[:, :, :HEAD_DIM].astype(jnp.float32)
    values = keyval[:, :, HEAD_DIM:].astype(jnp.float32)
    scores = jnp.einsum('rhd,shd->hrs', query.astype(jnp.float32), keys) / math.sqrt(HEAD_DIM)
    scores = jnp.where(valid[None, None, :], scores, -1e+30)
    peak = lax.optimization_barrier(jnp.max(scores, axis=2, keepdims=True))
    weights = jnp.where(valid[None, None, :], jnp.exp(scores - peak), 0.0)
    probs = (weights / lax.optimization_barrier(jnp.sum(weights, axis=2, keepdims=True))).astype(jnp.bfloat16)
    return jnp.einsum('hrs,shd->rhd', probs.astype(jnp.float32), values).astype(jnp.bfloat16)

def reference(ffn_hidden, ffn_weight, residual, norm_gain, kv_weight, destination, queries):
    ffn_out = jnp.dot(ffn_hidden, ffn_weight, preferred_element_type=jnp.float32)
    text = (residual.astype(jnp.float32) + ffn_out).astype(jnp.bfloat16)
    wide = text.astype(jnp.float32)
    scale = 1.0 / jnp.sqrt(lax.optimization_barrier(jnp.mean(wide * wide, axis=1, keepdims=True)) + 1e-06)
    normed = (wide * scale * norm_gain[None, :]).astype(jnp.bfloat16)
    keyval = jnp.dot(normed, kv_weight.reshape(D_TEXT, HEADS * 2 * HEAD_DIM), preferred_element_type=jnp.float32)
    keyval = keyval.astype(jnp.bfloat16).reshape(TOTAL_ROWS, HEADS, 2 * HEAD_DIM)
    dest = destination[:, 0]
    clip_ids = jnp.arange(N_CLIP, dtype=jnp.int32)
    query_clips = queries.reshape(N_CLIP, VIDEO, HEADS, HEAD_DIM)

    def one_clip(pair):
        clip, query = pair
        member = dest == clip
        chosen = jnp.nonzero(member, size=SLOTS, fill_value=0)[0].astype(jnp.int32)
        count = jnp.sum(member.astype(jnp.int32))
        valid = jnp.arange(SLOTS, dtype=jnp.int32) < count
        return attend_ref(query, keyval[chosen], valid)
    result = lax.map(one_clip, (clip_ids, query_clips))
    return result.reshape(TOKENS, QW)
```

```python
import functools
import math

import jax
import jax.numpy as jnp
from jax import lax
from jax.experimental import pallas as pl
from jax.experimental.pallas import tpu as pltpu
from jax.sharding import PartitionSpec as P

EPSILON = 1e-06
VMEM_LIMIT = 48 * 1024 * 1024
F32 = jnp.float32
BF16 = jnp.bfloat16


def whole():
    return pl.BlockSpec(memory_space=pltpu.VMEM)


def swap(value, axis, offset):
    size = lax.axis_size(axis)
    return lax.ppermute(value, axis, [(i, i ^ offset) for i in range(size)])


def slot_select(dest_ref, clip, core, clips, half, cores):
    rows = dest_ref.shape[1]
    named = dest_ref[pl.ds(clip, 1), :]
    onehot = (lax.broadcasted_iota(jnp.int32, (clips, rows), 0) == named).astype(F32)
    earlier = (
        lax.broadcasted_iota(jnp.int32, (rows, rows), 0)
        < lax.broadcasted_iota(jnp.int32, (rows, rows), 1)
    ).astype(F32)
    before = jnp.dot(onehot, earlier, preferred_element_type=F32)
    rank = jnp.sum(before * onehot, axis=0, keepdims=True).astype(jnp.int32)
    slot = ((rank // half) ^ core) * (clips * half) + (named ^ clip) * half + rank % half
    slots = cores * clips * half
    return (lax.broadcasted_iota(jnp.int32, (slots, rows), 0) == slot).astype(BF16)


def ffn_kernel(clips, half, cores, dest_ref, hidden_ref, weight_ref, residual_ref,
               own_ref, send_ref, text_ref, select_ref, total_ref):
    step = pl.program_id(0)
    clip, core = lax.axis_index("clip"), lax.axis_index("tp")
    share = clips * half

    @pl.when(step == 0)
    def _():
        select = slot_select(dest_ref, clip, core, clips, half, cores)
        select_ref[...] = select
        text_ref[...] = jnp.dot(
            select[:share], residual_ref[...], preferred_element_type=F32
        ).astype(BF16)
        total_ref[...] = jnp.zeros_like(total_ref)

    packed = jnp.dot(select_ref[...], hidden_ref[...], preferred_element_type=F32).astype(BF16)
    total_ref[...] += jnp.dot(packed, weight_ref[...], preferred_element_type=F32)

    @pl.when(step == pl.num_programs(0) - 1)
    def _():
        own_ref[...] = total_ref[:share, :]
        send_ref[...] = total_ref[share:, :]


def ffn(dest, hidden, weight, residual, clips, half, cores):
    rows, depth = hidden.shape
    width = weight.shape[1]
    share = clips * half
    steps = 8
    block = depth // steps
    return pl.pallas_call(
        functools.partial(ffn_kernel, clips, half, cores),
        grid=(steps,),
        in_specs=[
            pl.BlockSpec(dest.shape, lambda i: (0, 0)),
            pl.BlockSpec((rows, block), lambda i: (0, i)),
            pl.BlockSpec((block, width), lambda i: (i, 0)),
            pl.BlockSpec((rows, width), lambda i: (0, 0)),
        ],
        out_specs=[
            pl.BlockSpec((share, width), lambda i: (0, 0)),
            pl.BlockSpec(((cores - 1) * share, width), lambda i: (0, 0)),
            pl.BlockSpec((share, width), lambda i: (0, 0)),
        ],
        out_shape=[
            jax.ShapeDtypeStruct((share, width), F32),
            jax.ShapeDtypeStruct(((cores - 1) * share, width), F32),
            jax.ShapeDtypeStruct((share, width), BF16),
        ],
        scratch_shapes=[
            pltpu.VMEM((cores * share, rows), BF16),
            pltpu.VMEM((cores * share, width), F32),
        ],
        compiler_params=pltpu.CompilerParams(vmem_limit_bytes=VMEM_LIMIT),
        cost_estimate=pl.CostEstimate(
            flops=2 * cores * share * depth * (width + rows),
            bytes_accessed=2 * depth * (width + rows),
            transcendentals=0,
        ),
    )(dest, hidden, weight, residual)


def keyval_kernel(parts, cores, *refs):
    texts, (gain_ref, *weights), out_ref = refs[:parts], refs[parts:-1], refs[-1]
    seq = lax.axis_index("seq")
    width = texts[0].shape[1]
    squares = 0.0
    for text in texts:
        wide = text[...].astype(F32)
        squares += jnp.sum(wide * wide, axis=1, keepdims=True)
    scale = lax.rsqrt(squares / (parts * width) + EPSILON)
    totals = [0.0] * cores
    for k, text in enumerate(texts):
        place = pl.ds(pl.multiple_of((seq ^ k) * width, width), width)
        normed = (text[...].astype(F32) * scale * gain_ref[:, place]).astype(BF16)
        for c, weight in enumerate(weights):
            totals[c] += jnp.dot(normed, weight[place, :], preferred_element_type=F32)
    each = weights[0].shape[1]
    for c in range(cores):
        out_ref[:, c * each:(c + 1) * each] = totals[c].astype(BF16)


def attend_kernel(parts, cores, heads_here, half, dest_ref, query_ref, *refs):
    blocks, out_ref = refs[:-1], refs[-1]
    clip, seq, core = lax.axis_index("clip"), lax.axis_index("seq"), lax.axis_index("tp")
    clips = dest_ref.shape[0]
    share = clips * half
    dim = query_ref.shape[1] // (parts * cores * heads_here)
    counts = jnp.sum((dest_ref[...] == clip).astype(jnp.int32), axis=1, keepdims=True)
    lane = lax.broadcasted_iota(jnp.int32, (clips, cores * share), 1)
    source = ((lane % share) // half) ^ clip
    limit = jnp.sum(
        jnp.where(lax.broadcasted_iota(jnp.int32, lane.shape, 0) == source, counts, 0),
        axis=0, keepdims=True,
    )
    flat = lax.broadcasted_iota(jnp.int32, (1, cores * share), 1)
    valid = ((flat // share) ^ core) * half + flat % half < limit
    for k in range(parts):
        for c in range(cores):
            for i in range(heads_here):
                head = ((seq ^ k) * cores + (core ^ c)) * heads_here + i
                columns = pl.ds(pl.multiple_of(head * dim, dim), dim)
                at = [((c ^ g) * heads_here + i) * 2 * dim for g in range(cores)]
                keys = jnp.concatenate(
                    [blocks[k * cores + g][:, at[g]:at[g] + dim] for g in range(cores)], axis=0
                )
                values = jnp.concatenate(
                    [blocks[k * cores + g][:, at[g] + dim:at[g] + 2 * dim] for g in range(cores)],
                    axis=0,
                )
                scores = lax.dot_general(
                    query_ref[:, columns], keys, (((1,), (1,)), ((), ())),
                    preferred_element_type=F32,
                ) / math.sqrt(dim)
                scores = jnp.where(valid, scores, -1e30)
                peak = jnp.max(scores, axis=1, keepdims=True)
                weights = jnp.where(valid, jnp.exp(scores - peak), 0.0)
                probs = (weights / jnp.sum(weights, axis=1, keepdims=True)).astype(BF16)
                out_ref[:, columns] = jnp.dot(
                    probs, values, preferred_element_type=F32
                ).astype(BF16)


def shards(ffn_hidden, ffn_weight, residual, norm_gain, kv_weight, destination, queries):
    clips, parts, cores = lax.axis_size("clip"), lax.axis_size("seq"), lax.axis_size("tp")
    rows = ffn_hidden.shape[0]
    half = rows // min(8, clips) // cores
    share = clips * half
    heads_here = kv_weight.shape[1]
    dest = destination.reshape(clips, rows)
    weights = [kv_weight.reshape(kv_weight.shape[0], heads_here * kv_weight.shape[2])]
    for g in range(1, cores):
        weights.append(swap(weights[0], "tp", g))
    own, send, text = ffn(dest, ffn_hidden, ffn_weight, residual, clips, half, cores)
    for g in range(1, cores):
        own = own + swap(send[(g - 1) * share:g * share], "tp", g)
    text = (text.astype(F32) + own).astype(BF16)
    arrived = [text[:half]]
    for j in range(1, clips):
        arrived.append(swap(text[j * half:(j + 1) * half], "clip", j))
    arrived = jnp.concatenate(arrived, axis=0)
    texts = [arrived] + [swap(arrived, "seq", k) for k in range(1, parts)]
    keyval = pl.pallas_call(
        functools.partial(keyval_kernel, parts, cores),
        in_specs=[whole()] * (parts + 1 + cores),
        out_specs=whole(),
        out_shape=jax.ShapeDtypeStruct((share, cores * weights[0].shape[1]), BF16),
        compiler_params=pltpu.CompilerParams(vmem_limit_bytes=VMEM_LIMIT),
    )(*texts, norm_gain.reshape(1, -1), *weights)
    blocks = []
    for k in range(parts):
        block = swap(keyval, "seq", k) if k else keyval
        blocks += [block] + [swap(block, "tp", g) for g in range(1, cores)]
    return pl.pallas_call(
        functools.partial(attend_kernel, parts, cores, heads_here, half),
        in_specs=[whole()] * (2 + len(blocks)),
        out_specs=whole(),
        out_shape=jax.ShapeDtypeStruct(queries.shape, BF16),
        compiler_params=pltpu.CompilerParams(vmem_limit_bytes=VMEM_LIMIT),
    )(dest, queries, *blocks)


def solution(mesh):
    return jax.shard_map(
        shards,
        mesh=mesh,
        in_specs=(
            P("clip", "tp"),
            P("tp", "seq"),
            P("clip", "seq"),
            P(),
            P(None, ("seq", "tp"), None),
            P(),
            P(("clip", "seq", "tp"), None),
        ),
        out_specs=P(("clip", "seq", "tp"), None),
        check_vma=False,
    )
```

```python
import functools
import math

import jax
import jax.numpy as jnp
from jax import lax
from jax.experimental import pallas as pl
from jax.experimental.pallas import tpu as pltpu
from jax.sharding import PartitionSpec as P

EPSILON = 1e-06
VMEM_LIMIT = 24 * 1024 * 1024
VMEM_ALL = 60 * 1024 * 1024
F32 = jnp.float32
BF16 = jnp.bfloat16


def whole():
    return pl.BlockSpec(memory_space=pltpu.VMEM)


def swap(value, axis, offset):
    size = lax.axis_size(axis)
    return lax.ppermute(value, axis, [(i, i ^ offset) for i in range(size)])


def slot_select(dest_ref, clip, core, clips, half, cores):
    rows = dest_ref.shape[1]
    named = dest_ref[pl.ds(clip, 1), :]
    onehot = (lax.broadcasted_iota(jnp.int32, (clips, rows), 0) == named).astype(F32)
    earlier = (
        lax.broadcasted_iota(jnp.int32, (rows, rows), 0)
        < lax.broadcasted_iota(jnp.int32, (rows, rows), 1)
    ).astype(F32)
    before = jnp.dot(onehot, earlier, preferred_element_type=F32)
    rank = jnp.sum(before * onehot, axis=0, keepdims=True).astype(jnp.int32)
    slot = ((rank // half) ^ core) * (clips * half) + named * half + rank % half
    slots = cores * clips * half
    return (lax.broadcasted_iota(jnp.int32, (slots, rows), 0) == slot).astype(BF16)


def ffn_kernel(clips, half, cores, steps, dest_hbm, hidden_hbm, weight_hbm, residual_hbm,
               own_ref, send_ref, text_ref, dest_ref, hidden_ref, weight_ref, residual_ref,
               total_ref, sems):
    clip, core = lax.axis_index("clip"), lax.axis_index("tp")
    share = clips * half
    block = hidden_hbm.shape[1] // steps
    first = [
        pltpu.make_async_copy(dest_hbm, dest_ref, sems.at[2 * steps]),
        pltpu.make_async_copy(residual_hbm, residual_ref, sems.at[2 * steps + 1]),
    ]
    hidden_copies, weight_copies = [], []
    for i in range(steps):
        part = pl.ds(i * block, block)
        hidden_copies.append(
            pltpu.make_async_copy(hidden_hbm.at[:, part], hidden_ref.at[:, part], sems.at[i])
        )
        weight_copies.append(
            pltpu.make_async_copy(
                weight_hbm.at[part, :], weight_ref.at[part, :], sems.at[steps + i]
            )
        )
    first[0].start()
    for hidden_copy, weight_copy in zip(hidden_copies, weight_copies):
        hidden_copy.start()
        weight_copy.start()
    first[1].start()
    first[0].wait()
    select = slot_select(dest_ref, clip, core, clips, half, cores)
    for i in range(steps):
        part = pl.ds(i * block, block)
        hidden_copies[i].wait()
        packed = jnp.dot(select, hidden_ref[:, part], preferred_element_type=F32).astype(BF16)
        weight_copies[i].wait()
        product = jnp.dot(packed, weight_ref[part, :], preferred_element_type=F32)
        if i == 0:
            total_ref[...] = product
        elif i < steps - 1:
            total_ref[...] += product
        else:
            own_ref[...] = total_ref[:share, :] + product[:share]
            send_ref[...] = total_ref[share:, :] + product[share:]
    first[1].wait()
    text_ref[...] = jnp.dot(
        select[:share], residual_ref[...], preferred_element_type=F32
    ).astype(BF16)


def ffn(dest, hidden, weight, residual, clips, half, cores):
    rows, depth = hidden.shape
    width = weight.shape[1]
    share = clips * half
    steps = math.gcd(10, depth // 128)
    return pl.pallas_call(
        functools.partial(ffn_kernel, clips, half, cores, steps),
        in_specs=[pl.BlockSpec(memory_space=pltpu.HBM)] * 4,
        out_specs=[whole()] * 3,
        out_shape=[
            jax.ShapeDtypeStruct((share, width), F32),
            jax.ShapeDtypeStruct(((cores - 1) * share, width), F32),
            jax.ShapeDtypeStruct((share, width), BF16),
        ],
        scratch_shapes=[
            pltpu.VMEM(dest.shape, jnp.int32),
            pltpu.VMEM(hidden.shape, BF16),
            pltpu.VMEM(weight.shape, BF16),
            pltpu.VMEM(residual.shape, BF16),
            pltpu.VMEM((cores * share, width), F32),
            pltpu.SemaphoreType.DMA((2 * steps + 2,)),
        ],
        compiler_params=pltpu.CompilerParams(vmem_limit_bytes=VMEM_ALL),
        cost_estimate=pl.CostEstimate(
            flops=2 * cores * share * depth * (width + rows),
            bytes_accessed=2 * depth * (width + rows),
            transcendentals=0,
        ),
    )(dest, hidden, weight, residual)


def keyval_kernel(parts, cores, text_ref, gain_ref, *refs):
    weights, out_ref = refs[:-1], refs[-1]
    width = text_ref.shape[2]
    squares = 0.0
    for s in range(parts):
        wide = text_ref[s].astype(F32)
        squares += jnp.sum(wide * wide, axis=1, keepdims=True)
    scale = lax.rsqrt(squares / (parts * width) + EPSILON)
    totals = [0.0] * cores
    for s in range(parts):
        place = slice(s * width, (s + 1) * width)
        normed = (text_ref[s].astype(F32) * scale * gain_ref[:, place]).astype(BF16)
        for c, weight in enumerate(weights):
            totals[c] += jnp.dot(normed, weight[place, :], preferred_element_type=F32)
    each = weights[0].shape[1]
    for c in range(cores):
        out_ref[:, c * each:(c + 1) * each] = totals[c].astype(BF16)


def attend_kernel(parts, cores, heads_here, half, dest_ref, query_ref, *refs):
    blocks, out_ref = refs[:-1], refs[-1]
    clip, core = lax.axis_index("clip"), lax.axis_index("tp")
    clips = dest_ref.shape[0]
    share = clips * half
    dim = query_ref.shape[1] // (parts * cores * heads_here)
    counts = jnp.sum((dest_ref[...] == clip).astype(jnp.int32), axis=1, keepdims=True)
    lane = lax.broadcasted_iota(jnp.int32, (clips, cores * share), 1)
    source = (lane % share) // half
    limit = jnp.sum(
        jnp.where(lax.broadcasted_iota(jnp.int32, lane.shape, 0) == source, counts, 0),
        axis=0, keepdims=True,
    )
    flat = lax.broadcasted_iota(jnp.int32, (1, cores * share), 1)
    valid = ((flat // share) ^ core) * half + flat % half < limit
    for s in range(parts):
        for c in range(cores):
            for i in range(heads_here):
                head = (s * cores + (core ^ c)) * heads_here + i
                columns = pl.ds(pl.multiple_of(head * dim, dim), dim)
                at = [((c ^ g) * heads_here + i) * 2 * dim for g in range(cores)]
                keys = jnp.concatenate(
                    [blocks[g][s, :, at[g]:at[g] + dim] for g in range(cores)], axis=0
                )
                values = jnp.concatenate(
                    [blocks[g][s, :, at[g] + dim:at[g] + 2 * dim] for g in range(cores)], axis=0
                )
                scores = lax.dot_general(
                    query_ref[:, columns], keys, (((1,), (1,)), ((), ())),
                    preferred_element_type=F32,
                ) * (1.0 / math.sqrt(dim))
                scores = jnp.where(valid, scores, -1e30)
                peak = jnp.max(scores, axis=1, keepdims=True)
                weights = jnp.where(valid, jnp.exp(scores - peak), 0.0)
                probs = (weights / jnp.sum(weights, axis=1, keepdims=True)).astype(BF16)
                out_ref[:, columns] = jnp.dot(
                    probs, values, preferred_element_type=F32
                ).astype(BF16)


def shards(ffn_hidden, ffn_weight, residual, norm_gain, kv_weight, destination, queries):
    clips, parts, cores = lax.axis_size("clip"), lax.axis_size("seq"), lax.axis_size("tp")
    rows = ffn_hidden.shape[0]
    half = rows // min(8, clips) // cores
    share = clips * half
    heads_here = kv_weight.shape[1]
    dest = destination.reshape(clips, rows)
    weights = [kv_weight.reshape(kv_weight.shape[0], heads_here * kv_weight.shape[2])]
    for g in range(1, cores):
        weights.append(swap(weights[0], "tp", g))
    own, send, text = ffn(dest, ffn_hidden, ffn_weight, residual, clips, half, cores)
    for g in range(1, cores):
        own = own + swap(send[(g - 1) * share:g * share], "tp", g)
    text = (text.astype(F32) + own).astype(BF16)
    width = text.shape[1]
    text = jnp.broadcast_to(text[None], (parts, share, width)).reshape(-1, half, width)
    arrived = lax.all_to_all(text, ("seq", "clip"), 0, 0, tiled=True).reshape(parts, share, width)
    keyval = pl.pallas_call(
        functools.partial(keyval_kernel, parts, cores),
        in_specs=[whole()] * (2 + cores),
        out_specs=whole(),
        out_shape=jax.ShapeDtypeStruct((share, cores * weights[0].shape[1]), BF16),
        compiler_params=pltpu.CompilerParams(vmem_limit_bytes=VMEM_LIMIT),
    )(arrived, norm_gain.reshape(1, -1), *weights)
    block = lax.all_to_all(
        jnp.broadcast_to(keyval[None], (parts,) + keyval.shape), "seq", 0, 0, tiled=True
    )
    blocks = [block] + [swap(block, "tp", g) for g in range(1, cores)]
    return pl.pallas_call(
        functools.partial(attend_kernel, parts, cores, heads_here, half),
        in_specs=[whole()] * (2 + len(blocks)),
        out_specs=whole(),
        out_shape=jax.ShapeDtypeStruct(queries.shape, BF16),
        compiler_params=pltpu.CompilerParams(vmem_limit_bytes=VMEM_LIMIT),
    )(dest, queries, *blocks)


def solution(mesh):
    return jax.shard_map(
        shards,
        mesh=mesh,
        in_specs=(
            P("clip", "tp"),
            P("tp", "seq"),
            P("clip", "seq"),
            P(),
            P(None, ("seq", "tp"), None),
            P(),
            P(("clip", "seq", "tp"), None),
        ),
        out_specs=P(("clip", "seq", "tp"), None),
        check_vma=False,
    )
```

```python
import functools
import math

import jax
import jax.numpy as jnp
from jax import lax
from jax.experimental import pallas as pl
from jax.experimental.pallas import tpu as pltpu
from jax.sharding import PartitionSpec as P

EPSILON = 1e-06
VMEM_LIMIT = 24 * 1024 * 1024
VMEM_ALL = 60 * 1024 * 1024
F32 = jnp.float32
BF16 = jnp.bfloat16


def whole():
    return pl.BlockSpec(memory_space=pltpu.VMEM)


def swap(value, axis, offset):
    size = lax.axis_size(axis)
    return lax.ppermute(value, axis, [(i, i ^ offset) for i in range(size)])


def route(value, place):
    clips, cores = lax.axis_size("clip"), lax.axis_size("tp")
    pairs = [
        (i * cores + t, (i ^ (t * (clips // cores) + place)) * cores + t)
        for i in range(clips) for t in range(cores)
    ]
    return lax.ppermute(value, ("clip", "tp"), pairs)


def slot_select(dest_ref, clip, core, capacity, cores):
    clips, rows = dest_ref.shape
    named = dest_ref[pl.ds(clip, 1), :]
    onehot = (lax.broadcasted_iota(jnp.int32, (clips, rows), 0) == named).astype(F32)
    earlier = (
        lax.broadcasted_iota(jnp.int32, (rows, rows), 0)
        < lax.broadcasted_iota(jnp.int32, (rows, rows), 1)
    ).astype(F32)
    before = jnp.dot(onehot, earlier, preferred_element_type=F32)
    rank = jnp.sum(before * onehot, axis=0, keepdims=True).astype(jnp.int32)
    away = (named ^ clip) ^ (core * (clips // cores))
    slot = away * capacity + rank
    return (lax.broadcasted_iota(jnp.int32, (clips * capacity, rows), 0) == slot).astype(BF16)


def ffn_kernel(capacity, cores, steps, dest_hbm, hidden_hbm, weight_hbm, residual_hbm,
               own_ref, send_ref, text_ref, dest_ref, hidden_ref, weight_ref, residual_ref,
               packed_ref, total_ref, sems):
    clip, core = lax.axis_index("clip"), lax.axis_index("tp")
    share = own_ref.shape[0]
    block = hidden_hbm.shape[1] // steps
    get_dest = pltpu.make_async_copy(dest_hbm, dest_ref, sems.at[steps])
    get_hidden = pltpu.make_async_copy(hidden_hbm, hidden_ref, sems.at[steps + 1])
    get_residual = pltpu.make_async_copy(residual_hbm, residual_ref, sems.at[steps + 2])
    get_weight = [
        pltpu.make_async_copy(
            weight_hbm.at[pl.ds(i * block, block), :],
            weight_ref.at[pl.ds(i * block, block), :],
            sems.at[i],
        )
        for i in range(steps)
    ]
    for copy in [get_dest, get_hidden] + get_weight + [get_residual]:
        copy.start()
    get_dest.wait()
    select = slot_select(dest_ref, clip, core, capacity, cores)
    get_hidden.wait()
    packed_ref[...] = jnp.dot(select, hidden_ref[...], preferred_element_type=F32).astype(BF16)
    for i in range(steps):
        part = pl.ds(i * block, block)
        get_weight[i].wait()
        product = jnp.dot(packed_ref[:, part], weight_ref[part, :], preferred_element_type=F32)
        if i == 0:
            total_ref[...] = product
        elif i < steps - 1:
            total_ref[...] += product
        else:
            own_ref[...] = total_ref[:share, :] + product[:share]
            send_ref[...] = total_ref[share:, :] + product[share:]
    get_residual.wait()
    text_ref[...] = jnp.dot(
        select[:share], residual_ref[...], preferred_element_type=F32
    ).astype(BF16)


def ffn(dest, hidden, weight, residual, capacity, cores):
    rows, depth = hidden.shape
    width = weight.shape[1]
    slots = dest.shape[0] * capacity
    share = slots // cores
    steps = math.gcd(5, depth // 128)
    return pl.pallas_call(
        functools.partial(ffn_kernel, capacity, cores, steps),
        in_specs=[pl.BlockSpec(memory_space=pltpu.HBM)] * 4,
        out_specs=[whole()] * 3,
        out_shape=[
            pltpu.VMEM((share, width), F32),
            pltpu.VMEM((slots - share, width), F32),
            pltpu.VMEM((share, width), BF16),
        ],
        scratch_shapes=[
            pltpu.VMEM(dest.shape, jnp.int32),
            pltpu.VMEM(hidden.shape, BF16),
            pltpu.VMEM(weight.shape, BF16),
            pltpu.VMEM(residual.shape, BF16),
            pltpu.VMEM((slots, depth), BF16),
            pltpu.VMEM((slots, width), F32),
            pltpu.SemaphoreType.DMA((steps + 3,)),
        ],
        compiler_params=pltpu.CompilerParams(vmem_limit_bytes=VMEM_ALL),
        cost_estimate=pl.CostEstimate(
            flops=2 * slots * depth * (width + rows),
            bytes_accessed=2 * depth * (width + rows),
            transcendentals=0,
        ),
    )(dest, hidden, weight, residual)


def keyval_kernel(parts, cores, *refs):
    texts, (gain_ref, *weights), out_ref = refs[:parts], refs[parts:-1], refs[-1]
    seq = lax.axis_index("seq")
    width = texts[0].shape[1]
    squares = 0.0
    for text in texts:
        wide = text[...].astype(F32)
        squares += jnp.sum(wide * wide, axis=1, keepdims=True)
    scale = lax.rsqrt(squares / (parts * width) + EPSILON)
    totals = [0.0] * cores
    for k, text in enumerate(texts):
        place = pl.ds(pl.multiple_of((seq ^ k) * width, width), width)
        normed = (text[...].astype(F32) * scale * gain_ref[:, place]).astype(BF16)
        for c, weight in enumerate(weights):
            totals[c] += jnp.dot(normed, weight[place, :], preferred_element_type=F32)
    each = weights[0].shape[1]
    for c in range(cores):
        out_ref[:, c * each:(c + 1) * each] = totals[c].astype(BF16)


def attend_kernel(parts, cores, heads_here, capacity, dest_ref, query_ref, *refs):
    blocks, out_ref = refs[:-1], refs[-1]
    clip, seq, core = lax.axis_index("clip"), lax.axis_index("seq"), lax.axis_index("tp")
    clips = dest_ref.shape[0]
    slots = clips * capacity
    dim = query_ref.shape[1] // (parts * cores * heads_here)
    counts = jnp.sum((dest_ref[...] == clip).astype(jnp.int32), axis=1, keepdims=True)
    lane = lax.broadcasted_iota(jnp.int32, (clips, slots), 1)
    source = (lane // capacity) ^ (core * (clips // cores)) ^ clip
    limit = jnp.sum(
        jnp.where(lax.broadcasted_iota(jnp.int32, lane.shape, 0) == source, counts, 0),
        axis=0, keepdims=True,
    )
    valid = lax.broadcasted_iota(jnp.int32, (1, slots), 1) % capacity < limit
    heads = [(k, c, i) for k in range(parts) for c in range(cores) for i in range(heads_here)]

    def columns(head):
        k, c, i = head
        at = ((seq ^ k) * cores + (core ^ c)) * heads_here + i
        return pl.ds(pl.multiple_of(at * dim, dim), dim)

    def stored(head, offset):
        k, c, i = head
        parts_of = []
        for g in range(cores):
            at = ((c ^ g) * heads_here + i) * 2 * dim + offset
            parts_of.append(blocks[k * cores + g][:, at:at + dim])
        return jnp.concatenate(parts_of, axis=0)

    group = 8
    for first in range(0, len(heads), group):
        some = heads[first:first + group]
        scores = [
            lax.dot_general(
                query_ref[:, columns(head)], stored(head, 0), (((1,), (1,)), ((), ())),
                preferred_element_type=F32,
            )
            for head in some
        ]
        scores = [jnp.where(valid, score * (1.0 / math.sqrt(dim)), -1e30) for score in scores]
        peaks = [jnp.max(score, axis=1, keepdims=True) for score in scores]
        weights = [
            jnp.where(valid, jnp.exp(score - peak), 0.0) for score, peak in zip(scores, peaks)
        ]
        sums = [jnp.sum(weight, axis=1, keepdims=True) for weight in weights]
        probs = [(weight / total).astype(BF16) for weight, total in zip(weights, sums)]
        results = [
            jnp.dot(prob, stored(head, dim), preferred_element_type=F32).astype(BF16)
            for prob, head in zip(probs, some)
        ]
        for head, result in zip(some, results):
            out_ref[:, columns(head)] = result


def shards(ffn_hidden, ffn_weight, residual, norm_gain, kv_weight, destination, queries):
    clips, parts, cores = lax.axis_size("clip"), lax.axis_size("seq"), lax.axis_size("tp")
    rows = ffn_hidden.shape[0]
    capacity = rows // min(8, clips)
    share = clips * capacity // cores
    heads_here = kv_weight.shape[1]
    dest = destination.reshape(clips, rows)
    weight = kv_weight.reshape(kv_weight.shape[0], heads_here * kv_weight.shape[2])
    own, send, text = ffn(dest, ffn_hidden, ffn_weight, residual, capacity, cores)
    for g in range(1, cores):
        own = own + swap(send[(g - 1) * share:g * share], "tp", g)
    text = (text.astype(F32) + own).astype(BF16)
    weight, text = lax.optimization_barrier((weight, text))
    weights = [weight] + [swap(weight, "tp", g) for g in range(1, cores)]
    arrived = [
        route(text[i * capacity:(i + 1) * capacity], i) for i in range(clips // cores)
    ]
    arrived = jnp.concatenate(arrived, axis=0)
    texts = [arrived] + [swap(arrived, "seq", k) for k in range(1, parts)]
    keyval = pl.pallas_call(
        functools.partial(keyval_kernel, parts, cores),
        in_specs=[whole()] * (parts + 1 + cores),
        out_specs=whole(),
        out_shape=jax.ShapeDtypeStruct((share, cores * weight.shape[1]), BF16),
        compiler_params=pltpu.CompilerParams(vmem_limit_bytes=VMEM_LIMIT),
    )(*texts, norm_gain.reshape(1, -1), *weights)
    blocks = []
    for k in range(parts):
        block = swap(keyval, "seq", k) if k else keyval
        blocks += [block] + [swap(block, "tp", g) for g in range(1, cores)]
    return pl.pallas_call(
        functools.partial(attend_kernel, parts, cores, heads_here, capacity),
        in_specs=[whole()] * (2 + len(blocks)),
        out_specs=whole(),
        out_shape=jax.ShapeDtypeStruct(queries.shape, BF16),
        compiler_params=pltpu.CompilerParams(vmem_limit_bytes=VMEM_LIMIT),
    )(dest, queries, *blocks)


def solution(mesh):
    return jax.shard_map(
        shards,
        mesh=mesh,
        in_specs=(
            P("clip", "tp"),
            P("tp", "seq"),
            P("clip", "seq"),
            P(),
            P(None, ("seq", "tp"), None),
            P(),
            P(("clip", "seq", "tp"), None),
        ),
        out_specs=P(("clip", "seq", "tp"), None),
        check_vma=False,
    )
```

```python
import functools
import math

import jax
import jax.numpy as jnp
from jax import lax
from jax.experimental import pallas as pl
from jax.experimental.pallas import tpu as pltpu
from jax.sharding import PartitionSpec as P

EPSILON = 1e-06
VMEM_LIMIT = 24 * 1024 * 1024
VMEM_ALL = 60 * 1024 * 1024
F32 = jnp.float32
BF16 = jnp.bfloat16


def whole():
    return pl.BlockSpec(memory_space=pltpu.VMEM)


def swap(value, axis, offset):
    size = lax.axis_size(axis)
    return lax.ppermute(value, axis, [(i, i ^ offset) for i in range(size)])


def route_offsets(clips, cores):
    if clips == 4 and cores == 2:
        return [0, 3, 1, 2]
    return list(range(clips))


def route(value, place):
    clips, cores = lax.axis_size("clip"), lax.axis_size("tp")
    offsets = route_offsets(clips, cores)
    pairs = [
        (i * cores + t, (i ^ offsets[t * (clips // cores) + place]) * cores + t)
        for i in range(clips) for t in range(cores)
    ]
    return lax.ppermute(value, ("clip", "tp"), pairs)


def slot_select(dest_ref, clip, core, capacity, cores):
    clips, rows = dest_ref.shape
    named = dest_ref[pl.ds(clip, 1), :]
    onehot = (lax.broadcasted_iota(jnp.int32, (clips, rows), 0) == named).astype(F32)
    earlier = (
        lax.broadcasted_iota(jnp.int32, (rows, rows), 0)
        < lax.broadcasted_iota(jnp.int32, (rows, rows), 1)
    ).astype(F32)
    before = jnp.dot(onehot, earlier, preferred_element_type=F32)
    rank = jnp.sum(before * onehot, axis=0, keepdims=True).astype(jnp.int32)
    away = named ^ clip
    block = jnp.zeros_like(away)
    for place, offset in enumerate(route_offsets(clips, cores)):
        block = jnp.where(away == offset, place, block)
    slot = (block ^ (core * (clips // cores))) * capacity + rank
    return (lax.broadcasted_iota(jnp.int32, (clips * capacity, rows), 0) == slot).astype(BF16)


def ffn_kernel(capacity, cores, steps, dest_hbm, hidden_hbm, weight_hbm, residual_hbm,
               own_ref, send_ref, text_ref, dest_ref, hidden_ref, weight_ref, residual_ref,
               packed_ref, total_ref, sems):
    clip, core = lax.axis_index("clip"), lax.axis_index("tp")
    share = own_ref.shape[0]
    block = hidden_hbm.shape[1] // steps
    get_dest = pltpu.make_async_copy(dest_hbm, dest_ref, sems.at[steps])
    get_hidden = pltpu.make_async_copy(hidden_hbm, hidden_ref, sems.at[steps + 1])
    get_residual = pltpu.make_async_copy(residual_hbm, residual_ref, sems.at[steps + 2])
    get_weight = [
        pltpu.make_async_copy(
            weight_hbm.at[pl.ds(i * block, block), :],
            weight_ref.at[pl.ds(i * block, block), :],
            sems.at[i],
        )
        for i in range(steps)
    ]
    for copy in [get_dest, get_hidden] + get_weight + [get_residual]:
        copy.start()
    get_dest.wait()
    select = slot_select(dest_ref, clip, core, capacity, cores)
    get_hidden.wait()
    packed_ref[...] = jnp.dot(select, hidden_ref[...], preferred_element_type=F32).astype(BF16)
    for i in range(steps):
        part = pl.ds(i * block, block)
        get_weight[i].wait()
        product = jnp.dot(packed_ref[:, part], weight_ref[part, :], preferred_element_type=F32)
        if i == 0:
            total_ref[...] = product
        elif i < steps - 1:
            total_ref[...] += product
        else:
            own_ref[...] = total_ref[:share, :] + product[:share]
            send_ref[...] = total_ref[share:, :] + product[share:]
    get_residual.wait()
    text_ref[...] = jnp.dot(
        select[:share], residual_ref[...], preferred_element_type=F32
    ).astype(BF16)


def ffn(dest, hidden, weight, residual, capacity, cores):
    rows, depth = hidden.shape
    width = weight.shape[1]
    slots = dest.shape[0] * capacity
    share = slots // cores
    steps = math.gcd(5, depth // 128)
    return pl.pallas_call(
        functools.partial(ffn_kernel, capacity, cores, steps),
        in_specs=[pl.BlockSpec(memory_space=pltpu.HBM)] * 4,
        out_specs=[whole()] * 3,
        out_shape=[
            pltpu.VMEM((share, width), F32),
            pltpu.VMEM((slots - share, width), F32),
            pltpu.VMEM((share, width), BF16),
        ],
        scratch_shapes=[
            pltpu.VMEM(dest.shape, jnp.int32),
            pltpu.VMEM(hidden.shape, BF16),
            pltpu.VMEM(weight.shape, BF16),
            pltpu.VMEM(residual.shape, BF16),
            pltpu.VMEM((slots, depth), BF16),
            pltpu.VMEM((slots, width), F32),
            pltpu.SemaphoreType.DMA((steps + 3,)),
        ],
        compiler_params=pltpu.CompilerParams(vmem_limit_bytes=VMEM_LIMIT),
        cost_estimate=pl.CostEstimate(
            flops=2 * slots * depth * (width + rows),
            bytes_accessed=2 * depth * (width + rows),
            transcendentals=0,
        ),
    )(*[pltpu.with_memory_space_constraint(x, pltpu.HBM) for x in (dest, hidden, weight, residual)])


def keyval_kernel(parts, cores, *refs):
    texts, (gain_ref, *weights), out_ref = refs[:parts], refs[parts:-1], refs[-1]
    seq = lax.axis_index("seq")
    width = texts[0].shape[1]
    squares = 0.0
    for text in texts:
        wide = text[...].astype(F32)
        squares += jnp.sum(wide * wide, axis=1, keepdims=True)
    scale = lax.rsqrt(squares / (parts * width) + EPSILON)
    totals = [0.0] * cores
    for k, text in enumerate(texts):
        place = pl.ds(pl.multiple_of((seq ^ k) * width, width), width)
        normed = (text[...].astype(F32) * scale * gain_ref[:, place]).astype(BF16)
        for c, weight in enumerate(weights):
            totals[c] += jnp.dot(normed, weight[place, :], preferred_element_type=F32)
    each = weights[0].shape[1]
    for c in range(cores):
        out_ref[:, c * each:(c + 1) * each] = totals[c].astype(BF16)


def attend_kernel(parts, cores, heads_here, capacity, groups, dest_ref, query_ref, *refs):
    blocks, out_ref = refs[:-1], refs[-1]
    each = parts + cores - 1
    clip, seq, core = lax.axis_index("clip"), lax.axis_index("seq"), lax.axis_index("tp")
    clips = dest_ref.shape[0]
    slots = clips * capacity
    dim = query_ref.shape[1] // (parts * cores * heads_here)
    counts = jnp.sum((dest_ref[...] == clip).astype(jnp.int32), axis=1, keepdims=True)
    lane = lax.broadcasted_iota(jnp.int32, (clips, slots), 1)
    block = (lane // capacity) ^ (core * (clips // cores))
    source = jnp.zeros_like(lane)
    for place, offset in enumerate(route_offsets(clips, cores)):
        source = jnp.where(block == place, offset ^ clip, source)
    limit = jnp.sum(
        jnp.where(lax.broadcasted_iota(jnp.int32, lane.shape, 0) == source, counts, 0),
        axis=0, keepdims=True,
    )
    valid = lax.broadcasted_iota(jnp.int32, (1, slots), 1) % capacity < limit
    heads = [(k, c, i) for k in range(parts) for c in range(cores) for i in range(heads_here)]

    def columns(head):
        k, c, i = head
        at = ((seq ^ k) * cores + (core ^ c)) * heads_here + i
        return pl.ds(pl.multiple_of(at * dim, dim), dim)

    def stored(head, offset):
        k, c, i = head
        found = []
        for g in range(cores):
            at = ((c ^ g) * heads_here + i) * 2 * dim + offset
            for first in range(0, groups * each, each):
                if g == 0:
                    found.append(blocks[first + k][:, at:at + dim])
                else:
                    found.append(blocks[first + parts + g - 1][k, :, at:at + dim])
        return jnp.concatenate(found, axis=0)

    group = 8
    for first in range(0, len(heads), group):
        some = heads[first:first + group]
        scores = [
            lax.dot_general(
                query_ref[:, columns(head)], stored(head, 0), (((1,), (1,)), ((), ())),
                preferred_element_type=F32,
            )
            for head in some
        ]
        scores = [jnp.where(valid, score * (1.0 / math.sqrt(dim)), -1e30) for score in scores]
        peaks = [jnp.max(score, axis=1, keepdims=True) for score in scores]
        weights = [
            jnp.where(valid, jnp.exp(score - peak), 0.0) for score, peak in zip(scores, peaks)
        ]
        sums = [jnp.sum(weight, axis=1, keepdims=True) for weight in weights]
        probs = [(weight / total).astype(BF16) for weight, total in zip(weights, sums)]
        results = [
            jnp.dot(prob, stored(head, dim), preferred_element_type=F32).astype(BF16)
            for prob, head in zip(probs, some)
        ]
        for head, result in zip(some, results):
            out_ref[:, columns(head)] = result


def keyval(texts, gain, weights):
    parts, (rows, width) = len(texts), texts[0].shape
    wide = sum(weight.shape[1] for weight in weights)
    return pl.pallas_call(
        functools.partial(keyval_kernel, parts, len(weights)),
        in_specs=[whole()] * (parts + 1 + len(weights)),
        out_specs=whole(),
        out_shape=pltpu.VMEM((rows, wide), BF16),
        compiler_params=pltpu.CompilerParams(vmem_limit_bytes=VMEM_LIMIT),
        cost_estimate=pl.CostEstimate(
            flops=2 * rows * parts * width * wide,
            bytes_accessed=2 * parts * width * (rows + wide),
            transcendentals=0,
        ),
    )(*texts, gain, *weights)


def shards(ffn_hidden, ffn_weight, residual, norm_gain, kv_weight, destination, queries):
    clips, parts, cores = lax.axis_size("clip"), lax.axis_size("seq"), lax.axis_size("tp")
    rows = ffn_hidden.shape[0]
    capacity = rows // min(8, clips)
    share = clips * capacity // cores
    heads_here = kv_weight.shape[1]
    dest = destination.reshape(clips, rows)
    gain = norm_gain.reshape(1, -1)
    weight = kv_weight.reshape(kv_weight.shape[0], heads_here * kv_weight.shape[2])
    weights = [weight] + [swap(weight, "tp", g) for g in range(1, cores)]
    own, send, text = ffn(dest, ffn_hidden, ffn_weight, residual, capacity, cores)
    for g in range(1, cores):
        own = own + swap(send[(g - 1) * share:g * share], "tp", g)
    text = (text.astype(F32) + own).astype(BF16)
    places = clips // cores
    groups = math.gcd(2, places)
    blocks = []
    for first in range(0, places, places // groups):
        arrived = [
            route(text[i * capacity:(i + 1) * capacity], i)
            for i in range(first, first + places // groups)
        ]
        arrived = jnp.concatenate(arrived, axis=0)
        texts = [arrived] + [swap(arrived, "seq", k) for k in range(1, parts)]
        block = keyval(texts, gain, weights)
        block = [block] + [swap(block, "seq", k) for k in range(1, parts)]
        blocks += block + [swap(jnp.stack(block), "tp", g) for g in range(1, cores)]
    return pl.pallas_call(
        functools.partial(attend_kernel, parts, cores, heads_here, capacity, groups),
        in_specs=[whole()] * (2 + len(blocks)),
        out_specs=whole(),
        out_shape=jax.ShapeDtypeStruct(queries.shape, BF16),
        compiler_params=pltpu.CompilerParams(vmem_limit_bytes=VMEM_LIMIT),
    )(dest, queries, *blocks)


def solution(mesh):
    return jax.shard_map(
        shards,
        mesh=mesh,
        in_specs=(
            P("clip", "tp"),
            P("tp", "seq"),
            P("clip", "seq"),
            P(),
            P(None, ("seq", "tp"), None),
            P(),
            P(("clip", "seq", "tp"), None),
        ),
        out_specs=P(("clip", "seq", "tp"), None),
        check_vma=False,
    )
```

```python
import functools
import math

import jax
import jax.numpy as jnp
from jax import lax
from jax.experimental import pallas as pl
from jax.experimental.pallas import tpu as pltpu
from jax.sharding import PartitionSpec as P

EPSILON = 1e-06
VMEM_LIMIT = 24 * 1024 * 1024
VMEM_ALL = 60 * 1024 * 1024
F32 = jnp.float32
BF16 = jnp.bfloat16


def whole():
    return pl.BlockSpec(memory_space=pltpu.VMEM)


def swap(value, axis, offset):
    size = lax.axis_size(axis)
    return lax.ppermute(value, axis, [(i, i ^ offset) for i in range(size)])


def route_offsets(clips, cores):
    if clips == 4 and cores == 2:
        return [0, 3, 1, 2]
    return list(range(clips))


def deliver(value, place, step):
    clips, parts, cores = lax.axis_size("clip"), lax.axis_size("seq"), lax.axis_size("tp")
    offsets = route_offsets(clips, cores)
    pairs = []
    for i in range(clips):
        for s in range(parts):
            for t in range(cores):
                to = i ^ offsets[t * (clips // cores) + place]
                pairs.append(((i * parts + s) * cores + t, (to * parts + (s ^ step)) * cores + t))
    return lax.ppermute(value, ("clip", "seq", "tp"), pairs)


def slot_select(dest_ref, clip, core, capacity, cores):
    clips, rows = dest_ref.shape
    named = dest_ref[pl.ds(clip, 1), :]
    onehot = (lax.broadcasted_iota(jnp.int32, (clips, rows), 0) == named).astype(F32)
    earlier = (
        lax.broadcasted_iota(jnp.int32, (rows, rows), 0)
        < lax.broadcasted_iota(jnp.int32, (rows, rows), 1)
    ).astype(F32)
    before = jnp.dot(onehot, earlier, preferred_element_type=F32)
    rank = jnp.sum(before * onehot, axis=0, keepdims=True).astype(jnp.int32)
    away = named ^ clip
    block = jnp.zeros_like(away)
    for place, offset in enumerate(route_offsets(clips, cores)):
        block = jnp.where(away == offset, place, block)
    slot = (block ^ (core * (clips // cores))) * capacity + rank
    return (lax.broadcasted_iota(jnp.int32, (clips * capacity, rows), 0) == slot).astype(BF16)


def ffn_kernel(capacity, cores, steps, dest_hbm, hidden_hbm, weight_hbm, residual_hbm,
               own_ref, send_ref, text_ref, dest_ref, hidden_ref, weight_ref, residual_ref,
               packed_ref, total_ref, sems):
    clip, core = lax.axis_index("clip"), lax.axis_index("tp")
    share = own_ref.shape[0]
    block = hidden_hbm.shape[1] // steps
    get_dest = pltpu.make_async_copy(dest_hbm, dest_ref, sems.at[steps])
    get_hidden = pltpu.make_async_copy(hidden_hbm, hidden_ref, sems.at[steps + 1])
    get_residual = pltpu.make_async_copy(residual_hbm, residual_ref, sems.at[steps + 2])
    get_weight = [
        pltpu.make_async_copy(
            weight_hbm.at[pl.ds(i * block, block), :],
            weight_ref.at[pl.ds(i * block, block), :],
            sems.at[i],
        )
        for i in range(steps)
    ]
    for copy in [get_dest, get_hidden] + get_weight + [get_residual]:
        copy.start()
    get_dest.wait()
    select = slot_select(dest_ref, clip, core, capacity, cores)
    get_hidden.wait()
    packed_ref[...] = jnp.dot(select, hidden_ref[...], preferred_element_type=F32).astype(BF16)
    for i in range(steps):
        part = pl.ds(i * block, block)
        get_weight[i].wait()
        product = jnp.dot(packed_ref[:, part], weight_ref[part, :], preferred_element_type=F32)
        if i == 0:
            total_ref[...] = product
        elif i < steps - 1:
            total_ref[...] += product
        else:
            own_ref[...] = total_ref[:share, :] + product[:share]
            send_ref[...] = total_ref[share:, :] + product[share:]
    get_residual.wait()
    text_ref[...] = jnp.dot(
        select[:share], residual_ref[...], preferred_element_type=F32
    ).astype(BF16)


def ffn(dest, hidden, weight, residual, capacity, cores):
    rows, depth = hidden.shape
    width = weight.shape[1]
    slots = dest.shape[0] * capacity
    share = slots // cores
    steps = math.gcd(5, depth // 128)
    return pl.pallas_call(
        functools.partial(ffn_kernel, capacity, cores, steps),
        in_specs=[pl.BlockSpec(memory_space=pltpu.HBM)] * 4,
        out_specs=[whole()] * 3,
        out_shape=[
            pltpu.VMEM((share, width), F32),
            pltpu.VMEM((slots - share, width), F32),
            pltpu.VMEM((share, width), BF16),
        ],
        scratch_shapes=[
            pltpu.VMEM(dest.shape, jnp.int32),
            pltpu.VMEM(hidden.shape, BF16),
            pltpu.VMEM(weight.shape, BF16),
            pltpu.VMEM(residual.shape, BF16),
            pltpu.VMEM((slots, depth), BF16),
            pltpu.VMEM((slots, width), F32),
            pltpu.SemaphoreType.DMA((steps + 3,)),
        ],
        compiler_params=pltpu.CompilerParams(vmem_limit_bytes=VMEM_LIMIT),
        cost_estimate=pl.CostEstimate(
            flops=2 * slots * depth * (width + rows),
            bytes_accessed=2 * depth * (width + rows),
            transcendentals=0,
        ),
    )(*[pltpu.with_memory_space_constraint(x, pltpu.HBM) for x in (dest, hidden, weight, residual)])


def keyval_kernel(parts, cores, *refs):
    texts, (gain_ref, *weights), out_ref = refs[:parts], refs[parts:-1], refs[-1]
    seq = lax.axis_index("seq")
    width = texts[0].shape[1]
    squares = 0.0
    for text in texts:
        wide = text[...].astype(F32)
        squares += jnp.sum(wide * wide, axis=1, keepdims=True)
    scale = lax.rsqrt(squares / (parts * width) + EPSILON)
    totals = [0.0] * cores
    for k, text in enumerate(texts):
        place = pl.ds(pl.multiple_of((seq ^ k) * width, width), width)
        normed = (text[...].astype(F32) * scale * gain_ref[:, place]).astype(BF16)
        for c, weight in enumerate(weights):
            totals[c] += jnp.dot(normed, weight[place, :], preferred_element_type=F32)
    each = weights[0].shape[1]
    for c in range(cores):
        out_ref[:, c * each:(c + 1) * each] = totals[c].astype(BF16)


def attend_kernel(parts, cores, heads_here, capacity, pieces, dest_ref, query_ref, *refs):
    own, others, out_ref = refs[:parts * pieces], refs[parts * pieces:-1], refs[-1]
    clip, seq, core = lax.axis_index("clip"), lax.axis_index("seq"), lax.axis_index("tp")
    clips = dest_ref.shape[0]
    slots = clips * capacity
    dim = query_ref.shape[1] // (parts * cores * heads_here)
    counts = jnp.sum((dest_ref[...] == clip).astype(jnp.int32), axis=1, keepdims=True)
    lane = lax.broadcasted_iota(jnp.int32, (clips, slots), 1)
    block = (lane // capacity) ^ (core * (clips // cores))
    source = jnp.zeros_like(lane)
    for place, offset in enumerate(route_offsets(clips, cores)):
        source = jnp.where(block == place, offset ^ clip, source)
    limit = jnp.sum(
        jnp.where(lax.broadcasted_iota(jnp.int32, lane.shape, 0) == source, counts, 0),
        axis=0, keepdims=True,
    )
    valid = lax.broadcasted_iota(jnp.int32, (1, slots), 1) % capacity < limit
    heads = [(k, c, i) for k in range(parts) for c in range(cores) for i in range(heads_here)]

    def columns(head):
        k, c, i = head
        at = ((seq ^ k) * cores + (core ^ c)) * heads_here + i
        return pl.ds(pl.multiple_of(at * dim, dim), dim)

    def stored(head, offset):
        k, c, i = head
        found = []
        for g in range(cores):
            at = ((c ^ g) * heads_here + i) * 2 * dim + offset
            if g == 0:
                found += [own[k * pieces + p][:, at:at + dim] for p in range(pieces)]
            else:
                found.append(others[g - 1][k, :, at:at + dim])
        return jnp.concatenate(found, axis=0)

    group = 8
    for first in range(0, len(heads), group):
        some = heads[first:first + group]
        scores = [
            lax.dot_general(
                query_ref[:, columns(head)], stored(head, 0), (((1,), (1,)), ((), ())),
                preferred_element_type=F32,
            )
            for head in some
        ]
        scores = [jnp.where(valid, score * (1.0 / math.sqrt(dim)), -1e30) for score in scores]
        peaks = [jnp.max(score, axis=1, keepdims=True) for score in scores]
        weights = [
            jnp.where(valid, jnp.exp(score - peak), 0.0) for score, peak in zip(scores, peaks)
        ]
        sums = [jnp.sum(weight, axis=1, keepdims=True) for weight in weights]
        probs = [(weight / total).astype(BF16) for weight, total in zip(weights, sums)]
        results = [
            jnp.dot(prob, stored(head, dim), preferred_element_type=F32).astype(BF16)
            for prob, head in zip(probs, some)
        ]
        for head, result in zip(some, results):
            out_ref[:, columns(head)] = result


def keyval(texts, gain, weights):
    parts, (rows, width) = len(texts), texts[0].shape
    wide = sum(weight.shape[1] for weight in weights)
    return pl.pallas_call(
        functools.partial(keyval_kernel, parts, len(weights)),
        in_specs=[whole()] * (parts + 1 + len(weights)),
        out_specs=whole(),
        out_shape=pltpu.VMEM((rows, wide), BF16),
        compiler_params=pltpu.CompilerParams(vmem_limit_bytes=VMEM_LIMIT),
        cost_estimate=pl.CostEstimate(
            flops=2 * rows * parts * width * wide,
            bytes_accessed=2 * parts * width * (rows + wide),
            transcendentals=0,
        ),
    )(*texts, gain, *weights)


def shards(ffn_hidden, ffn_weight, residual, norm_gain, kv_weight, destination, queries):
    clips, parts, cores = lax.axis_size("clip"), lax.axis_size("seq"), lax.axis_size("tp")
    rows = ffn_hidden.shape[0]
    capacity = rows // min(8, clips)
    share = clips * capacity // cores
    heads_here = kv_weight.shape[1]
    dest = destination.reshape(clips, rows)
    gain = norm_gain.reshape(1, -1)
    weight = kv_weight.reshape(kv_weight.shape[0], heads_here * kv_weight.shape[2])
    weights = [weight] + [swap(weight, "tp", g) for g in range(1, cores)]
    own, send, text = ffn(dest, ffn_hidden, ffn_weight, residual, capacity, cores)
    for g in range(1, cores):
        own = own + swap(send[(g - 1) * share:g * share], "tp", g)
    text = (text.astype(F32) + own).astype(BF16)
    texts = [text] + [swap(text, "seq", k) for k in range(1, parts)]
    block = keyval(texts, gain, weights)
    places = clips // cores
    block = [block[i * capacity:(i + 1) * capacity] for i in range(places)]
    if places <= 2:
        order = list(range(parts))[::-1]
        found = {(k, i): deliver(block[i], i, k) for k in order for i in range(places)}
        own = [[found[k, i] for i in range(places)] for k in range(parts)]
    else:
        block = jnp.concatenate([deliver(block[i], i, 0) for i in range(places)], axis=0)
        own = [[block]] + [[swap(block, "seq", k)] for k in range(1, parts)]
    pieces = len(own[0])
    own = [piece for some in own for piece in some]
    packed = jnp.concatenate(own, axis=0).reshape(parts, share, -1)
    others = [swap(packed, "tp", g) for g in range(1, cores)]
    return pl.pallas_call(
        functools.partial(attend_kernel, parts, cores, heads_here, capacity, pieces),
        in_specs=[whole()] * (2 + len(own) + len(others)),
        out_specs=whole(),
        out_shape=jax.ShapeDtypeStruct(queries.shape, BF16),
        compiler_params=pltpu.CompilerParams(vmem_limit_bytes=VMEM_LIMIT),
    )(dest, queries, *own, *others)


def solution(mesh):
    return jax.shard_map(
        shards,
        mesh=mesh,
        in_specs=(
            P("clip", "tp"),
            P("tp", "seq"),
            P("clip", "seq"),
            P(),
            P(None, ("seq", "tp"), None),
            P(),
            P(("clip", "seq", "tp"), None),
        ),
        out_specs=P(("clip", "seq", "tp"), None),
        check_vma=False,
    )
```

```python
import functools
import math

import jax
import jax.numpy as jnp
from jax import lax
from jax.experimental import pallas as pl
from jax.experimental.pallas import tpu as pltpu
from jax.sharding import PartitionSpec as P

EPSILON = 1e-06
VMEM_LIMIT = 24 * 1024 * 1024
VMEM_ALL = 60 * 1024 * 1024
F32 = jnp.float32
BF16 = jnp.bfloat16


def whole():
    return pl.BlockSpec(memory_space=pltpu.VMEM)


def swap(value, axis, offset):
    size = lax.axis_size(axis)
    return lax.ppermute(value, axis, [(i, i ^ offset) for i in range(size)])


def route_offsets(clips, cores):
    if clips == 4 and cores == 2:
        return [0, 3, 1, 2]
    return list(range(clips))


def route(value, place):
    clips, cores = lax.axis_size("clip"), lax.axis_size("tp")
    offsets = route_offsets(clips, cores)
    here = [offsets[t * (clips // cores) + place] for t in range(cores)]
    pairs = [
        (i * cores + t, (i ^ here[t]) * cores + t)
        for i in range(clips) for t in range(cores) if here[t]
    ]
    moved = lax.ppermute(value, ("clip", "tp"), pairs)
    if all(here):
        return moved
    return jnp.where(lax.axis_index("tp") == here.index(0), value, moved)


def slot_select(dest_ref, clip, core, capacity, cores):
    clips, rows = dest_ref.shape
    named = dest_ref[pl.ds(clip, 1), :]
    onehot = (lax.broadcasted_iota(jnp.int32, (clips, rows), 0) == named).astype(F32)
    earlier = (
        lax.broadcasted_iota(jnp.int32, (rows, rows), 0)
        < lax.broadcasted_iota(jnp.int32, (rows, rows), 1)
    ).astype(F32)
    before = jnp.dot(onehot, earlier, preferred_element_type=F32)
    rank = jnp.sum(before * onehot, axis=0, keepdims=True).astype(jnp.int32)
    away = named ^ clip
    block = jnp.zeros_like(away)
    for place, offset in enumerate(route_offsets(clips, cores)):
        block = jnp.where(away == offset, place, block)
    slot = (block ^ (core * (clips // cores))) * capacity + rank
    return (lax.broadcasted_iota(jnp.int32, (clips * capacity, rows), 0) == slot).astype(BF16)


def ffn_kernel(capacity, cores, steps, dest_hbm, hidden_hbm, weight_hbm, residual_hbm,
               own_ref, send_ref, text_ref, dest_ref, hidden_ref, weight_ref, residual_ref,
               packed_ref, total_ref, sems):
    clip, core = lax.axis_index("clip"), lax.axis_index("tp")
    share = own_ref.shape[0]
    block = hidden_hbm.shape[1] // steps
    get_dest = pltpu.make_async_copy(dest_hbm, dest_ref, sems.at[steps])
    get_hidden = pltpu.make_async_copy(hidden_hbm, hidden_ref, sems.at[steps + 1])
    get_residual = pltpu.make_async_copy(residual_hbm, residual_ref, sems.at[steps + 2])
    get_weight = [
        pltpu.make_async_copy(
            weight_hbm.at[pl.ds(i * block, block), :],
            weight_ref.at[pl.ds(i * block, block), :],
            sems.at[i],
        )
        for i in range(steps)
    ]
    for copy in [get_dest, get_hidden] + get_weight + [get_residual]:
        copy.start()
    get_dest.wait()
    select = slot_select(dest_ref, clip, core, capacity, cores)
    get_hidden.wait()
    packed_ref[...] = jnp.dot(select, hidden_ref[...], preferred_element_type=F32).astype(BF16)
    for i in range(steps):
        part = pl.ds(i * block, block)
        get_weight[i].wait()
        product = jnp.dot(packed_ref[:, part], weight_ref[part, :], preferred_element_type=F32)
        if i == 0:
            total_ref[...] = product
        elif i < steps - 1:
            total_ref[...] += product
        else:
            own_ref[...] = total_ref[:share, :] + product[:share]
            send_ref[...] = total_ref[share:, :] + product[share:]
    get_residual.wait()
    text_ref[...] = jnp.dot(
        select[:share], residual_ref[...], preferred_element_type=F32
    ).astype(BF16)


def ffn(dest, hidden, weight, residual, capacity, cores):
    rows, depth = hidden.shape
    width = weight.shape[1]
    slots = dest.shape[0] * capacity
    share = slots // cores
    steps = math.gcd(5, depth // 128)
    return pl.pallas_call(
        functools.partial(ffn_kernel, capacity, cores, steps),
        in_specs=[pl.BlockSpec(memory_space=pltpu.HBM)] * 4,
        out_specs=[whole()] * 3,
        out_shape=[
            pltpu.VMEM((share, width), F32),
            pltpu.VMEM((slots - share, width), F32),
            pltpu.VMEM((share, width), BF16),
        ],
        scratch_shapes=[
            pltpu.VMEM(dest.shape, jnp.int32),
            pltpu.VMEM(hidden.shape, BF16),
            pltpu.VMEM(weight.shape, BF16),
            pltpu.VMEM(residual.shape, BF16),
            pltpu.VMEM((slots, depth), BF16),
            pltpu.VMEM((slots, width), F32),
            pltpu.SemaphoreType.DMA((steps + 3,)),
        ],
        compiler_params=pltpu.CompilerParams(vmem_limit_bytes=VMEM_LIMIT),
        cost_estimate=pl.CostEstimate(
            flops=2 * slots * depth * (width + rows),
            bytes_accessed=2 * depth * (width + rows),
            transcendentals=0,
        ),
    )(*[pltpu.with_memory_space_constraint(x, pltpu.HBM) for x in (dest, hidden, weight, residual)])


def keyval_kernel(parts, cores, *refs):
    texts, (gain_ref, *weights), out_ref = refs[:parts], refs[parts:-1], refs[-1]
    seq = lax.axis_index("seq")
    width = texts[0].shape[1]
    squares = 0.0
    for text in texts:
        wide = text[...].astype(F32)
        squares += jnp.sum(wide * wide, axis=1, keepdims=True)
    scale = lax.rsqrt(squares / (parts * width) + EPSILON)
    totals = [0.0] * cores
    for k, text in enumerate(texts):
        place = pl.ds(pl.multiple_of((seq ^ k) * width, width), width)
        normed = (text[...].astype(F32) * scale * gain_ref[:, place]).astype(BF16)
        for c, weight in enumerate(weights):
            totals[c] += jnp.dot(normed, weight[place, :], preferred_element_type=F32)
    each = weights[0].shape[1]
    for c in range(cores):
        out_ref[:, c * each:(c + 1) * each] = totals[c].astype(BF16)


def attend_kernel(parts, cores, heads_here, capacity, groups, dest_ref, query_ref, *refs):
    own, others, out_ref = refs[:parts * groups], refs[parts * groups:-1], refs[-1]
    clip, seq, core = lax.axis_index("clip"), lax.axis_index("seq"), lax.axis_index("tp")
    clips = dest_ref.shape[0]
    slots = clips * capacity
    dim = query_ref.shape[1] // (parts * cores * heads_here)
    counts = jnp.sum((dest_ref[...] == clip).astype(jnp.int32), axis=1, keepdims=True)
    lane = lax.broadcasted_iota(jnp.int32, (clips, slots), 1)
    block = (lane // capacity) ^ (core * (clips // cores))
    source = jnp.zeros_like(lane)
    for place, offset in enumerate(route_offsets(clips, cores)):
        source = jnp.where(block == place, offset ^ clip, source)
    limit = jnp.sum(
        jnp.where(lax.broadcasted_iota(jnp.int32, lane.shape, 0) == source, counts, 0),
        axis=0, keepdims=True,
    )
    valid = lax.broadcasted_iota(jnp.int32, (1, slots), 1) % capacity < limit
    heads = [(k, c, i) for k in range(parts) for c in range(cores) for i in range(heads_here)]

    def columns(head):
        k, c, i = head
        at = ((seq ^ k) * cores + (core ^ c)) * heads_here + i
        return pl.ds(pl.multiple_of(at * dim, dim), dim)

    def stored(head, offset):
        k, c, i = head
        found = []
        for g in range(cores):
            at = ((c ^ g) * heads_here + i) * 2 * dim + offset
            if g == 0:
                found += [own[n * parts + k][:, at:at + dim] for n in range(groups)]
            else:
                found += [others[g - 1][n * parts + k, :, at:at + dim] for n in range(groups)]
        return jnp.concatenate(found, axis=0)

    group = 8
    for first in range(0, len(heads), group):
        some = heads[first:first + group]
        scores = [
            lax.dot_general(
                query_ref[:, columns(head)], stored(head, 0), (((1,), (1,)), ((), ())),
                preferred_element_type=F32,
            )
            for head in some
        ]
        scores = [jnp.where(valid, score * (1.0 / math.sqrt(dim)), -1e30) for score in scores]
        peaks = [jnp.max(score, axis=1, keepdims=True) for score in scores]
        weights = [
            jnp.where(valid, jnp.exp(score - peak), 0.0) for score, peak in zip(scores, peaks)
        ]
        sums = [jnp.sum(weight, axis=1, keepdims=True) for weight in weights]
        probs = [(weight / total).astype(BF16) for weight, total in zip(weights, sums)]
        results = [
            jnp.dot(prob, stored(head, dim), preferred_element_type=F32).astype(BF16)
            for prob, head in zip(probs, some)
        ]
        for head, result in zip(some, results):
            out_ref[:, columns(head)] = result


def keyval(texts, gain, weights):
    parts, (rows, width) = len(texts), texts[0].shape
    wide = sum(weight.shape[1] for weight in weights)
    return pl.pallas_call(
        functools.partial(keyval_kernel, parts, len(weights)),
        in_specs=[whole()] * (parts + 1 + len(weights)),
        out_specs=whole(),
        out_shape=pltpu.VMEM((rows, wide), BF16),
        compiler_params=pltpu.CompilerParams(vmem_limit_bytes=VMEM_LIMIT),
        cost_estimate=pl.CostEstimate(
            flops=2 * rows * parts * width * wide,
            bytes_accessed=2 * parts * width * (rows + wide),
            transcendentals=0,
        ),
    )(*texts, gain, *weights)


def shards(ffn_hidden, ffn_weight, residual, norm_gain, kv_weight, destination, queries):
    clips, parts, cores = lax.axis_size("clip"), lax.axis_size("seq"), lax.axis_size("tp")
    rows = ffn_hidden.shape[0]
    capacity = rows // min(8, clips)
    share = clips * capacity // cores
    heads_here = kv_weight.shape[1]
    dest = destination.reshape(clips, rows)
    gain = norm_gain.reshape(1, -1)
    weight = kv_weight.reshape(kv_weight.shape[0], heads_here * kv_weight.shape[2])
    weights = [weight] + [swap(weight, "tp", g) for g in range(1, cores)]
    own, send, text = ffn(dest, ffn_hidden, ffn_weight, residual, capacity, cores)
    for g in range(1, cores):
        own = own + swap(send[(g - 1) * share:g * share], "tp", g)
    text = (text.astype(F32) + own).astype(BF16)
    places = clips // cores
    groups = math.gcd(2, places)
    own = []
    for first in range(0, places, places // groups):
        arrived = [
            route(text[i * capacity:(i + 1) * capacity], i)
            for i in range(first, first + places // groups)
        ]
        arrived = jnp.concatenate(arrived, axis=0)
        texts = [arrived] + [swap(arrived, "seq", k) for k in range(1, parts)]
        block = keyval(texts, gain, weights)
        own += [block] + [swap(block, "seq", k) for k in range(1, parts)]
    packed = jnp.stack(own)
    others = [swap(packed, "tp", g) for g in range(1, cores)]
    return pl.pallas_call(
        functools.partial(attend_kernel, parts, cores, heads_here, capacity, groups),
        in_specs=[whole()] * (2 + len(own) + len(others)),
        out_specs=whole(),
        out_shape=jax.ShapeDtypeStruct(queries.shape, BF16),
        compiler_params=pltpu.CompilerParams(vmem_limit_bytes=VMEM_LIMIT),
    )(dest, queries, *own, *others)


def solution(mesh):
    return jax.shard_map(
        shards,
        mesh=mesh,
        in_specs=(
            P("clip", "tp"),
            P("tp", "seq"),
            P("clip", "seq"),
            P(),
            P(None, ("seq", "tp"), None),
            P(),
            P(("clip", "seq", "tp"), None),
        ),
        out_specs=P(("clip", "seq", "tp"), None),
        check_vma=False,
    )
```

```python
import functools
import math

import jax
import jax.numpy as jnp
from jax import lax
from jax.experimental import pallas as pl
from jax.experimental.pallas import tpu as pltpu
from jax.sharding import PartitionSpec as P

EPSILON = 1e-06
VMEM_LIMIT = 24 * 1024 * 1024
VMEM_ALL = 60 * 1024 * 1024
F32 = jnp.float32
BF16 = jnp.bfloat16


def whole():
    return pl.BlockSpec(memory_space=pltpu.VMEM)


def swap(value, axis, offset):
    size = lax.axis_size(axis)
    return lax.ppermute(value, axis, [(i, i ^ offset) for i in range(size)])


def routing(clips, cores, capacity):
    if clips == 4 and cores == 2:
        half = capacity // 2
        runs = [
            [(0, 0, half), (3, 0, half), (1, 0, capacity)],
            [(0, half, half), (3, half, half), (2, 0, capacity)],
        ]
        return runs, [[0, 1], [2]]
    each = clips // cores
    runs = [[(t * each + i, 0, capacity) for i in range(each)] for t in range(cores)]
    return runs, [list(range(each))]


def route(value, offsets):
    clips, cores = lax.axis_size("clip"), lax.axis_size("tp")
    if not any(offsets):
        return value
    pairs = [
        (i * cores + t, (i ^ offsets[t]) * cores + t)
        for i in range(clips) for t in range(cores) if offsets[t]
    ]
    moved = lax.ppermute(value, ("clip", "tp"), pairs)
    if all(offsets):
        return moved
    return jnp.where(lax.axis_index("tp") == offsets.index(0), value, moved)


def slot_select(dest_ref, clip, core, capacity, cores):
    clips, rows = dest_ref.shape
    named = dest_ref[pl.ds(clip, 1), :]
    onehot = (lax.broadcasted_iota(jnp.int32, (clips, rows), 0) == named).astype(F32)
    earlier = (
        lax.broadcasted_iota(jnp.int32, (rows, rows), 0)
        < lax.broadcasted_iota(jnp.int32, (rows, rows), 1)
    ).astype(F32)
    before = jnp.dot(onehot, earlier, preferred_element_type=F32)
    rank = jnp.sum(before * onehot, axis=0, keepdims=True).astype(jnp.int32)
    away = named ^ clip
    slot = jnp.zeros_like(away)
    share = clips * capacity // cores
    for t, runs in enumerate(routing(clips, cores, capacity)[0]):
        at = 0
        for offset, first, count in runs:
            inside = (away == offset) & (rank >= first) & (rank < first + count)
            slot = jnp.where(inside, (core ^ t) * share + at - first + rank, slot)
            at += count
    return (lax.broadcasted_iota(jnp.int32, (clips * capacity, rows), 0) == slot).astype(BF16)


def ffn_kernel(capacity, cores, steps, dest_hbm, hidden_hbm, weight_hbm, residual_hbm,
               own_ref, send_ref, text_ref, dest_ref, hidden_ref, weight_ref, residual_ref,
               packed_ref, total_ref, sems):
    clip, core = lax.axis_index("clip"), lax.axis_index("tp")
    share = own_ref.shape[0]
    block = hidden_hbm.shape[1] // steps
    get_dest = pltpu.make_async_copy(dest_hbm, dest_ref, sems.at[steps])
    get_hidden = pltpu.make_async_copy(hidden_hbm, hidden_ref, sems.at[steps + 1])
    get_residual = pltpu.make_async_copy(residual_hbm, residual_ref, sems.at[steps + 2])
    get_weight = [
        pltpu.make_async_copy(
            weight_hbm.at[pl.ds(i * block, block), :],
            weight_ref.at[pl.ds(i * block, block), :],
            sems.at[i],
        )
        for i in range(steps)
    ]
    for copy in [get_dest, get_hidden] + get_weight + [get_residual]:
        copy.start()
    get_dest.wait()
    select = slot_select(dest_ref, clip, core, capacity, cores)
    get_hidden.wait()
    packed_ref[...] = jnp.dot(select, hidden_ref[...], preferred_element_type=F32).astype(BF16)
    for i in range(steps):
        part = pl.ds(i * block, block)
        get_weight[i].wait()
        product = jnp.dot(packed_ref[:, part], weight_ref[part, :], preferred_element_type=F32)
        if i == 0:
            total_ref[...] = product
        elif i < steps - 1:
            total_ref[...] += product
        else:
            own_ref[...] = total_ref[:share, :] + product[:share]
            send_ref[...] = total_ref[share:, :] + product[share:]
    get_residual.wait()
    text_ref[...] = jnp.dot(
        select[:share], residual_ref[...], preferred_element_type=F32
    ).astype(BF16)


def ffn(dest, hidden, weight, residual, capacity, cores):
    rows, depth = hidden.shape
    width = weight.shape[1]
    slots = dest.shape[0] * capacity
    share = slots // cores
    steps = math.gcd(5, depth // 128)
    return pl.pallas_call(
        functools.partial(ffn_kernel, capacity, cores, steps),
        in_specs=[pl.BlockSpec(memory_space=pltpu.HBM)] * 4,
        out_specs=[whole()] * 3,
        out_shape=[
            pltpu.VMEM((share, width), F32),
            pltpu.VMEM((slots - share, width), F32),
            pltpu.VMEM((share, width), BF16),
        ],
        scratch_shapes=[
            pltpu.VMEM(dest.shape, jnp.int32),
            pltpu.VMEM(hidden.shape, BF16),
            pltpu.VMEM(weight.shape, BF16),
            pltpu.VMEM(residual.shape, BF16),
            pltpu.VMEM((slots, depth), BF16),
            pltpu.VMEM((slots, width), F32),
            pltpu.SemaphoreType.DMA((steps + 3,)),
        ],
        compiler_params=pltpu.CompilerParams(vmem_limit_bytes=VMEM_LIMIT),
        cost_estimate=pl.CostEstimate(
            flops=2 * slots * depth * (width + rows),
            bytes_accessed=2 * depth * (width + rows),
            transcendentals=0,
        ),
    )(*[pltpu.with_memory_space_constraint(x, pltpu.HBM) for x in (dest, hidden, weight, residual)])


def keyval_kernel(parts, cores, *refs):
    texts, (gain_ref, *weights), out_ref = refs[:parts], refs[parts:-1], refs[-1]
    seq = lax.axis_index("seq")
    width = texts[0].shape[1]
    squares = 0.0
    for text in texts:
        wide = text[...].astype(F32)
        squares += jnp.sum(wide * wide, axis=1, keepdims=True)
    scale = lax.rsqrt(squares / (parts * width) + EPSILON)
    totals = [0.0] * cores
    for k, text in enumerate(texts):
        place = pl.ds(pl.multiple_of((seq ^ k) * width, width), width)
        normed = (text[...].astype(F32) * scale * gain_ref[:, place]).astype(BF16)
        for c, weight in enumerate(weights):
            totals[c] += jnp.dot(normed, weight[place, :], preferred_element_type=F32)
    each = weights[0].shape[1]
    for c in range(cores):
        out_ref[:, c * each:(c + 1) * each] = totals[c].astype(BF16)


def attend_kernel(parts, cores, heads_here, capacity, groups, dest_ref, query_ref, *refs):
    own, others, out_ref = refs[:parts * groups], refs[parts * groups:-1], refs[-1]
    clip, seq, core = lax.axis_index("clip"), lax.axis_index("seq"), lax.axis_index("tp")
    clips = dest_ref.shape[0]
    slots = clips * capacity
    dim = query_ref.shape[1] // (parts * cores * heads_here)
    counts = jnp.sum((dest_ref[...] == clip).astype(jnp.int32), axis=1, keepdims=True)
    share = slots // cores
    lane = lax.broadcasted_iota(jnp.int32, (clips, slots), 1)
    owner, place = (lane // share) ^ core, lane % share
    source, rank = jnp.zeros_like(lane), jnp.zeros_like(lane)
    for t, runs in enumerate(routing(clips, cores, capacity)[0]):
        at = 0
        for offset, first, count in runs:
            inside = (owner == t) & (place >= at) & (place < at + count)
            source = jnp.where(inside, offset ^ clip, source)
            rank = jnp.where(inside, first + place - at, rank)
            at += count
    here = lax.broadcasted_iota(jnp.int32, lane.shape, 0) == source
    valid = jnp.sum(jnp.where(here & (rank < counts), 1, 0), axis=0, keepdims=True) > 0
    heads = [(k, c, i) for k in range(parts) for c in range(cores) for i in range(heads_here)]

    def columns(head):
        k, c, i = head
        at = ((seq ^ k) * cores + (core ^ c)) * heads_here + i
        return pl.ds(pl.multiple_of(at * dim, dim), dim)

    def stored(head, offset):
        k, c, i = head
        found = []
        for g in range(cores):
            at = ((c ^ g) * heads_here + i) * 2 * dim + offset
            if g == 0:
                found += [own[n * parts + k][:, at:at + dim] for n in range(groups)]
            else:
                found += [others[g - 1][n * parts + k, :, at:at + dim] for n in range(groups)]
        return jnp.concatenate(found, axis=0)

    group = 8
    for first in range(0, len(heads), group):
        some = heads[first:first + group]
        scores = [
            lax.dot_general(
                query_ref[:, columns(head)], stored(head, 0), (((1,), (1,)), ((), ())),
                preferred_element_type=F32,
            )
            for head in some
        ]
        scores = [jnp.where(valid, score * (1.0 / math.sqrt(dim)), -1e30) for score in scores]
        peaks = [jnp.max(score, axis=1, keepdims=True) for score in scores]
        weights = [
            jnp.where(valid, jnp.exp(score - peak), 0.0) for score, peak in zip(scores, peaks)
        ]
        sums = [jnp.sum(weight, axis=1, keepdims=True) for weight in weights]
        probs = [(weight / total).astype(BF16) for weight, total in zip(weights, sums)]
        results = [
            jnp.dot(prob, stored(head, dim), preferred_element_type=F32).astype(BF16)
            for prob, head in zip(probs, some)
        ]
        for head, result in zip(some, results):
            out_ref[:, columns(head)] = result


def keyval(texts, gain, weights):
    parts, (rows, width) = len(texts), texts[0].shape
    wide = sum(weight.shape[1] for weight in weights)
    return pl.pallas_call(
        functools.partial(keyval_kernel, parts, len(weights)),
        in_specs=[whole()] * (parts + 1 + len(weights)),
        out_specs=whole(),
        out_shape=pltpu.VMEM((rows, wide), BF16),
        compiler_params=pltpu.CompilerParams(vmem_limit_bytes=VMEM_LIMIT),
        cost_estimate=pl.CostEstimate(
            flops=2 * rows * parts * width * wide,
            bytes_accessed=2 * parts * width * (rows + wide),
            transcendentals=0,
        ),
    )(*texts, gain, *[pltpu.with_memory_space_constraint(x, pltpu.VMEM) for x in weights])


def shards(ffn_hidden, ffn_weight, residual, norm_gain, kv_weight, destination, queries):
    clips, parts, cores = lax.axis_size("clip"), lax.axis_size("seq"), lax.axis_size("tp")
    rows = ffn_hidden.shape[0]
    capacity = rows // min(8, clips)
    share = clips * capacity // cores
    heads_here = kv_weight.shape[1]
    dest = destination.reshape(clips, rows)
    gain = norm_gain.reshape(1, -1)
    weight = kv_weight.reshape(kv_weight.shape[0], heads_here * kv_weight.shape[2])
    weights = [weight] + [swap(weight, "tp", g) for g in range(1, cores)]
    own, send, text = ffn(dest, ffn_hidden, ffn_weight, residual, capacity, cores)
    for g in range(1, cores):
        own = own + swap(send[(g - 1) * share:g * share], "tp", g)
    text = (text.astype(F32) + own).astype(BF16)
    runs, groups = routing(clips, cores, capacity)
    edges = [sum(run[2] for run in runs[0][:n]) for n in range(len(runs[0]) + 1)]
    arrived = [
        route(text[edges[n]:edges[n + 1]], [some[n][0] for some in runs])
        for n in range(len(runs[0]))
    ]
    own = []
    for group in groups:
        mine = jnp.concatenate([arrived[n] for n in group], axis=0)
        texts = [mine] + [swap(mine, "seq", k) for k in range(1, parts)]
        block = keyval(texts, gain, weights)
        own += [block] + [swap(block, "seq", k) for k in range(1, parts)]
    packed = jnp.stack(own)
    others = [swap(packed, "tp", g) for g in range(1, cores)]
    return pl.pallas_call(
        functools.partial(attend_kernel, parts, cores, heads_here, capacity, len(groups)),
        in_specs=[whole()] * (2 + len(own) + len(others)),
        out_specs=whole(),
        out_shape=jax.ShapeDtypeStruct(queries.shape, BF16),
        compiler_params=pltpu.CompilerParams(vmem_limit_bytes=VMEM_LIMIT),
    )(dest, queries, *own, *others)


def solution(mesh):
    return jax.shard_map(
        shards,
        mesh=mesh,
        in_specs=(
            P("clip", "tp"),
            P("tp", "seq"),
            P("clip", "seq"),
            P(),
            P(None, ("seq", "tp"), None),
            P(),
            P(("clip", "seq", "tp"), None),
        ),
        out_specs=P(("clip", "seq", "tp"), None),
        check_vma=False,
    )
```

```python
import functools
import math

import jax
import jax.numpy as jnp
from jax import lax
from jax.experimental import pallas as pl
from jax.experimental.pallas import tpu as pltpu
from jax.sharding import PartitionSpec as P

EPSILON = 1e-06
VMEM_LIMIT = 24 * 1024 * 1024
VMEM_ALL = 60 * 1024 * 1024
F32 = jnp.float32
BF16 = jnp.bfloat16


def whole():
    return pl.BlockSpec(memory_space=pltpu.VMEM)


def swap(value, axis, offset):
    size = lax.axis_size(axis)
    return lax.ppermute(value, axis, [(i, i ^ offset) for i in range(size)])


def routing(clips, cores, capacity):
    if clips == 4 and cores == 2:
        half = capacity // 2
        runs = [
            [(0, 0, half), (3, 0, half), (1, 0, capacity)],
            [(0, half, half), (3, half, half), (2, 0, capacity)],
        ]
        return runs, [[0, 1, 2]]
    each = clips // cores
    runs = [[(t * each + i, 0, capacity) for i in range(each)] for t in range(cores)]
    return runs, [list(range(each))]


def route(value, offsets):
    clips, cores = lax.axis_size("clip"), lax.axis_size("tp")
    if not any(offsets):
        return value
    pairs = [
        (i * cores + t, (i ^ offsets[t]) * cores + t)
        for i in range(clips) for t in range(cores) if offsets[t]
    ]
    moved = lax.ppermute(value, ("clip", "tp"), pairs)
    if all(offsets):
        return moved
    return jnp.where(lax.axis_index("tp") == offsets.index(0), value, moved)


def slot_select(dest_ref, clip, core, capacity, cores):
    clips, rows = dest_ref.shape
    named = dest_ref[pl.ds(clip, 1), :]
    onehot = (lax.broadcasted_iota(jnp.int32, (clips, rows), 0) == named).astype(F32)
    earlier = (
        lax.broadcasted_iota(jnp.int32, (rows, rows), 0)
        < lax.broadcasted_iota(jnp.int32, (rows, rows), 1)
    ).astype(F32)
    before = jnp.dot(onehot, earlier, preferred_element_type=F32)
    rank = jnp.sum(before * onehot, axis=0, keepdims=True).astype(jnp.int32)
    away = named ^ clip
    slot = jnp.zeros_like(away)
    share = clips * capacity // cores
    for t, runs in enumerate(routing(clips, cores, capacity)[0]):
        at = 0
        for offset, first, count in runs:
            inside = (away == offset) & (rank >= first) & (rank < first + count)
            slot = jnp.where(inside, (core ^ t) * share + at - first + rank, slot)
            at += count
    return (lax.broadcasted_iota(jnp.int32, (clips * capacity, rows), 0) == slot).astype(BF16)


def ffn_kernel(capacity, cores, steps, ahead, dest_hbm, hidden_hbm, weight_hbm, residual_hbm,
               own_ref, send_ref, text_ref, dest_ref, hidden_ref, weight_ref, residual_ref,
               total_ref, sems):
    clip, core = lax.axis_index("clip"), lax.axis_index("tp")
    share = own_ref.shape[0]
    block = hidden_hbm.shape[1] // steps
    get_dest = pltpu.make_async_copy(dest_hbm, dest_ref, sems.at[2 * steps])
    get_residual = pltpu.make_async_copy(residual_hbm, residual_ref, sems.at[2 * steps + 1])
    get_hidden, get_weight = [], []
    for i in range(steps):
        part = pl.ds(i * block, block)
        get_hidden.append(
            pltpu.make_async_copy(hidden_hbm.at[:, part], hidden_ref.at[:, part], sems.at[i])
        )
        get_weight.append(
            pltpu.make_async_copy(
                weight_hbm.at[part, :], weight_ref.at[part, :], sems.at[steps + i]
            )
        )

    def start(i):
        if i < steps:
            get_hidden[i].start()
            get_weight[i].start()
        elif i == steps:
            get_residual.start()

    get_dest.start()
    for i in range(ahead):
        start(i)
    get_dest.wait()
    select = slot_select(dest_ref, clip, core, capacity, cores)
    for i in range(steps):
        part = pl.ds(i * block, block)
        get_hidden[i].wait()
        packed = jnp.dot(select, hidden_ref[:, part], preferred_element_type=F32).astype(BF16)
        get_weight[i].wait()
        start(i + ahead)
        product = jnp.dot(packed, weight_ref[part, :], preferred_element_type=F32)
        if i == 0:
            total_ref[...] = product
        elif i < steps - 1:
            total_ref[...] += product
        else:
            own_ref[...] = total_ref[:share, :] + product[:share]
            send_ref[...] = total_ref[share:, :] + product[share:]
    get_residual.wait()
    text_ref[...] = jnp.dot(
        select[:share], residual_ref[...], preferred_element_type=F32
    ).astype(BF16)


def ffn(dest, hidden, weight, residual, capacity, cores):
    rows, depth = hidden.shape
    width = weight.shape[1]
    slots = dest.shape[0] * capacity
    share = slots // cores
    steps = math.gcd(10, depth // 128)
    ahead = min(3, steps)
    return pl.pallas_call(
        functools.partial(ffn_kernel, capacity, cores, steps, ahead),
        in_specs=[pl.BlockSpec(memory_space=pltpu.HBM)] * 4,
        out_specs=[whole()] * 3,
        out_shape=[
            pltpu.VMEM((share, width), F32),
            pltpu.VMEM((slots - share, width), F32),
            pltpu.VMEM((share, width), BF16),
        ],
        scratch_shapes=[
            pltpu.VMEM(dest.shape, jnp.int32),
            pltpu.VMEM(hidden.shape, BF16),
            pltpu.VMEM(weight.shape, BF16),
            pltpu.VMEM(residual.shape, BF16),
            pltpu.VMEM((slots, width), F32),
            pltpu.SemaphoreType.DMA((2 * steps + 2,)),
        ],
        compiler_params=pltpu.CompilerParams(vmem_limit_bytes=VMEM_LIMIT),
        cost_estimate=pl.CostEstimate(
            flops=2 * slots * depth * (width + rows),
            bytes_accessed=2 * depth * (width + rows),
            transcendentals=0,
        ),
    )(*[pltpu.with_memory_space_constraint(x, pltpu.HBM) for x in (dest, hidden, weight, residual)])


def keyval_kernel(parts, cores, *refs):
    texts, (gain_ref, *weights), out_ref = refs[:parts], refs[parts:-1], refs[-1]
    seq = lax.axis_index("seq")
    width = texts[0].shape[1]
    squares = 0.0
    for text in texts:
        wide = text[...].astype(F32)
        squares += jnp.sum(wide * wide, axis=1, keepdims=True)
    scale = lax.rsqrt(squares / (parts * width) + EPSILON)
    totals = [0.0] * cores
    for k, text in enumerate(texts):
        place = pl.ds(pl.multiple_of((seq ^ k) * width, width), width)
        normed = (text[...].astype(F32) * scale * gain_ref[:, place]).astype(BF16)
        for c, weight in enumerate(weights):
            totals[c] += jnp.dot(normed, weight[place, :], preferred_element_type=F32)
    each = weights[0].shape[1]
    for c in range(cores):
        out_ref[:, c * each:(c + 1) * each] = totals[c].astype(BF16)


def attend_kernel(parts, cores, heads_here, capacity, groups, dest_ref, query_ref, *refs):
    own, others, out_ref = refs[:parts * groups], refs[parts * groups:-1], refs[-1]
    clip, seq, core = lax.axis_index("clip"), lax.axis_index("seq"), lax.axis_index("tp")
    clips = dest_ref.shape[0]
    slots = clips * capacity
    dim = query_ref.shape[1] // (parts * cores * heads_here)
    counts = jnp.sum((dest_ref[...] == clip).astype(jnp.int32), axis=1, keepdims=True)
    share = slots // cores
    lane = lax.broadcasted_iota(jnp.int32, (clips, slots), 1)
    owner, place = (lane // share) ^ core, lane % share
    source, rank = jnp.zeros_like(lane), jnp.zeros_like(lane)
    for t, runs in enumerate(routing(clips, cores, capacity)[0]):
        at = 0
        for offset, first, count in runs:
            inside = (owner == t) & (place >= at) & (place < at + count)
            source = jnp.where(inside, offset ^ clip, source)
            rank = jnp.where(inside, first + place - at, rank)
            at += count
    here = lax.broadcasted_iota(jnp.int32, lane.shape, 0) == source
    valid = jnp.sum(jnp.where(here & (rank < counts), 1, 0), axis=0, keepdims=True) > 0
    heads = [(k, c, i) for k in range(parts) for c in range(cores) for i in range(heads_here)]

    def columns(head):
        k, c, i = head
        at = ((seq ^ k) * cores + (core ^ c)) * heads_here + i
        return pl.ds(pl.multiple_of(at * dim, dim), dim)

    def stored(head, offset):
        k, c, i = head
        found = []
        for g in range(cores):
            at = ((c ^ g) * heads_here + i) * 2 * dim + offset
            if g == 0:
                found += [own[n * parts + k][:, at:at + dim] for n in range(groups)]
            else:
                found += [others[g - 1][n * parts + k, :, at:at + dim] for n in range(groups)]
        return jnp.concatenate(found, axis=0)

    group = 8
    for first in range(0, len(heads), group):
        some = heads[first:first + group]
        scores = [
            lax.dot_general(
                query_ref[:, columns(head)], stored(head, 0), (((1,), (1,)), ((), ())),
                preferred_element_type=F32,
            )
            for head in some
        ]
        scores = [jnp.where(valid, score * (1.0 / math.sqrt(dim)), -1e30) for score in scores]
        peaks = [jnp.max(score, axis=1, keepdims=True) for score in scores]
        weights = [
            jnp.where(valid, jnp.exp(score - peak), 0.0) for score, peak in zip(scores, peaks)
        ]
        sums = [jnp.sum(weight, axis=1, keepdims=True) for weight in weights]
        probs = [(weight / total).astype(BF16) for weight, total in zip(weights, sums)]
        results = [
            jnp.dot(prob, stored(head, dim), preferred_element_type=F32).astype(BF16)
            for prob, head in zip(probs, some)
        ]
        for head, result in zip(some, results):
            out_ref[:, columns(head)] = result


def keyval(texts, gain, weights):
    parts, (rows, width) = len(texts), texts[0].shape
    wide = sum(weight.shape[1] for weight in weights)
    return pl.pallas_call(
        functools.partial(keyval_kernel, parts, len(weights)),
        in_specs=[whole()] * (parts + 1 + len(weights)),
        out_specs=whole(),
        out_shape=pltpu.VMEM((rows, wide), BF16),
        compiler_params=pltpu.CompilerParams(vmem_limit_bytes=VMEM_LIMIT),
        cost_estimate=pl.CostEstimate(
            flops=2 * rows * parts * width * wide,
            bytes_accessed=2 * parts * width * (rows + wide),
            transcendentals=0,
        ),
    )(*texts, gain, *[pltpu.with_memory_space_constraint(x, pltpu.VMEM) for x in weights])


def shards(ffn_hidden, ffn_weight, residual, norm_gain, kv_weight, destination, queries):
    clips, parts, cores = lax.axis_size("clip"), lax.axis_size("seq"), lax.axis_size("tp")
    rows = ffn_hidden.shape[0]
    capacity = rows // min(8, clips)
    share = clips * capacity // cores
    heads_here = kv_weight.shape[1]
    dest = destination.reshape(clips, rows)
    gain = norm_gain.reshape(1, -1)
    weight = kv_weight.reshape(kv_weight.shape[0], heads_here * kv_weight.shape[2])
    weights = [weight] + [swap(weight, "tp", g) for g in range(1, cores)]
    own, send, text = ffn(dest, ffn_hidden, ffn_weight, residual, capacity, cores)
    for g in range(1, cores):
        own = own + swap(send[(g - 1) * share:g * share], "tp", g)
    text = (text.astype(F32) + own).astype(BF16)
    runs, groups = routing(clips, cores, capacity)
    edges = [sum(run[2] for run in runs[0][:n]) for n in range(len(runs[0]) + 1)]
    arrived = [
        route(text[edges[n]:edges[n + 1]], [some[n][0] for some in runs])
        for n in range(len(runs[0]))
    ]
    own = []
    for group in groups:
        mine = jnp.concatenate([arrived[n] for n in group], axis=0)
        texts = [mine] + [swap(mine, "seq", k) for k in range(1, parts)]
        block = keyval(texts, gain, weights)
        own += [block] + [swap(block, "seq", k) for k in range(1, parts)]
    packed = jnp.stack(own)
    others = [swap(packed, "tp", g) for g in range(1, cores)]
    return pl.pallas_call(
        functools.partial(attend_kernel, parts, cores, heads_here, capacity, len(groups)),
        in_specs=[whole()] * (2 + len(own) + len(others)),
        out_specs=whole(),
        out_shape=jax.ShapeDtypeStruct(queries.shape, BF16),
        compiler_params=pltpu.CompilerParams(vmem_limit_bytes=VMEM_LIMIT),
    )(dest, queries, *own, *others)


def solution(mesh):
    return jax.shard_map(
        shards,
        mesh=mesh,
        in_specs=(
            P("clip", "tp"),
            P("tp", "seq"),
            P("clip", "seq"),
            P(),
            P(None, ("seq", "tp"), None),
            P(),
            P(("clip", "seq", "tp"), None),
        ),
        out_specs=P(("clip", "seq", "tp"), None),
        check_vma=False,
    )
```

```python
import functools
import math

import jax
import jax.numpy as jnp
from jax import lax
from jax.experimental import pallas as pl
from jax.experimental.pallas import tpu as pltpu
from jax.sharding import PartitionSpec as P

EPSILON = 1e-06
VMEM_LIMIT = 24 * 1024 * 1024
VMEM_ALL = 60 * 1024 * 1024
F32 = jnp.float32
BF16 = jnp.bfloat16


def whole():
    return pl.BlockSpec(memory_space=pltpu.VMEM)


def swap(value, axis, offset):
    size = lax.axis_size(axis)
    return lax.ppermute(value, axis, [(i, i ^ offset) for i in range(size)])


def routing(clips, cores, capacity):
    if clips == 4 and cores == 2:
        half = capacity // 2
        runs = [
            [(0, 0, half), (3, 0, half), (1, 0, capacity)],
            [(0, half, half), (3, half, half), (2, 0, capacity)],
        ]
        return runs, [[0], [1, 2]]
    each = clips // cores
    runs = [[(t * each + i, 0, capacity) for i in range(each)] for t in range(cores)]
    return runs, [list(range(each))]


def route(value, offsets):
    clips, cores = lax.axis_size("clip"), lax.axis_size("tp")
    if not any(offsets):
        return value
    pairs = [
        (i * cores + t, (i ^ offsets[t]) * cores + t)
        for i in range(clips) for t in range(cores) if offsets[t]
    ]
    moved = lax.ppermute(value, ("clip", "tp"), pairs)
    if all(offsets):
        return moved
    return jnp.where(lax.axis_index("tp") == offsets.index(0), value, moved)


def slot_select(dest_ref, clip, core, capacity, cores):
    clips, rows = dest_ref.shape
    named = dest_ref[pl.ds(clip, 1), :]
    onehot = (lax.broadcasted_iota(jnp.int32, (clips, rows), 0) == named).astype(F32)
    earlier = (
        lax.broadcasted_iota(jnp.int32, (rows, rows), 0)
        < lax.broadcasted_iota(jnp.int32, (rows, rows), 1)
    ).astype(F32)
    before = jnp.dot(onehot, earlier, preferred_element_type=F32)
    rank = jnp.sum(before * onehot, axis=0, keepdims=True).astype(jnp.int32)
    away = named ^ clip
    slot = jnp.zeros_like(away)
    share = clips * capacity // cores
    for t, runs in enumerate(routing(clips, cores, capacity)[0]):
        at = 0
        for offset, first, count in runs:
            inside = (away == offset) & (rank >= first) & (rank < first + count)
            slot = jnp.where(inside, (core ^ t) * share + at - first + rank, slot)
            at += count
    return (lax.broadcasted_iota(jnp.int32, (clips * capacity, rows), 0) == slot).astype(BF16)


def ffn_kernel(capacity, cores, edges, dest_hbm, hidden_hbm, weight_hbm, residual_hbm,
               own_ref, send_ref, text_ref, dest_ref, hidden_ref, weight_ref, residual_ref,
               packed_ref, total_ref, sems):
    clip, core = lax.axis_index("clip"), lax.axis_index("tp")
    share = own_ref.shape[0]
    steps = len(edges) - 1
    parts = [pl.ds(edges[i], edges[i + 1] - edges[i]) for i in range(steps)]
    get_dest = pltpu.make_async_copy(dest_hbm, dest_ref, sems.at[steps])
    get_hidden = pltpu.make_async_copy(hidden_hbm, hidden_ref, sems.at[steps + 1])
    get_residual = pltpu.make_async_copy(residual_hbm, residual_ref, sems.at[steps + 2])
    get_weight = [
        pltpu.make_async_copy(weight_hbm.at[part, :], weight_ref.at[part, :], sems.at[i])
        for i, part in enumerate(parts)
    ]
    for copy in [get_dest, get_hidden] + get_weight[:-1] + [get_residual, get_weight[-1]]:
        copy.start()
    get_dest.wait()
    select = slot_select(dest_ref, clip, core, capacity, cores)
    get_hidden.wait()
    packed_ref[...] = jnp.dot(select, hidden_ref[...], preferred_element_type=F32).astype(BF16)
    for i, part in enumerate(parts):
        if i == steps - 1:
            get_residual.wait()
            text_ref[...] = jnp.dot(
                select[:share], residual_ref[...], preferred_element_type=F32
            ).astype(BF16)
        get_weight[i].wait()
        product = jnp.dot(packed_ref[:, part], weight_ref[part, :], preferred_element_type=F32)
        if i < steps - 1:
            total_ref[...] = product if i == 0 else total_ref[...] + product
        elif i == 0:
            own_ref[...], send_ref[...] = product[:share], product[share:]
        else:
            own_ref[...] = total_ref[:share, :] + product[:share]
            send_ref[...] = total_ref[share:, :] + product[share:]


def ffn(dest, hidden, weight, residual, capacity, cores):
    rows, depth = hidden.shape
    width = weight.shape[1]
    slots = dest.shape[0] * capacity
    share = slots // cores
    unit = depth // 20
    edges = [0, 5 * unit, 10 * unit, 15 * unit, 19 * unit, depth] if unit % 128 == 0 else [0, depth]
    return pl.pallas_call(
        functools.partial(ffn_kernel, capacity, cores, edges),
        in_specs=[pl.BlockSpec(memory_space=pltpu.HBM)] * 4,
        out_specs=[whole()] * 3,
        out_shape=[
            pltpu.VMEM((share, width), F32),
            pltpu.VMEM((slots - share, width), F32),
            pltpu.VMEM((share, width), BF16),
        ],
        scratch_shapes=[
            pltpu.VMEM(dest.shape, jnp.int32),
            pltpu.VMEM(hidden.shape, BF16),
            pltpu.VMEM(weight.shape, BF16),
            pltpu.VMEM(residual.shape, BF16),
            pltpu.VMEM((slots, depth), BF16),
            pltpu.VMEM((slots, width), F32),
            pltpu.SemaphoreType.DMA((len(edges) + 2,)),
        ],
        compiler_params=pltpu.CompilerParams(vmem_limit_bytes=VMEM_LIMIT),
        cost_estimate=pl.CostEstimate(
            flops=2 * slots * depth * (width + rows),
            bytes_accessed=2 * depth * (width + rows),
            transcendentals=0,
        ),
    )(*[pltpu.with_memory_space_constraint(x, pltpu.HBM) for x in (dest, hidden, weight, residual)])


def keyval_kernel(parts, groups, *refs):
    found, (gain_ref, *weights), out_ref = refs[:groups * parts], refs[groups * parts:-1], refs[-1]
    seq = lax.axis_index("seq")
    texts = [
        jnp.concatenate([found[g * parts + k][...] for g in range(groups)], axis=0)
        for k in range(parts)
    ]
    width = texts[0].shape[1]
    squares = 0.0
    for text in texts:
        wide = text.astype(F32)
        squares += jnp.sum(wide * wide, axis=1, keepdims=True)
    scale = lax.rsqrt(squares / (parts * width) + EPSILON)
    totals = [0.0] * len(weights)
    for k, text in enumerate(texts):
        place = pl.ds(pl.multiple_of((seq ^ k) * width, width), width)
        normed = (text.astype(F32) * scale * gain_ref[:, place]).astype(BF16)
        for c, weight in enumerate(weights):
            totals[c] += jnp.dot(normed, weight[place, :], preferred_element_type=F32)
    each = weights[0].shape[1]
    for c in range(len(weights)):
        out_ref[:, c * each:(c + 1) * each] = totals[c].astype(BF16)


def attend_kernel(parts, cores, heads_here, capacity, dest_ref, query_ref, *refs):
    own, others, out_ref = refs[:parts], refs[parts:-1], refs[-1]
    clip, seq, core = lax.axis_index("clip"), lax.axis_index("seq"), lax.axis_index("tp")
    clips = dest_ref.shape[0]
    slots = clips * capacity
    dim = query_ref.shape[1] // (parts * cores * heads_here)
    counts = jnp.sum((dest_ref[...] == clip).astype(jnp.int32), axis=1, keepdims=True)
    share = slots // cores
    lane = lax.broadcasted_iota(jnp.int32, (clips, slots), 1)
    owner, place = (lane // share) ^ core, lane % share
    source, rank = jnp.zeros_like(lane), jnp.zeros_like(lane)
    for t, runs in enumerate(routing(clips, cores, capacity)[0]):
        at = 0
        for offset, first, count in runs:
            inside = (owner == t) & (place >= at) & (place < at + count)
            source = jnp.where(inside, offset ^ clip, source)
            rank = jnp.where(inside, first + place - at, rank)
            at += count
    here = lax.broadcasted_iota(jnp.int32, lane.shape, 0) == source
    valid = jnp.sum(jnp.where(here & (rank < counts), 1, 0), axis=0, keepdims=True) > 0
    heads = [(k, c, i) for k in range(parts) for c in range(cores) for i in range(heads_here)]

    def columns(head):
        k, c, i = head
        at = ((seq ^ k) * cores + (core ^ c)) * heads_here + i
        return pl.ds(pl.multiple_of(at * dim, dim), dim)

    def stored(head, offset):
        k, c, i = head
        found = []
        for g in range(cores):
            at = ((c ^ g) * heads_here + i) * 2 * dim + offset
            if g == 0:
                found.append(own[k][:, at:at + dim])
            else:
                found.append(others[g - 1][k, :, at:at + dim])
        return jnp.concatenate(found, axis=0)

    group = 8
    for first in range(0, len(heads), group):
        some = heads[first:first + group]
        scores = [
            lax.dot_general(
                query_ref[:, columns(head)], stored(head, 0), (((1,), (1,)), ((), ())),
                preferred_element_type=F32,
            )
            for head in some
        ]
        scores = [jnp.where(valid, score * (1.0 / math.sqrt(dim)), -1e30) for score in scores]
        peaks = [jnp.max(score, axis=1, keepdims=True) for score in scores]
        weights = [
            jnp.where(valid, jnp.exp(score - peak), 0.0) for score, peak in zip(scores, peaks)
        ]
        sums = [jnp.sum(weight, axis=1, keepdims=True) for weight in weights]
        probs = [(weight / total).astype(BF16) for weight, total in zip(weights, sums)]
        results = [
            jnp.dot(prob, stored(head, dim), preferred_element_type=F32).astype(BF16)
            for prob, head in zip(probs, some)
        ]
        for head, result in zip(some, results):
            out_ref[:, columns(head)] = result


def keyval(texts, gain, weights):
    groups, parts = len(texts), len(texts[0])
    rows, width = sum(some[0].shape[0] for some in texts), texts[0][0].shape[1]
    wide = sum(weight.shape[1] for weight in weights)
    return pl.pallas_call(
        functools.partial(keyval_kernel, parts, groups),
        in_specs=[whole()] * (groups * parts + 1 + len(weights)),
        out_specs=whole(),
        out_shape=pltpu.VMEM((rows, wide), BF16),
        compiler_params=pltpu.CompilerParams(vmem_limit_bytes=VMEM_LIMIT),
        cost_estimate=pl.CostEstimate(
            flops=2 * rows * parts * width * wide,
            bytes_accessed=2 * parts * width * (rows + wide),
            transcendentals=0,
        ),
    )(
        *[text for some in texts for text in some],
        gain,
        *[pltpu.with_memory_space_constraint(x, pltpu.VMEM) for x in weights],
    )


def shards(ffn_hidden, ffn_weight, residual, norm_gain, kv_weight, destination, queries):
    clips, parts, cores = lax.axis_size("clip"), lax.axis_size("seq"), lax.axis_size("tp")
    rows = ffn_hidden.shape[0]
    capacity = rows // min(8, clips)
    share = clips * capacity // cores
    heads_here = kv_weight.shape[1]
    dest = destination.reshape(clips, rows)
    gain = norm_gain.reshape(1, -1)
    weight = kv_weight.reshape(kv_weight.shape[0], heads_here * kv_weight.shape[2])
    weights = [swap(weight, "tp", g) for g in range(1, cores)]
    own, send, text = ffn(dest, ffn_hidden, ffn_weight, residual, capacity, cores)
    weights, own = lax.optimization_barrier(([weight] + weights, own))
    for g in range(1, cores):
        own = own + swap(send[(g - 1) * share:g * share], "tp", g)
    text = (text.astype(F32) + own).astype(BF16)
    runs, groups = routing(clips, cores, capacity)
    edges = [sum(run[2] for run in runs[0][:n]) for n in range(len(runs[0]) + 1)]
    arrived = [
        route(text[edges[n]:edges[n + 1]], [some[n][0] for some in runs])
        for n in range(len(runs[0]))
    ]
    texts = []
    for group in groups:
        mine = jnp.concatenate([arrived[n] for n in group], axis=0)
        mine, texts = lax.optimization_barrier((mine, texts))
        texts.append([mine] + [swap(mine, "seq", k) for k in range(1, parts)])
    block = keyval(texts, gain, weights)
    own = [block] + [swap(block, "seq", k) for k in range(1, parts)]
    packed = jnp.stack(own)
    others = [swap(packed, "tp", g) for g in range(1, cores)]
    return pl.pallas_call(
        functools.partial(attend_kernel, parts, cores, heads_here, capacity),
        in_specs=[whole()] * (2 + len(own) + len(others)),
        out_specs=whole(),
        out_shape=jax.ShapeDtypeStruct(queries.shape, BF16),
        compiler_params=pltpu.CompilerParams(vmem_limit_bytes=VMEM_LIMIT),
    )(dest, queries, *own, *others)


def solution(mesh):
    return jax.shard_map(
        shards,
        mesh=mesh,
        in_specs=(
            P("clip", "tp"),
            P("tp", "seq"),
            P("clip", "seq"),
            P(),
            P(None, ("seq", "tp"), None),
            P(),
            P(("clip", "seq", "tp"), None),
        ),
        out_specs=P(("clip", "seq", "tp"), None),
        check_vma=False,
    )
```

```python
import functools
import math

import jax
import jax.numpy as jnp
from jax import lax
from jax.experimental import pallas as pl
from jax.experimental.pallas import tpu as pltpu
from jax.sharding import PartitionSpec as P

EPSILON = 1e-06
VMEM_LIMIT = 24 * 1024 * 1024
VMEM_ALL = 60 * 1024 * 1024
F32 = jnp.float32
BF16 = jnp.bfloat16


def whole():
    return pl.BlockSpec(memory_space=pltpu.VMEM)


def swap(value, axis, offset):
    size = lax.axis_size(axis)
    return lax.ppermute(value, axis, [(i, i ^ offset) for i in range(size)])


def seq_steps(parts):
    return [0] + list(range(parts - 1, 0, -1))


def spread(value):
    return [swap(value, "seq", k) if k else value for k in seq_steps(lax.axis_size("seq"))]


def routing(clips, cores, capacity):
    if clips == 4 and cores == 2:
        half = capacity // 2
        runs = [
            [(0, 0, half), (3, 0, half), (1, 0, capacity)],
            [(0, half, half), (3, half, half), (2, 0, capacity)],
        ]
        return runs, [[0, 1], [2]]
    each = clips // cores
    runs = [[(t * each + i, 0, capacity) for i in range(each)] for t in range(cores)]
    return runs, [list(range(each))]


def route(value, offsets):
    clips, cores = lax.axis_size("clip"), lax.axis_size("tp")
    if not any(offsets):
        return value
    pairs = [
        (i * cores + t, (i ^ offsets[t]) * cores + t)
        for i in range(clips) for t in range(cores) if offsets[t]
    ]
    moved = lax.ppermute(value, ("clip", "tp"), pairs)
    if all(offsets):
        return moved
    return jnp.where(lax.axis_index("tp") == offsets.index(0), value, moved)


def slot_select(dest_ref, clip, core, capacity, cores):
    clips, rows = dest_ref.shape
    named = dest_ref[pl.ds(clip, 1), :]
    onehot = (lax.broadcasted_iota(jnp.int32, (clips, rows), 0) == named).astype(F32)
    earlier = (
        lax.broadcasted_iota(jnp.int32, (rows, rows), 0)
        < lax.broadcasted_iota(jnp.int32, (rows, rows), 1)
    ).astype(F32)
    before = jnp.dot(onehot, earlier, preferred_element_type=F32)
    rank = jnp.sum(before * onehot, axis=0, keepdims=True).astype(jnp.int32)
    away = named ^ clip
    slot = jnp.zeros_like(away)
    share = clips * capacity // cores
    for t, runs in enumerate(routing(clips, cores, capacity)[0]):
        at = 0
        for offset, first, count in runs:
            inside = (away == offset) & (rank >= first) & (rank < first + count)
            slot = jnp.where(inside, (core ^ t) * share + at - first + rank, slot)
            at += count
    return (lax.broadcasted_iota(jnp.int32, (clips * capacity, rows), 0) == slot).astype(BF16)


def ffn_kernel(capacity, cores, steps, dest_hbm, hidden_hbm, weight_hbm, residual_hbm,
               own_ref, send_ref, text_ref, dest_ref, hidden_ref, weight_ref, residual_ref,
               packed_ref, sems):
    clip, core = lax.axis_index("clip"), lax.axis_index("tp")
    share, width = own_ref.shape
    block = width // steps
    parts = [pl.ds(i * block, block) for i in range(steps)]
    get_dest = pltpu.make_async_copy(dest_hbm, dest_ref, sems.at[steps])
    get_hidden = pltpu.make_async_copy(hidden_hbm, hidden_ref, sems.at[steps + 1])
    get_residual = pltpu.make_async_copy(residual_hbm, residual_ref, sems.at[steps + 2])
    get_weight = [
        pltpu.make_async_copy(weight_hbm.at[:, part], weight_ref.at[:, part], sems.at[i])
        for i, part in enumerate(parts)
    ]
    for copy in [get_dest, get_hidden] + get_weight[:-1] + [get_residual, get_weight[-1]]:
        copy.start()
    get_dest.wait()
    select = slot_select(dest_ref, clip, core, capacity, cores)
    get_hidden.wait()
    packed_ref[...] = jnp.dot(select, hidden_ref[...], preferred_element_type=F32).astype(BF16)
    for i, part in enumerate(parts):
        if i == steps - 1:
            get_residual.wait()
            text_ref[...] = jnp.dot(
                select[:share], residual_ref[...], preferred_element_type=F32
            ).astype(BF16)
        get_weight[i].wait()
        product = jnp.dot(packed_ref[...], weight_ref[:, part], preferred_element_type=F32)
        own_ref[:, part] = product[:share]
        send_ref[:, part] = product[share:]


def ffn(dest, hidden, weight, residual, capacity, cores):
    rows, depth = hidden.shape
    width = weight.shape[1]
    slots = dest.shape[0] * capacity
    share = slots // cores
    steps = max(1, width // 256)
    return pl.pallas_call(
        functools.partial(ffn_kernel, capacity, cores, steps),
        in_specs=[pl.BlockSpec(memory_space=pltpu.HBM)] * 4,
        out_specs=[whole()] * 3,
        out_shape=[
            pltpu.VMEM((share, width), F32),
            pltpu.VMEM((slots - share, width), F32),
            pltpu.VMEM((share, width), BF16),
        ],
        scratch_shapes=[
            pltpu.VMEM(dest.shape, jnp.int32),
            pltpu.VMEM(hidden.shape, BF16),
            pltpu.VMEM(weight.shape, BF16),
            pltpu.VMEM(residual.shape, BF16),
            pltpu.VMEM((slots, depth), BF16),
            pltpu.SemaphoreType.DMA((steps + 3,)),
        ],
        compiler_params=pltpu.CompilerParams(vmem_limit_bytes=VMEM_LIMIT),
        cost_estimate=pl.CostEstimate(
            flops=2 * slots * depth * (width + rows),
            bytes_accessed=2 * depth * (width + rows),
            transcendentals=0,
        ),
    )(*[pltpu.with_memory_space_constraint(x, pltpu.HBM) for x in (dest, hidden, weight, residual)])


def keyval_kernel(parts, cores, *refs):
    texts, (gain_ref, *weights), out_ref = refs[:parts], refs[parts:-1], refs[-1]
    seq = lax.axis_index("seq")
    width = texts[0].shape[1]
    squares = 0.0
    for text in texts:
        wide = text[...].astype(F32)
        squares += jnp.sum(wide * wide, axis=1, keepdims=True)
    scale = lax.rsqrt(squares / (parts * width) + EPSILON)
    totals = [0.0] * cores
    for k, text in enumerate(texts):
        place = pl.ds(pl.multiple_of((seq ^ seq_steps(parts)[k]) * width, width), width)
        normed = (text[...].astype(F32) * scale * gain_ref[:, place]).astype(BF16)
        for c, weight in enumerate(weights):
            totals[c] += jnp.dot(normed, weight[place, :], preferred_element_type=F32)
    each = weights[0].shape[1]
    for c in range(cores):
        out_ref[:, c * each:(c + 1) * each] = totals[c].astype(BF16)


def attend_kernel(parts, cores, heads_here, capacity, groups, dest_ref, query_ref, *refs):
    own, others, out_ref = refs[:parts * groups], refs[parts * groups:-1], refs[-1]
    clip, seq, core = lax.axis_index("clip"), lax.axis_index("seq"), lax.axis_index("tp")
    clips = dest_ref.shape[0]
    slots = clips * capacity
    dim = query_ref.shape[1] // (parts * cores * heads_here)
    counts = jnp.sum((dest_ref[...] == clip).astype(jnp.int32), axis=1, keepdims=True)
    share = slots // cores
    lane = lax.broadcasted_iota(jnp.int32, (clips, slots), 1)
    owner, place = (lane // share) ^ core, lane % share
    source, rank = jnp.zeros_like(lane), jnp.zeros_like(lane)
    for t, runs in enumerate(routing(clips, cores, capacity)[0]):
        at = 0
        for offset, first, count in runs:
            inside = (owner == t) & (place >= at) & (place < at + count)
            source = jnp.where(inside, offset ^ clip, source)
            rank = jnp.where(inside, first + place - at, rank)
            at += count
    here = lax.broadcasted_iota(jnp.int32, lane.shape, 0) == source
    valid = jnp.sum(jnp.where(here & (rank < counts), 1, 0), axis=0, keepdims=True) > 0
    heads = [(k, c, i) for k in range(parts) for c in range(cores) for i in range(heads_here)]

    def columns(head):
        k, c, i = head
        at = ((seq ^ seq_steps(parts)[k]) * cores + (core ^ c)) * heads_here + i
        return pl.ds(pl.multiple_of(at * dim, dim), dim)

    def stored(head, offset):
        k, c, i = head
        found = []
        for g in range(cores):
            at = ((c ^ g) * heads_here + i) * 2 * dim + offset
            if g == 0:
                found += [own[n * parts + k][:, at:at + dim] for n in range(groups)]
            else:
                found += [
                    others[n * (cores - 1) + g - 1][k, :, at:at + dim] for n in range(groups)
                ]
        return jnp.concatenate(found, axis=0)

    group = 8
    for first in range(0, len(heads), group):
        some = heads[first:first + group]
        scores = [
            lax.dot_general(
                query_ref[:, columns(head)], stored(head, 0), (((1,), (1,)), ((), ())),
                preferred_element_type=F32,
            )
            for head in some
        ]
        scores = [jnp.where(valid, score * (1.0 / math.sqrt(dim)), -1e30) for score in scores]
        peaks = [jnp.max(score, axis=1, keepdims=True) for score in scores]
        weights = [
            jnp.where(valid, jnp.exp(score - peak), 0.0) for score, peak in zip(scores, peaks)
        ]
        sums = [jnp.sum(weight, axis=1, keepdims=True) for weight in weights]
        probs = [(weight / total).astype(BF16) for weight, total in zip(weights, sums)]
        results = [
            jnp.dot(prob, stored(head, dim), preferred_element_type=F32).astype(BF16)
            for prob, head in zip(probs, some)
        ]
        for head, result in zip(some, results):
            out_ref[:, columns(head)] = result


def keyval(texts, gain, weights):
    parts, (rows, width) = len(texts), texts[0].shape
    wide = sum(weight.shape[1] for weight in weights)
    return pl.pallas_call(
        functools.partial(keyval_kernel, parts, len(weights)),
        in_specs=[whole()] * (parts + 1 + len(weights)),
        out_specs=whole(),
        out_shape=pltpu.VMEM((rows, wide), BF16),
        compiler_params=pltpu.CompilerParams(vmem_limit_bytes=VMEM_LIMIT),
        cost_estimate=pl.CostEstimate(
            flops=2 * rows * parts * width * wide,
            bytes_accessed=2 * parts * width * (rows + wide),
            transcendentals=0,
        ),
    )(*texts, gain, *[pltpu.with_memory_space_constraint(x, pltpu.VMEM) for x in weights])


def shards(ffn_hidden, ffn_weight, residual, norm_gain, kv_weight, destination, queries):
    clips, parts, cores = lax.axis_size("clip"), lax.axis_size("seq"), lax.axis_size("tp")
    rows = ffn_hidden.shape[0]
    capacity = rows // min(8, clips)
    share = clips * capacity // cores
    heads_here = kv_weight.shape[1]
    dest = destination.reshape(clips, rows)
    gain = norm_gain.reshape(1, -1)
    weight = kv_weight.reshape(kv_weight.shape[0], heads_here * kv_weight.shape[2])
    weights = [weight] + [swap(weight, "tp", g) for g in range(1, cores)]
    own, send, text = ffn(dest, ffn_hidden, ffn_weight, residual, capacity, cores)
    for g in range(1, cores):
        own = own + swap(send[(g - 1) * share:g * share], "tp", g)
    text = (text.astype(F32) + own).astype(BF16)
    runs, groups = routing(clips, cores, capacity)
    edges = [sum(run[2] for run in runs[0][:n]) for n in range(len(runs[0]) + 1)]
    arrived = [
        route(text[edges[n]:edges[n + 1]], [some[n][0] for some in runs])
        for n in range(len(runs[0]))
    ]
    own, others = [], []
    for group in groups:
        mine = jnp.concatenate([arrived[n] for n in group], axis=0)
        block = spread(keyval(spread(mine), gain, weights))
        own += block
        others += [swap(jnp.stack(block), "tp", g) for g in range(1, cores)]
    return pl.pallas_call(
        functools.partial(attend_kernel, parts, cores, heads_here, capacity, len(groups)),
        in_specs=[whole()] * (2 + len(own) + len(others)),
        out_specs=whole(),
        out_shape=jax.ShapeDtypeStruct(queries.shape, BF16),
        compiler_params=pltpu.CompilerParams(vmem_limit_bytes=VMEM_LIMIT),
    )(dest, queries, *own, *others)


def solution(mesh):
    return jax.shard_map(
        shards,
        mesh=mesh,
        in_specs=(
            P("clip", "tp"),
            P("tp", "seq"),
            P("clip", "seq"),
            P(),
            P(None, ("seq", "tp"), None),
            P(),
            P(("clip", "seq", "tp"), None),
        ),
        out_specs=P(("clip", "seq", "tp"), None),
        check_vma=False,
    )
```

```python
import functools
import math

import jax
import jax.numpy as jnp
from jax import lax
from jax.experimental import pallas as pl
from jax.experimental.pallas import tpu as pltpu
from jax.sharding import PartitionSpec as P

EPSILON = 1e-06
VMEM_LIMIT = 24 * 1024 * 1024
VMEM_ALL = 60 * 1024 * 1024
F32 = jnp.float32
BF16 = jnp.bfloat16


def whole():
    return pl.BlockSpec(memory_space=pltpu.VMEM)


def swap(value, axis, offset):
    size = lax.axis_size(axis)
    return lax.ppermute(value, axis, [(i, i ^ offset) for i in range(size)])


def seq_steps(parts):
    return [0] + list(range(parts - 1, 0, -1))


def spread(value):
    return [swap(value, "seq", k) if k else value for k in seq_steps(lax.axis_size("seq"))]


def route_offsets(clips, cores):
    if clips == 4 and cores == 2:
        return [3, 0, 2, 1]
    return list(range(clips))


def route(value, place):
    clips, cores = lax.axis_size("clip"), lax.axis_size("tp")
    offsets = route_offsets(clips, cores)
    pairs = [
        (i * cores + t, (i ^ offsets[t * (clips // cores) + place]) * cores + t)
        for i in range(clips) for t in range(cores)
    ]
    return lax.ppermute(value, ("clip", "tp"), pairs)


def slot_select(dest_ref, clip, core, capacity, cores):
    clips, rows = dest_ref.shape
    named = dest_ref[pl.ds(clip, 1), :]
    onehot = (lax.broadcasted_iota(jnp.int32, (clips, rows), 0) == named).astype(F32)
    earlier = (
        lax.broadcasted_iota(jnp.int32, (rows, rows), 0)
        < lax.broadcasted_iota(jnp.int32, (rows, rows), 1)
    ).astype(F32)
    before = jnp.dot(onehot, earlier, preferred_element_type=F32)
    rank = jnp.sum(before * onehot, axis=0, keepdims=True).astype(jnp.int32)
    away = named ^ clip
    block = jnp.zeros_like(away)
    for place, offset in enumerate(route_offsets(clips, cores)):
        block = jnp.where(away == offset, place, block)
    slot = (block ^ (core * (clips // cores))) * capacity + rank
    return (lax.broadcasted_iota(jnp.int32, (clips * capacity, rows), 0) == slot).astype(BF16)


def ffn_kernel(capacity, cores, steps, dest_hbm, hidden_hbm, weight_hbm, residual_hbm,
               own_ref, send_ref, text_ref, dest_ref, hidden_ref, weight_ref, residual_ref,
               packed_ref, total_ref, sems):
    clip, core = lax.axis_index("clip"), lax.axis_index("tp")
    share = own_ref.shape[0]
    block = hidden_hbm.shape[1] // steps
    get_dest = pltpu.make_async_copy(dest_hbm, dest_ref, sems.at[steps])
    get_hidden = pltpu.make_async_copy(hidden_hbm, hidden_ref, sems.at[steps + 1])
    get_residual = pltpu.make_async_copy(residual_hbm, residual_ref, sems.at[steps + 2])
    get_weight = [
        pltpu.make_async_copy(
            weight_hbm.at[pl.ds(i * block, block), :],
            weight_ref.at[pl.ds(i * block, block), :],
            sems.at[i],
        )
        for i in range(steps)
    ]
    for copy in [get_dest, get_hidden] + get_weight + [get_residual]:
        copy.start()
    get_dest.wait()
    select = slot_select(dest_ref, clip, core, capacity, cores)
    get_hidden.wait()
    packed_ref[...] = jnp.dot(select, hidden_ref[...], preferred_element_type=F32).astype(BF16)
    for i in range(steps):
        part = pl.ds(i * block, block)
        get_weight[i].wait()
        product = jnp.dot(packed_ref[:, part], weight_ref[part, :], preferred_element_type=F32)
        if i == 0:
            total_ref[...] = product
        elif i < steps - 1:
            total_ref[...] += product
        else:
            own_ref[...] = total_ref[:share, :] + product[:share]
            send_ref[...] = total_ref[share:, :] + product[share:]
    get_residual.wait()
    text_ref[...] = jnp.dot(
        select[:share], residual_ref[...], preferred_element_type=F32
    ).astype(BF16)


def ffn(dest, hidden, weight, residual, capacity, cores):
    rows, depth = hidden.shape
    width = weight.shape[1]
    slots = dest.shape[0] * capacity
    share = slots // cores
    steps = math.gcd(5, depth // 128)
    return pl.pallas_call(
        functools.partial(ffn_kernel, capacity, cores, steps),
        in_specs=[pl.BlockSpec(memory_space=pltpu.HBM)] * 4,
        out_specs=[whole()] * 3,
        out_shape=[
            pltpu.VMEM((share, width), F32),
            pltpu.VMEM((slots - share, width), F32),
            pltpu.VMEM((share, width), BF16),
        ],
        scratch_shapes=[
            pltpu.VMEM(dest.shape, jnp.int32),
            pltpu.VMEM(hidden.shape, BF16),
            pltpu.VMEM(weight.shape, BF16),
            pltpu.VMEM(residual.shape, BF16),
            pltpu.VMEM((slots, depth), BF16),
            pltpu.VMEM((slots, width), F32),
            pltpu.SemaphoreType.DMA((steps + 3,)),
        ],
        compiler_params=pltpu.CompilerParams(vmem_limit_bytes=VMEM_LIMIT),
        cost_estimate=pl.CostEstimate(
            flops=2 * slots * depth * (width + rows),
            bytes_accessed=2 * depth * (width + rows),
            transcendentals=0,
        ),
    )(*[pltpu.with_memory_space_constraint(x, pltpu.HBM) for x in (dest, hidden, weight, residual)])


def keyval_kernel(parts, cores, *refs):
    texts, (gain_ref, *weights), out_ref = refs[:parts], refs[parts:-1], refs[-1]
    seq = lax.axis_index("seq")
    width = texts[0].shape[1]
    squares = 0.0
    for text in texts:
        wide = text[...].astype(F32)
        squares += jnp.sum(wide * wide, axis=1, keepdims=True)
    scale = lax.rsqrt(squares / (parts * width) + EPSILON)
    totals = [0.0] * cores
    for k, text in enumerate(texts):
        place = pl.ds(pl.multiple_of((seq ^ seq_steps(parts)[k]) * width, width), width)
        normed = (text[...].astype(F32) * scale * gain_ref[:, place]).astype(BF16)
        for c, weight in enumerate(weights):
            totals[c] += jnp.dot(normed, weight[place, :], preferred_element_type=F32)
    each = weights[0].shape[1]
    for c in range(cores):
        out_ref[:, c * each:(c + 1) * each] = totals[c].astype(BF16)


def attend_kernel(parts, cores, heads_here, capacity, steps, counts_of, dest_ref, query_ref, *refs):
    groups, stacks = sum(counts_of) // len(steps), len(counts_of)
    own, refs = refs[:groups * len(steps)], refs[groups * len(steps):]
    found_of = [
        [stack.at[n] for count, stack in zip(counts_of, refs[g * stacks:(g + 1) * stacks]) for n in range(count)]
        for g in range(cores - 1)
    ]
    done, out_ref = refs[(cores - 1) * stacks:-1], refs[-1]
    clip, seq, core = lax.axis_index("clip"), lax.axis_index("seq"), lax.axis_index("tp")
    clips = dest_ref.shape[0]
    slots = clips * capacity
    dim = query_ref.shape[1] // (parts * cores * heads_here)
    counts = jnp.sum((dest_ref[...] == clip).astype(jnp.int32), axis=1, keepdims=True)
    lane = lax.broadcasted_iota(jnp.int32, (clips, slots), 1)
    block = (lane // capacity) ^ (core * (clips // cores))
    source = jnp.zeros_like(lane)
    for place, offset in enumerate(route_offsets(clips, cores)):
        source = jnp.where(block == place, offset ^ clip, source)
    limit = jnp.sum(
        jnp.where(lax.broadcasted_iota(jnp.int32, lane.shape, 0) == source, counts, 0),
        axis=0, keepdims=True,
    )
    valid = lax.broadcasted_iota(jnp.int32, (1, slots), 1) % capacity < limit
    heads = [
        (k, c, i) for k in range(len(steps)) for c in range(cores) for i in range(heads_here)
    ]

    def columns(head):
        k, c, i = head
        at = ((seq ^ steps[k]) * cores + (core ^ c)) * heads_here + i
        return pl.ds(pl.multiple_of(at * dim, dim), dim)

    def stored(head, offset):
        k, c, i = head
        found = []
        for g in range(cores):
            at = ((c ^ g) * heads_here + i) * 2 * dim + offset
            for n in range(groups):
                block = own[n * len(steps) + k] if g == 0 else found_of[g - 1][n * len(steps) + k]
                found.append(block[:, at:at + dim])
        return jnp.concatenate(found, axis=0)

    if done:
        out_ref[...] = done[0][...]
    group = 8
    for first in range(0, len(heads), group):
        some = heads[first:first + group]
        scores = [
            lax.dot_general(
                query_ref[:, columns(head)], stored(head, 0), (((1,), (1,)), ((), ())),
                preferred_element_type=F32,
            )
            for head in some
        ]
        scores = [jnp.where(valid, score * (1.0 / math.sqrt(dim)), -1e30) for score in scores]
        peaks = [jnp.max(score, axis=1, keepdims=True) for score in scores]
        weights = [
            jnp.where(valid, jnp.exp(score - peak), 0.0) for score, peak in zip(scores, peaks)
        ]
        sums = [jnp.sum(weight, axis=1, keepdims=True) for weight in weights]
        probs = [(weight / total).astype(BF16) for weight, total in zip(weights, sums)]
        results = [
            jnp.dot(prob, stored(head, dim), preferred_element_type=F32).astype(BF16)
            for prob, head in zip(probs, some)
        ]
        for head, result in zip(some, results):
            out_ref[:, columns(head)] = result


def keyval(texts, gain, weights):
    parts, (rows, width) = len(texts), texts[0].shape
    wide = sum(weight.shape[1] for weight in weights)
    return pl.pallas_call(
        functools.partial(keyval_kernel, parts, len(weights)),
        in_specs=[whole()] * (parts + 1 + len(weights)),
        out_specs=whole(),
        out_shape=pltpu.VMEM((rows, wide), BF16),
        compiler_params=pltpu.CompilerParams(vmem_limit_bytes=VMEM_LIMIT),
        cost_estimate=pl.CostEstimate(
            flops=2 * rows * parts * width * wide,
            bytes_accessed=2 * parts * width * (rows + wide),
            transcendentals=0,
        ),
    )(*texts, gain, *[pltpu.with_memory_space_constraint(x, pltpu.VMEM) for x in weights])


def shards(ffn_hidden, ffn_weight, residual, norm_gain, kv_weight, destination, queries):
    clips, parts, cores = lax.axis_size("clip"), lax.axis_size("seq"), lax.axis_size("tp")
    rows = ffn_hidden.shape[0]
    capacity = rows // min(8, clips)
    share = clips * capacity // cores
    heads_here = kv_weight.shape[1]
    dest = destination.reshape(clips, rows)
    gain = norm_gain.reshape(1, -1)
    weight = kv_weight.reshape(kv_weight.shape[0], heads_here * kv_weight.shape[2])
    weights = [weight] + [swap(weight, "tp", g) for g in range(1, cores)]
    own, send, text = ffn(dest, ffn_hidden, ffn_weight, residual, capacity, cores)
    for g in range(1, cores):
        own = own + swap(send[(g - 1) * share:g * share], "tp", g)
    text = (text.astype(F32) + own).astype(BF16)
    places = clips // cores
    groups = math.gcd(2, places)
    own = []
    for first in range(0, places, places // groups):
        arrived = [
            route(text[i * capacity:(i + 1) * capacity], i)
            for i in range(first, first + places // groups)
        ]
        arrived = jnp.concatenate(arrived, axis=0)
        own.append(spread(keyval(spread(arrived), gain, weights)))

    def crossed(blocks):
        return [swap(jnp.stack(blocks), "tp", g) for g in range(1, cores)]

    def attend(steps, blocks, stacks, counts_of, done):
        return pl.pallas_call(
            functools.partial(
                attend_kernel, parts, cores, heads_here, capacity, steps, counts_of
            ),
            in_specs=[whole()] * (2 + len(blocks) + len(stacks) + len(done)),
            out_specs=whole(),
            out_shape=jax.ShapeDtypeStruct(queries.shape, BF16),
            compiler_params=pltpu.CompilerParams(vmem_limit_bytes=VMEM_LIMIT),
        )(dest, queries, *blocks, *stacks, *done)

    cut = max(1, parts // 2)
    steps = seq_steps(parts)
    soon = [block for some in own for block in some[:cut]]
    late = [block for some in own for block in some[cut:]]
    soon_crossed, late_crossed = crossed(soon), crossed(late)
    done = [attend(steps[:cut], soon, soon_crossed, [len(soon)], [])]
    return attend(steps[cut:], late, late_crossed, [len(late)], done)


def solution(mesh):
    return jax.shard_map(
        shards,
        mesh=mesh,
        in_specs=(
            P("clip", "tp"),
            P("tp", "seq"),
            P("clip", "seq"),
            P(),
            P(None, ("seq", "tp"), None),
            P(),
            P(("clip", "seq", "tp"), None),
        ),
        out_specs=P(("clip", "seq", "tp"), None),
        check_vma=False,
    )
```

```python
import functools
import math

import jax
import jax.numpy as jnp
from jax import lax
from jax.experimental import pallas as pl
from jax.experimental.pallas import tpu as pltpu
from jax.sharding import PartitionSpec as P

EPSILON = 1e-06
VMEM_LIMIT = 24 * 1024 * 1024
VMEM_ALL = 60 * 1024 * 1024
F32 = jnp.float32
BF16 = jnp.bfloat16


def whole():
    return pl.BlockSpec(memory_space=pltpu.VMEM)


def swap(value, axis, offset):
    size = lax.axis_size(axis)
    return lax.ppermute(value, axis, [(i, i ^ offset) for i in range(size)])


def relayed(value):
    found = {0: value}
    for k in sorted(range(1, lax.axis_size("seq")), key=lambda k: (bin(k).count("1"), -k)):
        low = k & -k
        found[k] = swap(found[k ^ low], "seq", low)
    return [found[k] for k in range(len(found))]


def route_offsets(clips, cores):
    if clips == 4 and cores == 2:
        return [0, 3, 1, 2]
    return list(range(clips))


def route(value, place):
    clips, cores = lax.axis_size("clip"), lax.axis_size("tp")
    offsets = route_offsets(clips, cores)
    pairs = [
        (i * cores + t, (i ^ offsets[t * (clips // cores) + place]) * cores + t)
        for i in range(clips) for t in range(cores)
    ]
    return lax.ppermute(value, ("clip", "tp"), pairs)


def slot_select(dest_ref, clip, core, capacity, cores):
    clips, rows = dest_ref.shape
    named = dest_ref[pl.ds(clip, 1), :]
    onehot = (lax.broadcasted_iota(jnp.int32, (clips, rows), 0) == named).astype(F32)
    earlier = (
        lax.broadcasted_iota(jnp.int32, (rows, rows), 0)
        < lax.broadcasted_iota(jnp.int32, (rows, rows), 1)
    ).astype(F32)
    before = jnp.dot(onehot, earlier, preferred_element_type=F32)
    rank = jnp.sum(before * onehot, axis=0, keepdims=True).astype(jnp.int32)
    away = named ^ clip
    block = jnp.zeros_like(away)
    for place, offset in enumerate(route_offsets(clips, cores)):
        block = jnp.where(away == offset, place, block)
    slot = (block ^ (core * (clips // cores))) * capacity + rank
    return (lax.broadcasted_iota(jnp.int32, (clips * capacity, rows), 0) == slot).astype(BF16)


def ffn_kernel(capacity, cores, steps, dest_hbm, hidden_hbm, weight_hbm, residual_hbm,
               own_ref, send_ref, text_ref, dest_ref, hidden_ref, weight_ref, residual_ref,
               packed_ref, total_ref, sems):
    clip, core = lax.axis_index("clip"), lax.axis_index("tp")
    share = own_ref.shape[0]
    block = hidden_hbm.shape[1] // steps
    get_dest = pltpu.make_async_copy(dest_hbm, dest_ref, sems.at[steps])
    get_hidden = pltpu.make_async_copy(hidden_hbm, hidden_ref, sems.at[steps + 1])
    get_residual = pltpu.make_async_copy(residual_hbm, residual_ref, sems.at[steps + 2])
    get_weight = [
        pltpu.make_async_copy(
            weight_hbm.at[pl.ds(i * block, block), :],
            weight_ref.at[pl.ds(i * block, block), :],
            sems.at[i],
        )
        for i in range(steps)
    ]
    for copy in [get_dest, get_hidden] + get_weight + [get_residual]:
        copy.start()
    get_dest.wait()
    select = slot_select(dest_ref, clip, core, capacity, cores)
    get_hidden.wait()
    packed_ref[...] = jnp.dot(select, hidden_ref[...], preferred_element_type=F32).astype(BF16)
    for i in range(steps):
        part = pl.ds(i * block, block)
        get_weight[i].wait()
        product = jnp.dot(packed_ref[:, part], weight_ref[part, :], preferred_element_type=F32)
        if i == 0:
            total_ref[...] = product
        elif i < steps - 1:
            total_ref[...] += product
        else:
            own_ref[...] = total_ref[:share, :] + product[:share]
            send_ref[...] = total_ref[share:, :] + product[share:]
    get_residual.wait()
    text_ref[...] = jnp.dot(
        select[:share], residual_ref[...], preferred_element_type=F32
    ).astype(BF16)


def ffn(dest, hidden, weight, residual, capacity, cores):
    rows, depth = hidden.shape
    width = weight.shape[1]
    slots = dest.shape[0] * capacity
    share = slots // cores
    steps = math.gcd(5, depth // 128)
    return pl.pallas_call(
        functools.partial(ffn_kernel, capacity, cores, steps),
        in_specs=[pl.BlockSpec(memory_space=pltpu.HBM)] * 4,
        out_specs=[whole()] * 3,
        out_shape=[
            pltpu.VMEM((share, width), F32),
            pltpu.VMEM((slots - share, width), F32),
            pltpu.VMEM((share, width), BF16),
        ],
        scratch_shapes=[
            pltpu.VMEM(dest.shape, jnp.int32),
            pltpu.VMEM(hidden.shape, BF16),
            pltpu.VMEM(weight.shape, BF16),
            pltpu.VMEM(residual.shape, BF16),
            pltpu.VMEM((slots, depth), BF16),
            pltpu.VMEM((slots, width), F32),
            pltpu.SemaphoreType.DMA((steps + 3,)),
        ],
        compiler_params=pltpu.CompilerParams(vmem_limit_bytes=VMEM_LIMIT),
        cost_estimate=pl.CostEstimate(
            flops=2 * slots * depth * (width + rows),
            bytes_accessed=2 * depth * (width + rows),
            transcendentals=0,
        ),
    )(*[pltpu.with_memory_space_constraint(x, pltpu.HBM) for x in (dest, hidden, weight, residual)])


def keyval_kernel(parts, cores, *refs):
    texts, (gain_ref, *weights), out_ref = refs[:parts], refs[parts:-1], refs[-1]
    seq = lax.axis_index("seq")
    width = texts[0].shape[1]
    squares = 0.0
    for text in texts:
        wide = text[...].astype(F32)
        squares += jnp.sum(wide * wide, axis=1, keepdims=True)
    scale = lax.rsqrt(squares / (parts * width) + EPSILON)
    totals = [0.0] * cores
    for k, text in enumerate(texts):
        place = pl.ds(pl.multiple_of((seq ^ k) * width, width), width)
        normed = (text[...].astype(F32) * scale * gain_ref[:, place]).astype(BF16)
        for c, weight in enumerate(weights):
            totals[c] += jnp.dot(normed, weight[place, :], preferred_element_type=F32)
    each = weights[0].shape[1]
    for c in range(cores):
        out_ref[:, c * each:(c + 1) * each] = totals[c].astype(BF16)


def attend_kernel(parts, cores, heads_here, capacity, groups, dest_ref, query_ref, *refs):
    blocks, out_ref = refs[:-1], refs[-1]
    each = parts + cores - 1
    clip, seq, core = lax.axis_index("clip"), lax.axis_index("seq"), lax.axis_index("tp")
    clips = dest_ref.shape[0]
    slots = clips * capacity
    dim = query_ref.shape[1] // (parts * cores * heads_here)
    counts = jnp.sum((dest_ref[...] == clip).astype(jnp.int32), axis=1, keepdims=True)
    lane = lax.broadcasted_iota(jnp.int32, (clips, slots), 1)
    block = (lane // capacity) ^ (core * (clips // cores))
    source = jnp.zeros_like(lane)
    for place, offset in enumerate(route_offsets(clips, cores)):
        source = jnp.where(block == place, offset ^ clip, source)
    limit = jnp.sum(
        jnp.where(lax.broadcasted_iota(jnp.int32, lane.shape, 0) == source, counts, 0),
        axis=0, keepdims=True,
    )
    valid = lax.broadcasted_iota(jnp.int32, (1, slots), 1) % capacity < limit
    heads = [(k, c, i) for k in range(parts) for c in range(cores) for i in range(heads_here)]

    def columns(head):
        k, c, i = head
        at = ((seq ^ k) * cores + (core ^ c)) * heads_here + i
        return pl.ds(pl.multiple_of(at * dim, dim), dim)

    def stored(head, offset):
        k, c, i = head
        found = []
        for g in range(cores):
            at = ((c ^ g) * heads_here + i) * 2 * dim + offset
            for first in range(0, groups * each, each):
                if g == 0:
                    found.append(blocks[first + k][:, at:at + dim])
                else:
                    found.append(blocks[first + parts + g - 1][k, :, at:at + dim])
        return jnp.concatenate(found, axis=0)

    group = 8
    for first in range(0, len(heads), group):
        some = heads[first:first + group]
        scores = [
            lax.dot_general(
                query_ref[:, columns(head)], stored(head, 0), (((1,), (1,)), ((), ())),
                preferred_element_type=F32,
            )
            for head in some
        ]
        scores = [jnp.where(valid, score * (1.0 / math.sqrt(dim)), -1e30) for score in scores]
        peaks = [jnp.max(score, axis=1, keepdims=True) for score in scores]
        weights = [
            jnp.where(valid, jnp.exp(score - peak), 0.0) for score, peak in zip(scores, peaks)
        ]
        sums = [jnp.sum(weight, axis=1, keepdims=True) for weight in weights]
        probs = [(weight / total).astype(BF16) for weight, total in zip(weights, sums)]
        results = [
            jnp.dot(prob, stored(head, dim), preferred_element_type=F32).astype(BF16)
            for prob, head in zip(probs, some)
        ]
        for head, result in zip(some, results):
            out_ref[:, columns(head)] = result


def keyval(texts, gain, weights):
    parts, (rows, width) = len(texts), texts[0].shape
    wide = sum(weight.shape[1] for weight in weights)
    return pl.pallas_call(
        functools.partial(keyval_kernel, parts, len(weights)),
        in_specs=[whole()] * (parts + 1 + len(weights)),
        out_specs=whole(),
        out_shape=pltpu.VMEM((rows, wide), BF16),
        compiler_params=pltpu.CompilerParams(vmem_limit_bytes=VMEM_LIMIT),
        cost_estimate=pl.CostEstimate(
            flops=2 * rows * parts * width * wide,
            bytes_accessed=2 * parts * width * (rows + wide),
            transcendentals=0,
        ),
    )(*texts, gain, *[pltpu.with_memory_space_constraint(x, pltpu.VMEM) for x in weights])


def shards(ffn_hidden, ffn_weight, residual, norm_gain, kv_weight, destination, queries):
    clips, parts, cores = lax.axis_size("clip"), lax.axis_size("seq"), lax.axis_size("tp")
    rows = ffn_hidden.shape[0]
    capacity = rows // min(8, clips)
    share = clips * capacity // cores
    heads_here = kv_weight.shape[1]
    dest = destination.reshape(clips, rows)
    gain = norm_gain.reshape(1, -1)
    weight = kv_weight.reshape(kv_weight.shape[0], heads_here * kv_weight.shape[2])
    weights = [weight] + [swap(weight, "tp", g) for g in range(1, cores)]
    own, send, text = ffn(dest, ffn_hidden, ffn_weight, residual, capacity, cores)
    for g in range(1, cores):
        own = own + swap(send[(g - 1) * share:g * share], "tp", g)
    text = (text.astype(F32) + own).astype(BF16)
    places = clips // cores
    groups = math.gcd(2, places)
    blocks = []
    for first in range(0, places, places // groups):
        arrived = [
            route(text[i * capacity:(i + 1) * capacity], i)
            for i in range(first, first + places // groups)
        ]
        arrived = jnp.concatenate(arrived, axis=0)
        block = keyval(relayed(arrived), gain, weights)
        block = [block] + [swap(block, "seq", k) for k in range(1, parts)]
        blocks += block + [swap(jnp.stack(block), "tp", g) for g in range(1, cores)]
    return pl.pallas_call(
        functools.partial(attend_kernel, parts, cores, heads_here, capacity, groups),
        in_specs=[whole()] * (2 + len(blocks)),
        out_specs=whole(),
        out_shape=jax.ShapeDtypeStruct(queries.shape, BF16),
        compiler_params=pltpu.CompilerParams(vmem_limit_bytes=VMEM_LIMIT),
    )(dest, queries, *blocks)


def solution(mesh):
    return jax.shard_map(
        shards,
        mesh=mesh,
        in_specs=(
            P("clip", "tp"),
            P("tp", "seq"),
            P("clip", "seq"),
            P(),
            P(None, ("seq", "tp"), None),
            P(),
            P(("clip", "seq", "tp"), None),
        ),
        out_specs=P(("clip", "seq", "tp"), None),
        check_vma=False,
    )
```

```python
import functools
import math

import jax
import jax.numpy as jnp
from jax import lax
from jax.experimental import pallas as pl
from jax.experimental.pallas import tpu as pltpu
from jax.sharding import PartitionSpec as P

EPSILON = 1e-06
VMEM_LIMIT = 24 * 1024 * 1024
VMEM_ALL = 60 * 1024 * 1024
F32 = jnp.float32
BF16 = jnp.bfloat16


def whole():
    return pl.BlockSpec(memory_space=pltpu.VMEM)


def swap(value, axis, offset):
    size = lax.axis_size(axis)
    return lax.ppermute(value, axis, [(i, i ^ offset) for i in range(size)])


def relayed(value):
    found = {0: value}
    for k in sorted(range(1, lax.axis_size("seq")), key=lambda k: (bin(k).count("1"), -k)):
        low = k & -k
        found[k] = swap(found[k ^ low], "seq", low)
    return [found[k] for k in range(len(found))]


def routing(clips, cores, capacity):
    if clips == 4 and cores == 2:
        half = capacity // 2
        runs = [
            [(0, 0, half), (3, 0, half), (1, 0, capacity)],
            [(0, half, half), (3, half, half), (2, 0, capacity)],
        ]
        return runs, [[0, 1], [2]]
    each = clips // cores
    runs = [[(t * each + i, 0, capacity) for i in range(each)] for t in range(cores)]
    return runs, [list(range(each))]


def route(value, offsets):
    clips, cores = lax.axis_size("clip"), lax.axis_size("tp")
    if not any(offsets):
        return value
    pairs = [
        (i * cores + t, (i ^ offsets[t]) * cores + t)
        for i in range(clips) for t in range(cores) if offsets[t]
    ]
    moved = lax.ppermute(value, ("clip", "tp"), pairs)
    if all(offsets):
        return moved
    return jnp.where(lax.axis_index("tp") == offsets.index(0), value, moved)


def slot_select(dest_ref, clip, core, capacity, cores):
    clips, rows = dest_ref.shape
    named = dest_ref[pl.ds(clip, 1), :]
    onehot = (lax.broadcasted_iota(jnp.int32, (clips, rows), 0) == named).astype(F32)
    earlier = (
        lax.broadcasted_iota(jnp.int32, (rows, rows), 0)
        < lax.broadcasted_iota(jnp.int32, (rows, rows), 1)
    ).astype(F32)
    before = jnp.dot(onehot, earlier, preferred_element_type=F32)
    rank = jnp.sum(before * onehot, axis=0, keepdims=True).astype(jnp.int32)
    away = named ^ clip
    slot = jnp.zeros_like(away)
    share = clips * capacity // cores
    for t, runs in enumerate(routing(clips, cores, capacity)[0]):
        at = 0
        for offset, first, count in runs:
            inside = (away == offset) & (rank >= first) & (rank < first + count)
            slot = jnp.where(inside, (core ^ t) * share + at - first + rank, slot)
            at += count
    return (lax.broadcasted_iota(jnp.int32, (clips * capacity, rows), 0) == slot).astype(BF16)


def ffn_kernel(capacity, cores, edges, dest_hbm, hidden_hbm, weight_hbm, residual_hbm,
               own_ref, send_ref, text_ref, dest_ref, hidden_ref, weight_ref, residual_ref,
               packed_ref, total_ref, sems):
    clip, core = lax.axis_index("clip"), lax.axis_index("tp")
    share = own_ref.shape[0]
    steps = len(edges) - 1
    parts = [pl.ds(edges[i], edges[i + 1] - edges[i]) for i in range(steps)]
    get_dest = pltpu.make_async_copy(dest_hbm, dest_ref, sems.at[steps])
    get_hidden = pltpu.make_async_copy(hidden_hbm, hidden_ref, sems.at[steps + 1])
    get_residual = pltpu.make_async_copy(residual_hbm, residual_ref, sems.at[steps + 2])
    get_weight = [
        pltpu.make_async_copy(weight_hbm.at[part, :], weight_ref.at[part, :], sems.at[i])
        for i, part in enumerate(parts)
    ]
    for copy in [get_dest, get_hidden] + get_weight[:-1] + [get_residual, get_weight[-1]]:
        copy.start()
    get_dest.wait()
    select = slot_select(dest_ref, clip, core, capacity, cores)
    get_hidden.wait()
    packed_ref[...] = jnp.dot(select, hidden_ref[...], preferred_element_type=F32).astype(BF16)
    for i, part in enumerate(parts):
        if i == steps - 1:
            get_residual.wait()
            text_ref[...] = jnp.dot(
                select[:share], residual_ref[...], preferred_element_type=F32
            ).astype(BF16)
        get_weight[i].wait()
        product = jnp.dot(packed_ref[:, part], weight_ref[part, :], preferred_element_type=F32)
        if i < steps - 1:
            total_ref[...] = product if i == 0 else total_ref[...] + product
        elif i == 0:
            own_ref[...], send_ref[...] = product[:share], product[share:]
        else:
            own_ref[...] = total_ref[:share, :] + product[:share]
            send_ref[...] = total_ref[share:, :] + product[share:]


def ffn(dest, hidden, weight, residual, capacity, cores):
    rows, depth = hidden.shape
    width = weight.shape[1]
    slots = dest.shape[0] * capacity
    share = slots // cores
    unit = depth // 20
    edges = [0, 5 * unit, 10 * unit, 15 * unit, 19 * unit, depth] if unit % 128 == 0 else [0, depth]
    return pl.pallas_call(
        functools.partial(ffn_kernel, capacity, cores, edges),
        in_specs=[pl.BlockSpec(memory_space=pltpu.HBM)] * 4,
        out_specs=[whole()] * 3,
        out_shape=[
            pltpu.VMEM((share, width), F32),
            pltpu.VMEM((slots - share, width), F32),
            pltpu.VMEM((share, width), BF16),
        ],
        scratch_shapes=[
            pltpu.VMEM(dest.shape, jnp.int32),
            pltpu.VMEM(hidden.shape, BF16),
            pltpu.VMEM(weight.shape, BF16),
            pltpu.VMEM(residual.shape, BF16),
            pltpu.VMEM((slots, depth), BF16),
            pltpu.VMEM((slots, width), F32),
            pltpu.SemaphoreType.DMA((len(edges) + 2,)),
        ],
        compiler_params=pltpu.CompilerParams(vmem_limit_bytes=VMEM_LIMIT),
        cost_estimate=pl.CostEstimate(
            flops=2 * slots * depth * (width + rows),
            bytes_accessed=2 * depth * (width + rows),
            transcendentals=0,
        ),
    )(*[pltpu.with_memory_space_constraint(x, pltpu.HBM) for x in (dest, hidden, weight, residual)])


def keyval_kernel(parts, groups, *refs):
    found, (gain_ref, *weights), out_ref = refs[:groups * parts], refs[groups * parts:-1], refs[-1]
    seq = lax.axis_index("seq")
    texts = [
        jnp.concatenate([found[g * parts + k][...] for g in range(groups)], axis=0)
        for k in range(parts)
    ]
    width = texts[0].shape[1]
    squares = 0.0
    for text in texts:
        wide = text.astype(F32)
        squares += jnp.sum(wide * wide, axis=1, keepdims=True)
    scale = lax.rsqrt(squares / (parts * width) + EPSILON)
    totals = [0.0] * len(weights)
    for k, text in enumerate(texts):
        place = pl.ds(pl.multiple_of((seq ^ k) * width, width), width)
        normed = (text.astype(F32) * scale * gain_ref[:, place]).astype(BF16)
        for c, weight in enumerate(weights):
            totals[c] += jnp.dot(normed, weight[place, :], preferred_element_type=F32)
    each = weights[0].shape[1]
    for c in range(len(weights)):
        out_ref[:, c * each:(c + 1) * each] = totals[c].astype(BF16)


def attend_kernel(parts, cores, heads_here, capacity, dest_ref, query_ref, *refs):
    own, others, out_ref = refs[:parts], refs[parts:-1], refs[-1]
    clip, seq, core = lax.axis_index("clip"), lax.axis_index("seq"), lax.axis_index("tp")
    clips = dest_ref.shape[0]
    slots = clips * capacity
    dim = query_ref.shape[1] // (parts * cores * heads_here)
    counts = jnp.sum((dest_ref[...] == clip).astype(jnp.int32), axis=1, keepdims=True)
    share = slots // cores
    lane = lax.broadcasted_iota(jnp.int32, (clips, slots), 1)
    owner, place = (lane // share) ^ core, lane % share
    source, rank = jnp.zeros_like(lane), jnp.zeros_like(lane)
    for t, runs in enumerate(routing(clips, cores, capacity)[0]):
        at = 0
        for offset, first, count in runs:
            inside = (owner == t) & (place >= at) & (place < at + count)
            source = jnp.where(inside, offset ^ clip, source)
            rank = jnp.where(inside, first + place - at, rank)
            at += count
    here = lax.broadcasted_iota(jnp.int32, lane.shape, 0) == source
    valid = jnp.sum(jnp.where(here & (rank < counts), 1, 0), axis=0, keepdims=True) > 0
    heads = [(k, c, i) for k in range(parts) for c in range(cores) for i in range(heads_here)]

    def columns(head):
        k, c, i = head
        at = ((seq ^ k) * cores + (core ^ c)) * heads_here + i
        return pl.ds(pl.multiple_of(at * dim, dim), dim)

    def stored(head, offset):
        k, c, i = head
        found = []
        for g in range(cores):
            at = ((c ^ g) * heads_here + i) * 2 * dim + offset
            if g == 0:
                found.append(own[k][:, at:at + dim])
            else:
                found.append(others[g - 1][k, :, at:at + dim])
        return jnp.concatenate(found, axis=0)

    group = 8
    for first in range(0, len(heads), group):
        some = heads[first:first + group]
        scores = [
            lax.dot_general(
                query_ref[:, columns(head)], stored(head, 0), (((1,), (1,)), ((), ())),
                preferred_element_type=F32,
            )
            for head in some
        ]
        scores = [jnp.where(valid, score * (1.0 / math.sqrt(dim)), -1e30) for score in scores]
        peaks = [jnp.max(score, axis=1, keepdims=True) for score in scores]
        weights = [
            jnp.where(valid, jnp.exp(score - peak), 0.0) for score, peak in zip(scores, peaks)
        ]
        sums = [jnp.sum(weight, axis=1, keepdims=True) for weight in weights]
        probs = [(weight / total).astype(BF16) for weight, total in zip(weights, sums)]
        results = [
            jnp.dot(prob, stored(head, dim), preferred_element_type=F32).astype(BF16)
            for prob, head in zip(probs, some)
        ]
        for head, result in zip(some, results):
            out_ref[:, columns(head)] = result


def keyval(texts, gain, weights):
    groups, parts = len(texts), len(texts[0])
    rows, width = sum(some[0].shape[0] for some in texts), texts[0][0].shape[1]
    wide = sum(weight.shape[1] for weight in weights)
    return pl.pallas_call(
        functools.partial(keyval_kernel, parts, groups),
        in_specs=[whole()] * (groups * parts + 1 + len(weights)),
        out_specs=whole(),
        out_shape=pltpu.VMEM((rows, wide), BF16),
        compiler_params=pltpu.CompilerParams(vmem_limit_bytes=VMEM_LIMIT),
        cost_estimate=pl.CostEstimate(
            flops=2 * rows * parts * width * wide,
            bytes_accessed=2 * parts * width * (rows + wide),
            transcendentals=0,
        ),
    )(
        *[text for some in texts for text in some],
        gain,
        *[pltpu.with_memory_space_constraint(x, pltpu.VMEM) for x in weights],
    )


def shards(ffn_hidden, ffn_weight, residual, norm_gain, kv_weight, destination, queries):
    clips, parts, cores = lax.axis_size("clip"), lax.axis_size("seq"), lax.axis_size("tp")
    rows = ffn_hidden.shape[0]
    capacity = rows // min(8, clips)
    share = clips * capacity // cores
    heads_here = kv_weight.shape[1]
    dest = destination.reshape(clips, rows)
    gain = norm_gain.reshape(1, -1)
    weight = kv_weight.reshape(kv_weight.shape[0], heads_here * kv_weight.shape[2])
    weights = [swap(weight, "tp", g) for g in range(1, cores)]
    own, send, text = ffn(dest, ffn_hidden, ffn_weight, residual, capacity, cores)
    weights, own = lax.optimization_barrier(([weight] + weights, own))
    for g in range(1, cores):
        own = own + swap(send[(g - 1) * share:g * share], "tp", g)
    text = (text.astype(F32) + own).astype(BF16)
    runs, groups = routing(clips, cores, capacity)
    edges = [sum(run[2] for run in runs[0][:n]) for n in range(len(runs[0]) + 1)]
    arrived = [
        route(text[edges[n]:edges[n + 1]], [some[n][0] for some in runs])
        for n in range(len(runs[0]))
    ]
    texts = []
    for group in groups:
        mine = jnp.concatenate([arrived[n] for n in group], axis=0)
        texts.append(relayed(mine))
    block = keyval(texts, gain, weights)
    own = [block] + [swap(block, "seq", k) for k in range(1, parts)]
    packed = jnp.stack(own)
    others = [swap(packed, "tp", g) for g in range(1, cores)]
    return pl.pallas_call(
        functools.partial(attend_kernel, parts, cores, heads_here, capacity),
        in_specs=[whole()] * (2 + len(own) + len(others)),
        out_specs=whole(),
        out_shape=jax.ShapeDtypeStruct(queries.shape, BF16),
        compiler_params=pltpu.CompilerParams(vmem_limit_bytes=VMEM_LIMIT),
    )(dest, queries, *own, *others)


def solution(mesh):
    return jax.shard_map(
        shards,
        mesh=mesh,
        in_specs=(
            P("clip", "tp"),
            P("tp", "seq"),
            P("clip", "seq"),
            P(),
            P(None, ("seq", "tp"), None),
            P(),
            P(("clip", "seq", "tp"), None),
        ),
        out_specs=P(("clip", "seq", "tp"), None),
        check_vma=False,
    )
```

```python
import functools
import math

import jax
import jax.numpy as jnp
from jax import lax
from jax.experimental import pallas as pl
from jax.experimental.pallas import tpu as pltpu
from jax.sharding import PartitionSpec as P

EPSILON = 1e-06
VMEM_LIMIT = 24 * 1024 * 1024
VMEM_ALL = 60 * 1024 * 1024
F32 = jnp.float32
BF16 = jnp.bfloat16


def whole():
    return pl.BlockSpec(memory_space=pltpu.VMEM)


def swap(value, axis, offset):
    size = lax.axis_size(axis)
    return lax.ppermute(value, axis, [(i, i ^ offset) for i in range(size)])


def relayed(value):
    found = {0: value}
    for k in sorted(range(1, lax.axis_size("seq")), key=lambda k: (bin(k).count("1"), -k)):
        low = k & -k
        found[k] = swap(found[k ^ low], "seq", low)
    return [found[k] for k in range(len(found))]


def routing(clips, cores, capacity):
    if clips == 4 and cores == 2:
        runs = [[(1, 0, capacity), (0, 0, capacity)], [(2, 0, capacity), (3, 0, capacity)]]
        return runs, [[0], [1]]
    each = clips // cores
    runs = [[(t * each + i, 0, capacity) for i in range(each)] for t in range(cores)]
    return runs, [list(range(each))]


def route(value, offsets):
    clips, cores = lax.axis_size("clip"), lax.axis_size("tp")
    if not any(offsets):
        return value
    pairs = [
        (i * cores + t, (i ^ offsets[t]) * cores + t)
        for i in range(clips) for t in range(cores) if offsets[t]
    ]
    moved = lax.ppermute(value, ("clip", "tp"), pairs)
    if all(offsets):
        return moved
    return jnp.where(lax.axis_index("tp") == offsets.index(0), value, moved)


def slot_select(dest_ref, clip, core, capacity, cores):
    clips, rows = dest_ref.shape
    named = dest_ref[pl.ds(clip, 1), :]
    onehot = (lax.broadcasted_iota(jnp.int32, (clips, rows), 0) == named).astype(F32)
    earlier = (
        lax.broadcasted_iota(jnp.int32, (rows, rows), 0)
        < lax.broadcasted_iota(jnp.int32, (rows, rows), 1)
    ).astype(F32)
    before = jnp.dot(onehot, earlier, preferred_element_type=F32)
    rank = jnp.sum(before * onehot, axis=0, keepdims=True).astype(jnp.int32)
    away = named ^ clip
    slot = jnp.zeros_like(away)
    share = clips * capacity // cores
    for t, runs in enumerate(routing(clips, cores, capacity)[0]):
        at = 0
        for offset, first, count in runs:
            inside = (away == offset) & (rank >= first) & (rank < first + count)
            slot = jnp.where(inside, (core ^ t) * share + at - first + rank, slot)
            at += count
    return (lax.broadcasted_iota(jnp.int32, (clips * capacity, rows), 0) == slot).astype(BF16)


def ffn_kernel(capacity, cores, edges, dest_hbm, hidden_hbm, weight_hbm, residual_hbm,
               own_ref, send_ref, text_ref, dest_ref, hidden_ref, weight_ref, residual_ref,
               packed_ref, total_ref, sems):
    clip, core = lax.axis_index("clip"), lax.axis_index("tp")
    share = own_ref.shape[0]
    steps = len(edges) - 1
    parts = [pl.ds(edges[i], edges[i + 1] - edges[i]) for i in range(steps)]
    get_dest = pltpu.make_async_copy(dest_hbm, dest_ref, sems.at[steps])
    get_hidden = pltpu.make_async_copy(hidden_hbm, hidden_ref, sems.at[steps + 1])
    get_residual = pltpu.make_async_copy(residual_hbm, residual_ref, sems.at[steps + 2])
    get_weight = [
        pltpu.make_async_copy(weight_hbm.at[part, :], weight_ref.at[part, :], sems.at[i])
        for i, part in enumerate(parts)
    ]
    for copy in [get_dest, get_hidden] + get_weight[:-1] + [get_residual, get_weight[-1]]:
        copy.start()
    get_dest.wait()
    select = slot_select(dest_ref, clip, core, capacity, cores)
    get_hidden.wait()
    packed_ref[...] = jnp.dot(select, hidden_ref[...], preferred_element_type=F32).astype(BF16)
    for i, part in enumerate(parts):
        if i == steps - 1:
            get_residual.wait()
            text_ref[...] = jnp.dot(
                select[:share], residual_ref[...], preferred_element_type=F32
            ).astype(BF16)
        get_weight[i].wait()
        product = jnp.dot(packed_ref[:, part], weight_ref[part, :], preferred_element_type=F32)
        if i < steps - 1:
            total_ref[...] = product if i == 0 else total_ref[...] + product
        elif i == 0:
            own_ref[...], send_ref[...] = product[:share], product[share:]
        else:
            own_ref[...] = total_ref[:share, :] + product[:share]
            send_ref[...] = total_ref[share:, :] + product[share:]


def ffn(dest, hidden, weight, residual, capacity, cores):
    rows, depth = hidden.shape
    width = weight.shape[1]
    slots = dest.shape[0] * capacity
    share = slots // cores
    unit = depth // 20
    edges = [0, 6 * unit, 12 * unit, 18 * unit, depth] if unit % 128 == 0 else [0, depth]
    return pl.pallas_call(
        functools.partial(ffn_kernel, capacity, cores, edges),
        in_specs=[pl.BlockSpec(memory_space=pltpu.HBM)] * 4,
        out_specs=[whole()] * 3,
        out_shape=[
            pltpu.VMEM((share, width), F32),
            pltpu.VMEM((slots - share, width), F32),
            pltpu.VMEM((share, width), BF16),
        ],
        scratch_shapes=[
            pltpu.VMEM(dest.shape, jnp.int32),
            pltpu.VMEM(hidden.shape, BF16),
            pltpu.VMEM(weight.shape, BF16),
            pltpu.VMEM(residual.shape, BF16),
            pltpu.VMEM((slots, depth), BF16),
            pltpu.VMEM((slots, width), F32),
            pltpu.SemaphoreType.DMA((len(edges) + 2,)),
        ],
        compiler_params=pltpu.CompilerParams(vmem_limit_bytes=VMEM_LIMIT),
        cost_estimate=pl.CostEstimate(
            flops=2 * slots * depth * (width + rows),
            bytes_accessed=2 * depth * (width + rows),
            transcendentals=0,
        ),
    )(*[pltpu.with_memory_space_constraint(x, pltpu.HBM) for x in (dest, hidden, weight, residual)])


def keyval_kernel(parts, groups, *refs):
    found, (gain_ref, *weights), out_ref = refs[:groups * parts], refs[groups * parts:-1], refs[-1]
    seq = lax.axis_index("seq")
    texts = [
        jnp.concatenate([found[g * parts + k][...] for g in range(groups)], axis=0)
        for k in range(parts)
    ]
    width = texts[0].shape[1]
    squares = 0.0
    for text in texts:
        wide = text.astype(F32)
        squares += jnp.sum(wide * wide, axis=1, keepdims=True)
    scale = lax.rsqrt(squares / (parts * width) + EPSILON)
    totals = [0.0] * len(weights)
    for k, text in enumerate(texts):
        place = pl.ds(pl.multiple_of((seq ^ k) * width, width), width)
        normed = (text.astype(F32) * scale * gain_ref[:, place]).astype(BF16)
        for c, weight in enumerate(weights):
            totals[c] += jnp.dot(normed, weight[place, :], preferred_element_type=F32)
    each = weights[0].shape[1]
    for c in range(len(weights)):
        out_ref[:, c * each:(c + 1) * each] = totals[c].astype(BF16)


def attend_kernel(parts, cores, heads_here, capacity, dest_ref, query_ref, *refs):
    own, others, out_ref = refs[:parts], refs[parts:-1], refs[-1]
    clip, seq, core = lax.axis_index("clip"), lax.axis_index("seq"), lax.axis_index("tp")
    clips = dest_ref.shape[0]
    slots = clips * capacity
    dim = query_ref.shape[1] // (parts * cores * heads_here)
    counts = jnp.sum((dest_ref[...] == clip).astype(jnp.int32), axis=1, keepdims=True)
    share = slots // cores
    lane = lax.broadcasted_iota(jnp.int32, (clips, slots), 1)
    owner, place = (lane // share) ^ core, lane % share
    source, rank = jnp.zeros_like(lane), jnp.zeros_like(lane)
    for t, runs in enumerate(routing(clips, cores, capacity)[0]):
        at = 0
        for offset, first, count in runs:
            inside = (owner == t) & (place >= at) & (place < at + count)
            source = jnp.where(inside, offset ^ clip, source)
            rank = jnp.where(inside, first + place - at, rank)
            at += count
    here = lax.broadcasted_iota(jnp.int32, lane.shape, 0) == source
    valid = jnp.sum(jnp.where(here & (rank < counts), 1, 0), axis=0, keepdims=True) > 0
    heads = [(k, c, i) for k in range(parts) for c in range(cores) for i in range(heads_here)]

    def columns(head):
        k, c, i = head
        at = ((seq ^ k) * cores + (core ^ c)) * heads_here + i
        return pl.ds(pl.multiple_of(at * dim, dim), dim)

    def stored(head, offset):
        k, c, i = head
        found = []
        for g in range(cores):
            at = ((c ^ g) * heads_here + i) * 2 * dim + offset
            if g == 0:
                found.append(own[k][:, at:at + dim])
            else:
                found.append(others[g - 1][k, :, at:at + dim])
        return jnp.concatenate(found, axis=0)

    group = 8
    for first in range(0, len(heads), group):
        some = heads[first:first + group]
        scores = [
            lax.dot_general(
                query_ref[:, columns(head)], stored(head, 0), (((1,), (1,)), ((), ())),
                preferred_element_type=F32,
            )
            for head in some
        ]
        scores = [jnp.where(valid, score * (1.0 / math.sqrt(dim)), -1e30) for score in scores]
        peaks = [jnp.max(score, axis=1, keepdims=True) for score in scores]
        weights = [
            jnp.where(valid, jnp.exp(score - peak), 0.0) for score, peak in zip(scores, peaks)
        ]
        sums = [jnp.sum(weight, axis=1, keepdims=True) for weight in weights]
        probs = [(weight / total).astype(BF16) for weight, total in zip(weights, sums)]
        results = [
            jnp.dot(prob, stored(head, dim), preferred_element_type=F32).astype(BF16)
            for prob, head in zip(probs, some)
        ]
        for head, result in zip(some, results):
            out_ref[:, columns(head)] = result


def keyval(texts, gain, weights):
    groups, parts = len(texts), len(texts[0])
    rows, width = sum(some[0].shape[0] for some in texts), texts[0][0].shape[1]
    wide = sum(weight.shape[1] for weight in weights)
    return pl.pallas_call(
        functools.partial(keyval_kernel, parts, groups),
        in_specs=[whole()] * (groups * parts + 1 + len(weights)),
        out_specs=whole(),
        out_shape=pltpu.VMEM((rows, wide), BF16),
        compiler_params=pltpu.CompilerParams(vmem_limit_bytes=VMEM_LIMIT),
        cost_estimate=pl.CostEstimate(
            flops=2 * rows * parts * width * wide,
            bytes_accessed=2 * parts * width * (rows + wide),
            transcendentals=0,
        ),
    )(
        *[text for some in texts for text in some],
        gain,
        *[pltpu.with_memory_space_constraint(x, pltpu.VMEM) for x in weights],
    )


def shards(ffn_hidden, ffn_weight, residual, norm_gain, kv_weight, destination, queries):
    clips, parts, cores = lax.axis_size("clip"), lax.axis_size("seq"), lax.axis_size("tp")
    rows = ffn_hidden.shape[0]
    capacity = rows // min(8, clips)
    share = clips * capacity // cores
    heads_here = kv_weight.shape[1]
    dest = destination.reshape(clips, rows)
    gain = norm_gain.reshape(1, -1)
    weight = kv_weight.reshape(kv_weight.shape[0], heads_here * kv_weight.shape[2])
    weights = [swap(weight, "tp", g) for g in range(1, cores)]
    own, send, text = ffn(dest, ffn_hidden, ffn_weight, residual, capacity, cores)
    weights, own = lax.optimization_barrier(([weight] + weights, own))
    for g in range(1, cores):
        own = own + swap(send[(g - 1) * share:g * share], "tp", g)
    text = (text.astype(F32) + own).astype(BF16)
    runs, groups = routing(clips, cores, capacity)
    edges = [sum(run[2] for run in runs[0][:n]) for n in range(len(runs[0]) + 1)]
    pieces = lax.optimization_barrier(
        [text[edges[n]:edges[n + 1]] for n in range(len(runs[0]))]
    )
    arrived = [
        route(piece, [some[n][0] for some in runs]) for n, piece in enumerate(pieces)
    ]
    texts = []
    for group in groups:
        mine = jnp.concatenate([arrived[n] for n in group], axis=0)
        texts.append(relayed(mine))
    block = keyval(texts, gain, weights)
    own = [block] + [swap(block, "seq", k) for k in range(1, parts)]
    packed = jnp.stack(own)
    others = [swap(packed, "tp", g) for g in range(1, cores)]
    return pl.pallas_call(
        functools.partial(attend_kernel, parts, cores, heads_here, capacity),
        in_specs=[whole()] * (2 + len(own) + len(others)),
        out_specs=whole(),
        out_shape=jax.ShapeDtypeStruct(queries.shape, BF16),
        compiler_params=pltpu.CompilerParams(vmem_limit_bytes=VMEM_LIMIT),
    )(dest, queries, *own, *others)


def solution(mesh):
    return jax.shard_map(
        shards,
        mesh=mesh,
        in_specs=(
            P("clip", "tp"),
            P("tp", "seq"),
            P("clip", "seq"),
            P(),
            P(None, ("seq", "tp"), None),
            P(),
            P(("clip", "seq", "tp"), None),
        ),
        out_specs=P(("clip", "seq", "tp"), None),
        check_vma=False,
    )
```

```python
import functools
import math

import jax
import jax.numpy as jnp
from jax import lax
from jax.experimental import pallas as pl
from jax.experimental.pallas import tpu as pltpu
from jax.sharding import PartitionSpec as P

EPSILON = 1e-06
VMEM_LIMIT = 24 * 1024 * 1024
VMEM_ALL = 60 * 1024 * 1024
F32 = jnp.float32
BF16 = jnp.bfloat16


def whole():
    return pl.BlockSpec(memory_space=pltpu.VMEM)


def swap(value, axis, offset):
    size = lax.axis_size(axis)
    return lax.ppermute(value, axis, [(i, i ^ offset) for i in range(size)])


def relayed(value):
    found = {0: value}
    for k in sorted(range(1, lax.axis_size("seq")), key=lambda k: (bin(k).count("1"), -k)):
        low = k & -k
        found[k] = swap(found[k ^ low], "seq", low)
    return [found[k] for k in range(len(found))]


def routing(clips, cores, capacity):
    if clips == 4 and cores == 2:
        runs = [[(1, 0, capacity), (0, 0, capacity)], [(2, 0, capacity), (3, 0, capacity)]]
        return runs, [[0], [1]]
    each = clips // cores
    runs = [[(t * each + i, 0, capacity) for i in range(each)] for t in range(cores)]
    return runs, [list(range(each))]


def route(value, offsets):
    clips, cores = lax.axis_size("clip"), lax.axis_size("tp")
    if not any(offsets):
        return value
    pairs = [
        (i * cores + t, (i ^ offsets[t]) * cores + t)
        for i in range(clips) for t in range(cores) if offsets[t]
    ]
    moved = lax.ppermute(value, ("clip", "tp"), pairs)
    if all(offsets):
        return moved
    return jnp.where(lax.axis_index("tp") == offsets.index(0), value, moved)


def slot_select(dest_ref, clip, core, capacity, cores):
    clips, rows = dest_ref.shape
    named = dest_ref[pl.ds(clip, 1), :]
    onehot = (lax.broadcasted_iota(jnp.int32, (clips, rows), 0) == named).astype(F32)
    earlier = (
        lax.broadcasted_iota(jnp.int32, (rows, rows), 0)
        < lax.broadcasted_iota(jnp.int32, (rows, rows), 1)
    ).astype(F32)
    before = jnp.dot(onehot, earlier, preferred_element_type=F32)
    rank = jnp.sum(before * onehot, axis=0, keepdims=True).astype(jnp.int32)
    away = named ^ clip
    slot = jnp.zeros_like(away)
    share = clips * capacity // cores
    for t, runs in enumerate(routing(clips, cores, capacity)[0]):
        at = 0
        for offset, first, count in runs:
            inside = (away == offset) & (rank >= first) & (rank < first + count)
            slot = jnp.where(inside, (core ^ t) * share + at - first + rank, slot)
            at += count
    return (lax.broadcasted_iota(jnp.int32, (clips * capacity, rows), 0) == slot).astype(BF16)


def ffn_kernel(capacity, cores, edges, dest_hbm, hidden_hbm, weight_hbm, residual_hbm,
               own_ref, send_ref, text_ref, dest_ref, hidden_ref, weight_ref, residual_ref,
               packed_ref, total_ref, sems):
    clip, core = lax.axis_index("clip"), lax.axis_index("tp")
    share = own_ref.shape[0]
    steps = len(edges) - 1
    parts = [pl.ds(edges[i], edges[i + 1] - edges[i]) for i in range(steps)]
    get_dest = pltpu.make_async_copy(dest_hbm, dest_ref, sems.at[steps])
    get_hidden = pltpu.make_async_copy(hidden_hbm, hidden_ref, sems.at[steps + 1])
    get_residual = pltpu.make_async_copy(residual_hbm, residual_ref, sems.at[steps + 2])
    get_weight = [
        pltpu.make_async_copy(weight_hbm.at[part, :], weight_ref.at[part, :], sems.at[i])
        for i, part in enumerate(parts)
    ]
    for copy in [get_dest, get_hidden] + get_weight[:-1] + [get_residual, get_weight[-1]]:
        copy.start()
    get_dest.wait()
    select = slot_select(dest_ref, clip, core, capacity, cores)
    get_hidden.wait()
    packed_ref[...] = jnp.dot(select, hidden_ref[...], preferred_element_type=F32).astype(BF16)
    for i, part in enumerate(parts):
        if i == steps - 1:
            get_residual.wait()
            text_ref[...] = jnp.dot(
                select[:share], residual_ref[...], preferred_element_type=F32
            ).astype(BF16)
        get_weight[i].wait()
        product = jnp.dot(packed_ref[:, part], weight_ref[part, :], preferred_element_type=F32)
        if i < steps - 1:
            total_ref[...] = product if i == 0 else total_ref[...] + product
        elif i == 0:
            own_ref[...], send_ref[...] = product[:share], product[share:]
        else:
            own_ref[...] = total_ref[:share, :] + product[:share]
            send_ref[...] = total_ref[share:, :] + product[share:]


def ffn(dest, hidden, weight, residual, capacity, cores):
    rows, depth = hidden.shape
    width = weight.shape[1]
    slots = dest.shape[0] * capacity
    share = slots // cores
    unit = depth // 20
    edges = [0, 6 * unit, 12 * unit, 18 * unit, depth] if unit % 128 == 0 else [0, depth]
    return pl.pallas_call(
        functools.partial(ffn_kernel, capacity, cores, edges),
        in_specs=[pl.BlockSpec(memory_space=pltpu.HBM)] * 4,
        out_specs=[whole()] * 3,
        out_shape=[
            pltpu.VMEM((share, width), F32),
            pltpu.VMEM((slots - share, width), F32),
            pltpu.VMEM((share, width), BF16),
        ],
        scratch_shapes=[
            pltpu.VMEM(dest.shape, jnp.int32),
            pltpu.VMEM(hidden.shape, BF16),
            pltpu.VMEM(weight.shape, BF16),
            pltpu.VMEM(residual.shape, BF16),
            pltpu.VMEM((slots, depth), BF16),
            pltpu.VMEM((slots, width), F32),
            pltpu.SemaphoreType.DMA((len(edges) + 2,)),
        ],
        compiler_params=pltpu.CompilerParams(vmem_limit_bytes=VMEM_LIMIT),
        cost_estimate=pl.CostEstimate(
            flops=2 * slots * depth * (width + rows),
            bytes_accessed=2 * depth * (width + rows),
            transcendentals=0,
        ),
    )(*[pltpu.with_memory_space_constraint(x, pltpu.HBM) for x in (dest, hidden, weight, residual)])


def keyval_kernel(parts, groups, *refs):
    found, (gain_ref, *weights), out_ref = refs[:groups * parts], refs[groups * parts:-1], refs[-1]
    seq = lax.axis_index("seq")
    texts = [
        jnp.concatenate([found[g * parts + k][...] for g in range(groups)], axis=0)
        for k in range(parts)
    ]
    width = texts[0].shape[1]
    squares = 0.0
    for text in texts:
        wide = text.astype(F32)
        squares += jnp.sum(wide * wide, axis=1, keepdims=True)
    scale = lax.rsqrt(squares / (parts * width) + EPSILON)
    totals = [0.0] * len(weights)
    for k, text in enumerate(texts):
        place = pl.ds(pl.multiple_of((seq ^ k) * width, width), width)
        normed = (text.astype(F32) * scale * gain_ref[:, place]).astype(BF16)
        for c, weight in enumerate(weights):
            totals[c] += jnp.dot(normed, weight[place, :], preferred_element_type=F32)
    each = weights[0].shape[1]
    for c in range(len(weights)):
        out_ref[:, c * each:(c + 1) * each] = totals[c].astype(BF16)


def attend_kernel(parts, cores, heads_here, capacity, dest_ref, query_ref, *refs):
    own, others, out_ref = refs[:parts], refs[parts:-1], refs[-1]
    clip, seq, core = lax.axis_index("clip"), lax.axis_index("seq"), lax.axis_index("tp")
    clips = dest_ref.shape[0]
    slots = clips * capacity
    dim = query_ref.shape[1] // (parts * cores * heads_here)
    counts = jnp.sum((dest_ref[...] == clip).astype(jnp.int32), axis=1, keepdims=True)
    share = slots // cores
    lane = lax.broadcasted_iota(jnp.int32, (clips, slots), 1)
    owner, place = (lane // share) ^ core, lane % share
    source, rank = jnp.zeros_like(lane), jnp.zeros_like(lane)
    for t, runs in enumerate(routing(clips, cores, capacity)[0]):
        at = 0
        for offset, first, count in runs:
            inside = (owner == t) & (place >= at) & (place < at + count)
            source = jnp.where(inside, offset ^ clip, source)
            rank = jnp.where(inside, first + place - at, rank)
            at += count
    here = lax.broadcasted_iota(jnp.int32, lane.shape, 0) == source
    valid = jnp.sum(jnp.where(here & (rank < counts), 1, 0), axis=0, keepdims=True) > 0
    heads = [(k, c, i) for k in range(parts) for c in range(cores) for i in range(heads_here)]

    def columns(head):
        k, c, i = head
        at = ((seq ^ k) * cores + (core ^ c)) * heads_here + i
        return pl.ds(pl.multiple_of(at * dim, dim), dim)

    def stored(head, offset):
        k, c, i = head
        found = []
        for g in range(cores):
            at = ((c ^ g) * heads_here + i) * 2 * dim + offset
            if g == 0:
                found.append(own[k][:, at:at + dim])
            else:
                found.append(others[g - 1][k, :, at:at + dim])
        return jnp.concatenate(found, axis=0)

    group = 8
    for first in range(0, len(heads), group):
        some = heads[first:first + group]
        scores = [
            lax.dot_general(
                query_ref[:, columns(head)], stored(head, 0), (((1,), (1,)), ((), ())),
                preferred_element_type=F32,
            )
            for head in some
        ]
        scores = [jnp.where(valid, score * (1.0 / math.sqrt(dim)), -1e30) for score in scores]
        peaks = [jnp.max(score, axis=1, keepdims=True) for score in scores]
        weights = [
            jnp.where(valid, jnp.exp(score - peak), 0.0) for score, peak in zip(scores, peaks)
        ]
        sums = [jnp.sum(weight, axis=1, keepdims=True) for weight in weights]
        probs = [(weight / total).astype(BF16) for weight, total in zip(weights, sums)]
        results = [
            jnp.dot(prob, stored(head, dim), preferred_element_type=F32).astype(BF16)
            for prob, head in zip(probs, some)
        ]
        for head, result in zip(some, results):
            out_ref[:, columns(head)] = result


def keyval(texts, gain, weights):
    groups, parts = len(texts), len(texts[0])
    rows, width = sum(some[0].shape[0] for some in texts), texts[0][0].shape[1]
    wide = sum(weight.shape[1] for weight in weights)
    return pl.pallas_call(
        functools.partial(keyval_kernel, parts, groups),
        in_specs=[whole()] * (groups * parts + 1 + len(weights)),
        out_specs=whole(),
        out_shape=pltpu.VMEM((rows, wide), BF16),
        compiler_params=pltpu.CompilerParams(vmem_limit_bytes=VMEM_LIMIT),
        cost_estimate=pl.CostEstimate(
            flops=2 * rows * parts * width * wide,
            bytes_accessed=2 * parts * width * (rows + wide),
            transcendentals=0,
        ),
    )(
        *[text for some in texts for text in some],
        gain,
        *[pltpu.with_memory_space_constraint(x, pltpu.VMEM) for x in weights],
    )


def shards(ffn_hidden, ffn_weight, residual, norm_gain, kv_weight, destination, queries):
    clips, parts, cores = lax.axis_size("clip"), lax.axis_size("seq"), lax.axis_size("tp")
    rows = ffn_hidden.shape[0]
    capacity = rows // min(8, clips)
    share = clips * capacity // cores
    heads_here = kv_weight.shape[1]
    dest = destination.reshape(clips, rows)
    gain = norm_gain.reshape(1, -1)
    weight = kv_weight.reshape(kv_weight.shape[0], heads_here * kv_weight.shape[2])
    weights = [swap(weight, "tp", g) for g in range(1, cores)]
    own, send, text = ffn(dest, ffn_hidden, ffn_weight, residual, capacity, cores)
    weights = [weight] + weights
    for g in range(1, cores):
        own = own + swap(send[(g - 1) * share:g * share], "tp", g)
    text = (text.astype(F32) + own).astype(BF16)
    runs, groups = routing(clips, cores, capacity)
    edges = [sum(run[2] for run in runs[0][:n]) for n in range(len(runs[0]) + 1)]
    pieces = lax.optimization_barrier(
        [text[edges[n]:edges[n + 1]] for n in range(len(runs[0]))]
    )
    arrived = [
        route(piece, [some[n][0] for some in runs]) for n, piece in enumerate(pieces)
    ]
    texts = []
    for group in groups:
        mine = jnp.concatenate([arrived[n] for n in group], axis=0)
        texts.append(relayed(mine))
    block = keyval(texts, gain, weights)
    own = [block] + [swap(block, "seq", k) for k in range(1, parts)]
    packed = jnp.stack(own)
    others = [swap(packed, "tp", g) for g in range(1, cores)]
    return pl.pallas_call(
        functools.partial(attend_kernel, parts, cores, heads_here, capacity),
        in_specs=[whole()] * (2 + len(own) + len(others)),
        out_specs=whole(),
        out_shape=jax.ShapeDtypeStruct(queries.shape, BF16),
        compiler_params=pltpu.CompilerParams(vmem_limit_bytes=VMEM_LIMIT),
    )(dest, queries, *own, *others)


def solution(mesh):
    return jax.shard_map(
        shards,
        mesh=mesh,
        in_specs=(
            P("clip", "tp"),
            P("tp", "seq"),
            P("clip", "seq"),
            P(),
            P(None, ("seq", "tp"), None),
            P(),
            P(("clip", "seq", "tp"), None),
        ),
        out_specs=P(("clip", "seq", "tp"), None),
        check_vma=False,
    )
```

```python
import functools
import math

import jax
import jax.numpy as jnp
from jax import lax
from jax.experimental import pallas as pl
from jax.experimental.pallas import tpu as pltpu
from jax.sharding import PartitionSpec as P

EPSILON = 1e-06
VMEM_LIMIT = 24 * 1024 * 1024
VMEM_ALL = 60 * 1024 * 1024
F32 = jnp.float32
BF16 = jnp.bfloat16


def whole():
    return pl.BlockSpec(memory_space=pltpu.VMEM)


def swap(value, axis, offset):
    size = lax.axis_size(axis)
    return lax.ppermute(value, axis, [(i, i ^ offset) for i in range(size)])


def relayed(value):
    found = {0: value}
    for k in sorted(range(1, lax.axis_size("seq")), key=lambda k: (bin(k).count("1"), -k)):
        low = k & -k
        found[k] = swap(found[k ^ low], "seq", low)
    return [found[k] for k in range(len(found))]


def routing(clips, cores, capacity):
    if clips == 4 and cores == 2:
        half = capacity // 2
        runs = [
            [(0, 0, half), (3, 0, half), (1, 0, capacity)],
            [(0, half, half), (3, half, half), (2, 0, capacity)],
        ]
        return runs, [[0, 1], [2]]
    each = clips // cores
    runs = [[(t * each + i, 0, capacity) for i in range(each)] for t in range(cores)]
    return runs, [list(range(each))]


def route(value, offsets):
    clips, cores = lax.axis_size("clip"), lax.axis_size("tp")
    if not any(offsets):
        return value
    pairs = [
        (i * cores + t, (i ^ offsets[t]) * cores + t)
        for i in range(clips) for t in range(cores) if offsets[t]
    ]
    moved = lax.ppermute(value, ("clip", "tp"), pairs)
    if all(offsets):
        return moved
    return jnp.where(lax.axis_index("tp") == offsets.index(0), value, moved)


def slot_select(dest_ref, clip, core, capacity, cores):
    clips, rows = dest_ref.shape
    named = dest_ref[pl.ds(clip, 1), :]
    onehot = (lax.broadcasted_iota(jnp.int32, (clips, rows), 0) == named).astype(F32)
    earlier = (
        lax.broadcasted_iota(jnp.int32, (rows, rows), 0)
        < lax.broadcasted_iota(jnp.int32, (rows, rows), 1)
    ).astype(F32)
    before = jnp.dot(onehot, earlier, preferred_element_type=F32)
    rank = jnp.sum(before * onehot, axis=0, keepdims=True).astype(jnp.int32)
    away = named ^ clip
    slot = jnp.zeros_like(away)
    share = clips * capacity // cores
    for t, runs in enumerate(routing(clips, cores, capacity)[0]):
        at = 0
        for offset, first, count in runs:
            inside = (away == offset) & (rank >= first) & (rank < first + count)
            slot = jnp.where(inside, (core ^ t) * share + at - first + rank, slot)
            at += count
    return (lax.broadcasted_iota(jnp.int32, (clips * capacity, rows), 0) == slot).astype(BF16)


def ffn_kernel(capacity, cores, edges, dest_hbm, hidden_hbm, weight_hbm, residual_hbm,
               own_ref, send_ref, text_ref, dest_ref, hidden_ref, weight_ref, residual_ref,
               packed_ref, total_ref, sems):
    clip, core = lax.axis_index("clip"), lax.axis_index("tp")
    share = own_ref.shape[0]
    steps = len(edges) - 1
    parts = [pl.ds(edges[i], edges[i + 1] - edges[i]) for i in range(steps)]
    get_dest = pltpu.make_async_copy(dest_hbm, dest_ref, sems.at[steps])
    get_hidden = pltpu.make_async_copy(hidden_hbm, hidden_ref, sems.at[steps + 1])
    get_residual = pltpu.make_async_copy(residual_hbm, residual_ref, sems.at[steps + 2])
    get_weight = [
        pltpu.make_async_copy(weight_hbm.at[part, :], weight_ref.at[part, :], sems.at[i])
        for i, part in enumerate(parts)
    ]
    for copy in [get_dest, get_hidden] + get_weight[:-1] + [get_residual, get_weight[-1]]:
        copy.start()
    get_dest.wait()
    select = slot_select(dest_ref, clip, core, capacity, cores)
    get_hidden.wait()
    packed_ref[...] = jnp.dot(select, hidden_ref[...], preferred_element_type=F32).astype(BF16)
    for i, part in enumerate(parts):
        if i == steps - 1:
            get_residual.wait()
            text_ref[...] = jnp.dot(
                select[:share], residual_ref[...], preferred_element_type=F32
            ).astype(BF16)
        get_weight[i].wait()
        product = jnp.dot(packed_ref[:, part], weight_ref[part, :], preferred_element_type=F32)
        if i < steps - 1:
            total_ref[...] = product if i == 0 else total_ref[...] + product
        elif i == 0:
            own_ref[...], send_ref[...] = product[:share], product[share:]
        else:
            own_ref[...] = total_ref[:share, :] + product[:share]
            send_ref[...] = total_ref[share:, :] + product[share:]


def ffn(dest, hidden, weight, residual, capacity, cores):
    rows, depth = hidden.shape
    width = weight.shape[1]
    slots = dest.shape[0] * capacity
    share = slots // cores
    unit = depth // 20
    edges = [0, 5 * unit, 10 * unit, 15 * unit, 19 * unit, depth] if unit % 128 == 0 else [0, depth]
    return pl.pallas_call(
        functools.partial(ffn_kernel, capacity, cores, edges),
        in_specs=[pl.BlockSpec(memory_space=pltpu.HBM)] * 4,
        out_specs=[whole()] * 3,
        out_shape=[
            pltpu.VMEM((share, width), F32),
            pltpu.VMEM((slots - share, width), F32),
            pltpu.VMEM((share, width), BF16),
        ],
        scratch_shapes=[
            pltpu.VMEM(dest.shape, jnp.int32),
            pltpu.VMEM(hidden.shape, BF16),
            pltpu.VMEM(weight.shape, BF16),
            pltpu.VMEM(residual.shape, BF16),
            pltpu.VMEM((slots, depth), BF16),
            pltpu.VMEM((slots, width), F32),
            pltpu.SemaphoreType.DMA((len(edges) + 2,)),
        ],
        compiler_params=pltpu.CompilerParams(vmem_limit_bytes=VMEM_LIMIT),
        cost_estimate=pl.CostEstimate(
            flops=2 * slots * depth * (width + rows),
            bytes_accessed=2 * depth * (width + rows),
            transcendentals=0,
        ),
    )(*[pltpu.with_memory_space_constraint(x, pltpu.HBM) for x in (dest, hidden, weight, residual)])


def keyval_kernel(parts, groups, *refs):
    found, (gain_ref, *weights), out_ref = refs[:groups * parts], refs[groups * parts:-1], refs[-1]
    seq = lax.axis_index("seq")
    texts = [
        jnp.concatenate([found[g * parts + k][...] for g in range(groups)], axis=0)
        for k in range(parts)
    ]
    width = texts[0].shape[1]
    squares = 0.0
    for text in texts:
        wide = text.astype(F32)
        squares += jnp.sum(wide * wide, axis=1, keepdims=True)
    scale = lax.rsqrt(squares / (parts * width) + EPSILON)
    totals = [0.0] * len(weights)
    for k, text in enumerate(texts):
        place = pl.ds(pl.multiple_of((seq ^ k) * width, width), width)
        normed = (text.astype(F32) * scale * gain_ref[:, place]).astype(BF16)
        for c, weight in enumerate(weights):
            totals[c] += jnp.dot(normed, weight[place, :], preferred_element_type=F32)
    each = weights[0].shape[1]
    for c in range(len(weights)):
        out_ref[:, c * each:(c + 1) * each] = totals[c].astype(BF16)


def attend_kernel(parts, cores, heads_here, capacity, steps, dest_ref, query_ref, *refs):
    own, refs = refs[:len(steps)], refs[len(steps):]
    others, done, out_ref = refs[:cores - 1], refs[cores - 1:-1], refs[-1]
    clip, seq, core = lax.axis_index("clip"), lax.axis_index("seq"), lax.axis_index("tp")
    clips = dest_ref.shape[0]
    slots = clips * capacity
    dim = query_ref.shape[1] // (parts * cores * heads_here)
    counts = jnp.sum((dest_ref[...] == clip).astype(jnp.int32), axis=1, keepdims=True)
    share = slots // cores
    lane = lax.broadcasted_iota(jnp.int32, (clips, slots), 1)
    owner, place = (lane // share) ^ core, lane % share
    source, rank = jnp.zeros_like(lane), jnp.zeros_like(lane)
    for t, runs in enumerate(routing(clips, cores, capacity)[0]):
        at = 0
        for offset, first, count in runs:
            inside = (owner == t) & (place >= at) & (place < at + count)
            source = jnp.where(inside, offset ^ clip, source)
            rank = jnp.where(inside, first + place - at, rank)
            at += count
    here = lax.broadcasted_iota(jnp.int32, lane.shape, 0) == source
    valid = jnp.sum(jnp.where(here & (rank < counts), 1, 0), axis=0, keepdims=True) > 0
    heads = [
        (k, c, i) for k in range(len(steps)) for c in range(cores) for i in range(heads_here)
    ]

    def columns(head):
        k, c, i = head
        at = ((seq ^ steps[k]) * cores + (core ^ c)) * heads_here + i
        return pl.ds(pl.multiple_of(at * dim, dim), dim)

    def stored(head, offset):
        k, c, i = head
        found = []
        for g in range(cores):
            at = ((c ^ g) * heads_here + i) * 2 * dim + offset
            if g == 0:
                found.append(own[k][:, at:at + dim])
            else:
                found.append(others[g - 1][k, :, at:at + dim])
        return jnp.concatenate(found, axis=0)

    if done:
        out_ref[...] = done[0][...]
    group = 8
    for first in range(0, len(heads), group):
        some = heads[first:first + group]
        scores = [
            lax.dot_general(
                query_ref[:, columns(head)], stored(head, 0), (((1,), (1,)), ((), ())),
                preferred_element_type=F32,
            )
            for head in some
        ]
        scores = [jnp.where(valid, score * (1.0 / math.sqrt(dim)), -1e30) for score in scores]
        peaks = [jnp.max(score, axis=1, keepdims=True) for score in scores]
        weights = [
            jnp.where(valid, jnp.exp(score - peak), 0.0) for score, peak in zip(scores, peaks)
        ]
        sums = [jnp.sum(weight, axis=1, keepdims=True) for weight in weights]
        probs = [(weight / total).astype(BF16) for weight, total in zip(weights, sums)]
        results = [
            jnp.dot(prob, stored(head, dim), preferred_element_type=F32).astype(BF16)
            for prob, head in zip(probs, some)
        ]
        for head, result in zip(some, results):
            out_ref[:, columns(head)] = result


def keyval(texts, gain, weights):
    groups, parts = len(texts), len(texts[0])
    rows, width = sum(some[0].shape[0] for some in texts), texts[0][0].shape[1]
    wide = sum(weight.shape[1] for weight in weights)
    return pl.pallas_call(
        functools.partial(keyval_kernel, parts, groups),
        in_specs=[whole()] * (groups * parts + 1 + len(weights)),
        out_specs=whole(),
        out_shape=pltpu.VMEM((rows, wide), BF16),
        compiler_params=pltpu.CompilerParams(vmem_limit_bytes=VMEM_LIMIT),
        cost_estimate=pl.CostEstimate(
            flops=2 * rows * parts * width * wide,
            bytes_accessed=2 * parts * width * (rows + wide),
            transcendentals=0,
        ),
    )(
        *[text for some in texts for text in some],
        gain,
        *[pltpu.with_memory_space_constraint(x, pltpu.VMEM) for x in weights],
    )


def shards(ffn_hidden, ffn_weight, residual, norm_gain, kv_weight, destination, queries):
    clips, parts, cores = lax.axis_size("clip"), lax.axis_size("seq"), lax.axis_size("tp")
    rows = ffn_hidden.shape[0]
    capacity = rows // min(8, clips)
    share = clips * capacity // cores
    heads_here = kv_weight.shape[1]
    dest = destination.reshape(clips, rows)
    gain = norm_gain.reshape(1, -1)
    weight = kv_weight.reshape(kv_weight.shape[0], heads_here * kv_weight.shape[2])
    weights = [swap(weight, "tp", g) for g in range(1, cores)]
    own, send, text = ffn(dest, ffn_hidden, ffn_weight, residual, capacity, cores)
    weights, own = lax.optimization_barrier(([weight] + weights, own))
    for g in range(1, cores):
        own = own + swap(send[(g - 1) * share:g * share], "tp", g)
    text = (text.astype(F32) + own).astype(BF16)
    runs, groups = routing(clips, cores, capacity)
    edges = [sum(run[2] for run in runs[0][:n]) for n in range(len(runs[0]) + 1)]
    arrived = [
        route(text[edges[n]:edges[n + 1]], [some[n][0] for some in runs])
        for n in range(len(runs[0]))
    ]
    texts = []
    for group in groups:
        mine = jnp.concatenate([arrived[n] for n in group], axis=0)
        texts.append(relayed(mine))
    block = keyval(texts, gain, weights)
    own = [block] + [swap(block, "seq", k) for k in range(1, parts)]

    def attend(steps, done):
        some = [own[k] for k in steps]
        others = [swap(jnp.stack(some), "tp", g) for g in range(1, cores)]
        return pl.pallas_call(
            functools.partial(attend_kernel, parts, cores, heads_here, capacity, steps),
            in_specs=[whole()] * (2 + len(some) + len(others) + len(done)),
            out_specs=whole(),
            out_shape=jax.ShapeDtypeStruct(queries.shape, BF16),
            compiler_params=pltpu.CompilerParams(vmem_limit_bytes=VMEM_LIMIT),
        )(dest, queries, *some, *others, *done)

    order = [0] + list(range(parts - 1, 0, -1))
    cut = max(1, parts // 2)
    output = attend(order[:cut], [])
    return attend(order[:cut - 1:-1], [output]) if order[cut:] else output


def solution(mesh):
    return jax.shard_map(
        shards,
        mesh=mesh,
        in_specs=(
            P("clip", "tp"),
            P("tp", "seq"),
            P("clip", "seq"),
            P(),
            P(None, ("seq", "tp"), None),
            P(),
            P(("clip", "seq", "tp"), None),
        ),
        out_specs=P(("clip", "seq", "tp"), None),
        check_vma=False,
    )
```

```python
import functools
import math

import jax
import jax.numpy as jnp
from jax import lax
from jax.experimental import pallas as pl
from jax.experimental.pallas import tpu as pltpu
from jax.sharding import PartitionSpec as P

EPSILON = 1e-06
VMEM_LIMIT = 24 * 1024 * 1024
VMEM_ALL = 60 * 1024 * 1024
F32 = jnp.float32
BF16 = jnp.bfloat16


def whole():
    return pl.BlockSpec(memory_space=pltpu.VMEM)


def swap(value, axis, offset):
    size = lax.axis_size(axis)
    return lax.ppermute(value, axis, [(i, i ^ offset) for i in range(size)])


def relayed(value):
    found = {0: value}
    for k in sorted(range(1, lax.axis_size("seq")), key=lambda k: (bin(k).count("1"), -k)):
        low = k & -k
        found[k] = swap(found[k ^ low], "seq", low)
    return [found[k] for k in range(len(found))]


def routing(clips, cores, capacity):
    if clips == 4 and cores == 2:
        half = capacity // 2
        runs = [
            [(0, 0, half), (3, 0, half), (1, 0, capacity)],
            [(0, half, half), (3, half, half), (2, 0, capacity)],
        ]
        return runs, [[0, 1], [2]]
    each = clips // cores
    runs = [[(t * each + i, 0, capacity) for i in range(each)] for t in range(cores)]
    return runs, [list(range(each))]


def route(value, offsets):
    clips, cores = lax.axis_size("clip"), lax.axis_size("tp")
    if not any(offsets):
        return value
    pairs = [
        (i * cores + t, (i ^ offsets[t]) * cores + t)
        for i in range(clips) for t in range(cores) if offsets[t]
    ]
    moved = lax.ppermute(value, ("clip", "tp"), pairs)
    if all(offsets):
        return moved
    return jnp.where(lax.axis_index("tp") == offsets.index(0), value, moved)


def slot_select(dest_ref, clip, core, capacity, cores):
    clips, rows = dest_ref.shape
    named = dest_ref[pl.ds(clip, 1), :]
    onehot = (lax.broadcasted_iota(jnp.int32, (clips, rows), 0) == named).astype(F32)
    earlier = (
        lax.broadcasted_iota(jnp.int32, (rows, rows), 0)
        < lax.broadcasted_iota(jnp.int32, (rows, rows), 1)
    ).astype(F32)
    before = jnp.dot(onehot, earlier, preferred_element_type=F32)
    rank = jnp.sum(before * onehot, axis=0, keepdims=True).astype(jnp.int32)
    away = named ^ clip
    slot = jnp.zeros_like(away)
    share = clips * capacity // cores
    for t, runs in enumerate(routing(clips, cores, capacity)[0]):
        at = 0
        for offset, first, count in runs:
            inside = (away == offset) & (rank >= first) & (rank < first + count)
            slot = jnp.where(inside, (core ^ t) * share + at - first + rank, slot)
            at += count
    return (lax.broadcasted_iota(jnp.int32, (clips * capacity, rows), 0) == slot).astype(BF16)


def ffn_kernel(capacity, cores, edges, dest_hbm, hidden_hbm, weight_hbm, residual_hbm,
               own_ref, send_ref, text_ref, dest_ref, hidden_ref, weight_ref, residual_ref,
               packed_ref, total_ref, sems):
    clip, core = lax.axis_index("clip"), lax.axis_index("tp")
    share = own_ref.shape[0]
    steps = len(edges) - 1
    parts = [pl.ds(edges[i], edges[i + 1] - edges[i]) for i in range(steps)]
    get_dest = pltpu.make_async_copy(dest_hbm, dest_ref, sems.at[steps])
    get_hidden = pltpu.make_async_copy(hidden_hbm, hidden_ref, sems.at[steps + 1])
    get_residual = pltpu.make_async_copy(residual_hbm, residual_ref, sems.at[steps + 2])
    get_weight = [
        pltpu.make_async_copy(weight_hbm.at[part, :], weight_ref.at[part, :], sems.at[i])
        for i, part in enumerate(parts)
    ]
    for copy in [get_dest, get_hidden] + get_weight[:-1] + [get_residual, get_weight[-1]]:
        copy.start()
    get_dest.wait()
    select = slot_select(dest_ref, clip, core, capacity, cores)
    get_hidden.wait()
    packed_ref[...] = jnp.dot(select, hidden_ref[...], preferred_element_type=F32).astype(BF16)
    for i, part in enumerate(parts):
        if i == steps - 1:
            get_residual.wait()
            text_ref[...] = jnp.dot(
                select[:share], residual_ref[...], preferred_element_type=F32
            ).astype(BF16)
        get_weight[i].wait()
        product = jnp.dot(packed_ref[:, part], weight_ref[part, :], preferred_element_type=F32)
        if i < steps - 1:
            total_ref[...] = product if i == 0 else total_ref[...] + product
        elif i == 0:
            own_ref[...], send_ref[...] = product[:share], product[share:]
        else:
            own_ref[...] = total_ref[:share, :] + product[:share]
            send_ref[...] = total_ref[share:, :] + product[share:]


def ffn(dest, hidden, weight, residual, capacity, cores):
    rows, depth = hidden.shape
    width = weight.shape[1]
    slots = dest.shape[0] * capacity
    share = slots // cores
    unit = depth // 20
    edges = [0, 5 * unit, 10 * unit, 15 * unit, 19 * unit, depth] if unit % 128 == 0 else [0, depth]
    return pl.pallas_call(
        functools.partial(ffn_kernel, capacity, cores, edges),
        in_specs=[pl.BlockSpec(memory_space=pltpu.HBM)] * 4,
        out_specs=[whole()] * 3,
        out_shape=[
            pltpu.VMEM((share, width), F32),
            pltpu.VMEM((slots - share, width), F32),
            pltpu.VMEM((share, width), BF16),
        ],
        scratch_shapes=[
            pltpu.VMEM(dest.shape, jnp.int32),
            pltpu.VMEM(hidden.shape, BF16),
            pltpu.VMEM(weight.shape, BF16),
            pltpu.VMEM(residual.shape, BF16),
            pltpu.VMEM((slots, depth), BF16),
            pltpu.VMEM((slots, width), F32),
            pltpu.SemaphoreType.DMA((len(edges) + 2,)),
        ],
        compiler_params=pltpu.CompilerParams(vmem_limit_bytes=VMEM_LIMIT),
        cost_estimate=pl.CostEstimate(
            flops=2 * slots * depth * (width + rows),
            bytes_accessed=2 * depth * (width + rows),
            transcendentals=0,
        ),
    )(*[pltpu.with_memory_space_constraint(x, pltpu.HBM) for x in (dest, hidden, weight, residual)])


def keyval_kernel(parts, groups, *refs):
    found, (gain_ref, *weights), out_ref = refs[:groups * parts], refs[groups * parts:-1], refs[-1]
    seq = lax.axis_index("seq")
    texts = [
        jnp.concatenate([found[g * parts + k][...] for g in range(groups)], axis=0)
        for k in range(parts)
    ]
    width = texts[0].shape[1]
    squares = 0.0
    for text in texts:
        wide = text.astype(F32)
        squares += jnp.sum(wide * wide, axis=1, keepdims=True)
    scale = lax.rsqrt(squares / (parts * width) + EPSILON)
    totals = [0.0] * len(weights)
    for k, text in enumerate(texts):
        place = pl.ds(pl.multiple_of((seq ^ k) * width, width), width)
        normed = (text.astype(F32) * scale * gain_ref[:, place]).astype(BF16)
        for c, weight in enumerate(weights):
            totals[c] += jnp.dot(normed, weight[place, :], preferred_element_type=F32)
    each = weights[0].shape[1]
    for c in range(len(weights)):
        out_ref[:, c * each:(c + 1) * each] = totals[c].astype(BF16)


def attend_kernel(parts, cores, heads_here, capacity, steps, dest_ref, query_ref, *refs):
    own, refs = refs[:len(steps)], refs[len(steps):]
    others, done, out_ref = refs[:cores - 1], refs[cores - 1:-1], refs[-1]
    clip, seq, core = lax.axis_index("clip"), lax.axis_index("seq"), lax.axis_index("tp")
    clips = dest_ref.shape[0]
    slots = clips * capacity
    dim = query_ref.shape[1] // (parts * cores * heads_here)
    counts = jnp.sum((dest_ref[...] == clip).astype(jnp.int32), axis=1, keepdims=True)
    share = slots // cores
    lane = lax.broadcasted_iota(jnp.int32, (clips, slots), 1)
    owner, place = (lane // share) ^ core, lane % share
    source, rank = jnp.zeros_like(lane), jnp.zeros_like(lane)
    for t, runs in enumerate(routing(clips, cores, capacity)[0]):
        at = 0
        for offset, first, count in runs:
            inside = (owner == t) & (place >= at) & (place < at + count)
            source = jnp.where(inside, offset ^ clip, source)
            rank = jnp.where(inside, first + place - at, rank)
            at += count
    here = lax.broadcasted_iota(jnp.int32, lane.shape, 0) == source
    valid = jnp.sum(jnp.where(here & (rank < counts), 1, 0), axis=0, keepdims=True) > 0
    heads = [
        (k, c, i) for k in range(len(steps)) for c in range(cores) for i in range(heads_here)
    ]

    def columns(head):
        k, c, i = head
        at = ((seq ^ steps[k]) * cores + (core ^ c)) * heads_here + i
        return pl.ds(pl.multiple_of(at * dim, dim), dim)

    def stored(head, offset):
        k, c, i = head
        found = []
        for g in range(cores):
            at = ((c ^ g) * heads_here + i) * 2 * dim + offset
            if g == 0:
                found.append(own[k][:, at:at + dim])
            else:
                found.append(others[g - 1][k, :, at:at + dim])
        return jnp.concatenate(found, axis=0)

    if done:
        out_ref[...] = done[0][...]
    group = 8
    for first in range(0, len(heads), group):
        some = heads[first:first + group]
        scores = [
            lax.dot_general(
                query_ref[:, columns(head)], stored(head, 0), (((1,), (1,)), ((), ())),
                preferred_element_type=F32,
            )
            for head in some
        ]
        scores = [jnp.where(valid, score * (1.0 / math.sqrt(dim)), -1e30) for score in scores]
        peaks = [jnp.max(score, axis=1, keepdims=True) for score in scores]
        weights = [
            jnp.where(valid, jnp.exp(score - peak), 0.0) for score, peak in zip(scores, peaks)
        ]
        sums = [jnp.sum(weight, axis=1, keepdims=True) for weight in weights]
        probs = [(weight / total).astype(BF16) for weight, total in zip(weights, sums)]
        results = [
            jnp.dot(prob, stored(head, dim), preferred_element_type=F32).astype(BF16)
            for prob, head in zip(probs, some)
        ]
        for head, result in zip(some, results):
            out_ref[:, columns(head)] = result


def keyval(texts, gain, weights):
    groups, parts = len(texts), len(texts[0])
    rows, width = sum(some[0].shape[0] for some in texts), texts[0][0].shape[1]
    wide = sum(weight.shape[1] for weight in weights)
    return pl.pallas_call(
        functools.partial(keyval_kernel, parts, groups),
        in_specs=[whole()] * (groups * parts + 1 + len(weights)),
        out_specs=whole(),
        out_shape=pltpu.VMEM((rows, wide), BF16),
        compiler_params=pltpu.CompilerParams(vmem_limit_bytes=VMEM_LIMIT),
        cost_estimate=pl.CostEstimate(
            flops=2 * rows * parts * width * wide,
            bytes_accessed=2 * parts * width * (rows + wide),
            transcendentals=0,
        ),
    )(
        *[text for some in texts for text in some],
        gain,
        *[pltpu.with_memory_space_constraint(x, pltpu.VMEM) for x in weights],
    )


def shards(ffn_hidden, ffn_weight, residual, norm_gain, kv_weight, destination, queries):
    clips, parts, cores = lax.axis_size("clip"), lax.axis_size("seq"), lax.axis_size("tp")
    rows = ffn_hidden.shape[0]
    capacity = rows // min(8, clips)
    share = clips * capacity // cores
    heads_here = kv_weight.shape[1]
    dest = destination.reshape(clips, rows)
    gain = norm_gain.reshape(1, -1)
    weight = kv_weight.reshape(kv_weight.shape[0], heads_here * kv_weight.shape[2])
    weights = [swap(weight, "tp", g) for g in range(1, cores)]
    own, send, text = ffn(dest, ffn_hidden, ffn_weight, residual, capacity, cores)
    weights, own = lax.optimization_barrier(([weight] + weights, own))
    for g in range(1, cores):
        own = own + swap(send[(g - 1) * share:g * share], "tp", g)
    text = (text.astype(F32) + own).astype(BF16)
    runs, groups = routing(clips, cores, capacity)
    edges = [sum(run[2] for run in runs[0][:n]) for n in range(len(runs[0]) + 1)]
    arrived = [
        route(text[edges[n]:edges[n + 1]], [some[n][0] for some in runs])
        for n in range(len(runs[0]))
    ]
    texts = []
    for group in groups:
        mine = jnp.concatenate([arrived[n] for n in group], axis=0)
        texts.append(relayed(mine))
    block = keyval(texts, gain, weights)
    own = [block] + [swap(block, "seq", k) for k in range(1, parts)]

    def attend(steps, done):
        some = [own[k] for k in steps]
        others = [swap(jnp.stack(some), "tp", g) for g in range(1, cores)]
        return pl.pallas_call(
            functools.partial(attend_kernel, parts, cores, heads_here, capacity, steps),
            in_specs=[whole()] * (2 + len(some) + len(others) + len(done)),
            out_specs=whole(),
            out_shape=jax.ShapeDtypeStruct(queries.shape, BF16),
            compiler_params=pltpu.CompilerParams(vmem_limit_bytes=VMEM_LIMIT),
        )(dest, queries, *some, *others, *done)

    soon = sorted({0, parts // 2})
    late = [k for k in range(parts) if k not in soon]
    output = attend(soon, [])
    return attend(late, [output]) if late else output


def solution(mesh):
    return jax.shard_map(
        shards,
        mesh=mesh,
        in_specs=(
            P("clip", "tp"),
            P("tp", "seq"),
            P("clip", "seq"),
            P(),
            P(None, ("seq", "tp"), None),
            P(),
            P(("clip", "seq", "tp"), None),
        ),
        out_specs=P(("clip", "seq", "tp"), None),
        check_vma=False,
    )
```
